512 devices in a mesh: lat: 16 (over x, y_hi, core), lon: 32 (over z, y_lo).
Axes of the slice: x: 4, y: 4 (y_hi: 2, y_lo: 2; y = y_hi * 2 + y_lo), z: 16, core: 2. Of those that a mesh axis runs over, the one named last changes fastest.
Arguments:
- tracer: float32 [8, 256, 36864], P(None, 'lat', 'lon'), may hold values from -6 to 6
- flux: float32 [256, 36864], P('lat', 'lon'), may hold values from -6 to 6
- winds: float32 [3, 8, 256, 768], P(None, None, 'lat', 'lon'), may hold values from -0.3 to 0.3
- obs_cells: int32 [8192, 3], P(('lat', 'lon')), may hold values from 0 to 767, as said below
- obs_count: int32 [512], P(('lat', 'lon')), may hold values from 1 to 16, as said below
- obs_value: float32 [8192], P(('lat', 'lon')), may hold values from -6 to 6
- obs_var: float32 [8192], P(('lat', 'lon')), may hold values from 21.333334 to 341.33334
Outputs:
- tracer_out: float32 [8, 256, 36864], P(None, 'lat', 'lon')
- flux_out: float32 [256, 36864], P('lat', 'lon')
The draws below stay inside these ranges and needn't reach their ends.
Inputs may be any that keep to these rules, and one draw needn't show every extreme that they name: `obs_cells`: slot k lies in the block of 16 slots of device k div 16 (devices in lat-major order), and its cell lies in that device's block of the grid: row in its 16 rows, column in its 24 columns, level below 8. Each device's first slot is the last row, last column and highest level of its block, its second slot the first row, first column and level 0 of its block. Cells may repeat. Live slots are the first obs_count of each device's slots; some device has all 16 slots live.
All inputs are finite; a program needn't handle non-finite values.
Results may differ from the reference program's by a relative error of at most 0.0001.
Values sent between devices are 32-bit elements; how exact they have to be, the bound alone decides.
A program may use at most 64 MiB of HBM per device.

```python
import math
import jax
import jax.numpy as jnp
from jax import lax

M = 48
LEV = 8
CLAT = 16
CLON = 24
OBS_DEV = 16
NS_ITERS = 5
NLAT = 256
NLON = 768
NOBS = 8192
N_LAT = 16
N_LON = 32


def draw_obs_cells(key, part):
    slots = jnp.arange(NOBS, dtype=jnp.int32)
    device = slots // OBS_DEV
    within = slots % OBS_DEV
    lat_dev = device // N_LON
    lon_dev = device % N_LON
    key_row, key_col, key_lev = jax.random.split(jax.random.fold_in(key, 11), 3)
    row_off = jax.random.randint(key_row, (NOBS,), 0, CLAT, dtype=jnp.int32)
    col_off = jax.random.randint(key_col, (NOBS,), 0, CLON, dtype=jnp.int32)
    levels = jax.random.randint(key_lev, (NOBS,), 0, LEV, dtype=jnp.int32)
    row_off = jnp.where(within == 0, CLAT - 1, jnp.where(within == 1, 0, row_off))
    col_off = jnp.where(within == 0, CLON - 1, jnp.where(within == 1, 0, col_off))
    levels = jnp.where(within == 0, LEV - 1, jnp.where(within == 1, 0, levels))
    rows = lat_dev * CLAT + row_off
    columns = lon_dev * CLON + col_off
    return jnp.stack([rows, columns, levels], axis=1).astype(jnp.int32)


def draw_obs_count(key, part):
    device = jnp.arange(N_LAT * N_LON, dtype=jnp.int32)
    lat_dev = device // N_LON
    lon_dev = device % N_LON
    quarter = OBS_DEV // 4
    base = quarter + lat_dev * (OBS_DEV - quarter) // max(N_LAT - 1, 1)
    jitter = jax.random.randint(jax.random.fold_in(key, 23), (N_LAT * N_LON,), 0, OBS_DEV // 8 + 1, dtype=jnp.int32)
    jitter = jnp.where(lon_dev == 0, 0, jitter)
    return jnp.maximum(base - jitter, 1).astype(jnp.int32)


def steps_of(key, dims, pieces, low, high):
    gain = 1.0
    for dim, parts in pieces:
        draws = jax.random.uniform(jax.random.fold_in(jax.random.fold_in(key, 6), dim), (parts,), jnp.float32, low / len(pieces), high / len(pieces))
        gain = gain * jnp.repeat(jnp.exp(draws), dims[dim] // parts).reshape((-1,) + (1,) * (len(dims) - 1 - dim))
    return gain


def bell_draw(key, dims, spread, bound, pieces=(), kind=jnp.bfloat16):
    factor_of = steps_of(key, dims, pieces, -0.22, 0.18) if pieces else 1.0
    values = jax.random.normal(key, dims, jnp.float32) * spread * factor_of
    return jnp.minimum(jnp.maximum(values, -bound), bound).astype(kind)


def setup_inputs(seed: int = 0) -> dict:
    splits = jax.random.split(jax.random.key(seed), 8)
    tracer = bell_draw(splits[0], (LEV, NLAT, NLON * M), 1.0, 6.0, ((1, 16), (2, 32)), jnp.float32)
    flux = bell_draw(splits[1], (NLAT, NLON * M), 1.0, 6.0, ((0, 16), (1, 32)), jnp.float32)
    winds = jnp.clip(jax.random.uniform(splits[2], (3, LEV, NLAT, NLON), jnp.float32, -0.3, 0.3) * steps_of(splits[2], (3, LEV, NLAT, NLON), ((2, 16), (3, 32)), -0.4, 0.0), -0.3, 0.3)
    obs_cells = draw_obs_cells(jax.random.fold_in(splits[7], 71), 0)
    obs_count = draw_obs_count(jax.random.fold_in(splits[7], 71), 0)
    obs_value = bell_draw(splits[5], (NOBS,), 1.0, 6.0, ((0, 512),), jnp.float32)
    obs_var = jnp.clip(jnp.exp(math.log(341.33334) - 2.7725887 * jax.random.uniform(splits[6], (NOBS,), jnp.float32) ** steps_of(splits[6], (NOBS,), ((0, 512),), -0.2, 0.2)), 21.333334, 341.33334)
    return dict(tracer=tracer, flux=flux, winds=winds, obs_cells=obs_cells, obs_count=obs_count, obs_value=obs_value, obs_var=obs_var)


KH = 0.15

def advance(center, lat_minus, lat_plus, lon_prev, lon_next, wind_u, wind_v, wind_w):
    zeros = jnp.zeros_like(center[:1])
    above = jnp.concatenate([center[1:], zeros], axis=0)
    below = jnp.concatenate([zeros, center[:-1]], axis=0)
    result = center - 0.5 * wind_u * (lon_next - lon_prev) + KH * (lon_next - 2.0 * center + lon_prev)
    result = result - 0.5 * wind_v * (lat_plus - lat_minus) + KH * (lat_plus - 2.0 * center + lat_minus)
    result = result - 0.5 * wind_w * (above - below) + KH * (above - 2.0 * center + below)
    return result

def member_transform(gram, proj, members):
    eye = jnp.eye(members, dtype=jnp.float32)
    hp = lax.Precision.HIGHEST
    system = (members - 1.0) * eye + gram
    scale = jnp.sqrt(jnp.sum(system * system))
    root_now = system / scale
    inverse_now = eye
    for step in range(NS_ITERS):
        factor = 0.5 * (3.0 * eye - jnp.dot(inverse_now, root_now, precision=hp))
        root_now = jnp.dot(root_now, factor, precision=hp)
        inverse_now = jnp.dot(factor, inverse_now, precision=hp)
    wmean = jnp.dot(inverse_now, jnp.dot(inverse_now, proj, precision=hp), precision=hp) / scale
    root = jnp.sqrt((members - 1.0) / scale) * inverse_now
    centering = eye - 1.0 / members
    return jnp.dot(centering, wmean[:, None] + root, precision=hp) + 1.0 / members

def transport(field, winds):
    wind_u = winds[0][..., None]
    wind_v = winds[1][..., None]
    wind_w = winds[2][..., None]
    lon_next = jnp.roll(field, -1, axis=2)
    lon_prev = jnp.roll(field, 1, axis=2)
    zero_row = jnp.zeros_like(field[:, :1])
    lat_plus = jnp.concatenate([field[:, 1:], zero_row], axis=1)
    lat_minus = jnp.concatenate([zero_row, field[:, :-1]], axis=1)
    return advance(field, lat_minus, lat_plus, lon_prev, lon_next, wind_u, wind_v, wind_w)

def reference(tracer, flux, winds, obs_cells, obs_count, obs_value, obs_var):
    hp = lax.Precision.HIGHEST
    field = tracer.reshape(LEV, NLAT, NLON, M)
    surface = flux.reshape(NLAT, NLON, M)
    field = field.at[0].add(surface)
    field = transport(field, winds)
    field = transport(field, winds)
    observed = field[obs_cells[:, 2], obs_cells[:, 0], obs_cells[:, 1]]
    slots = jnp.arange(NOBS, dtype=jnp.int32)
    live = (slots % OBS_DEV < obs_count[slots // OBS_DEV]).astype(jnp.float32)
    hbar = lax.optimization_barrier(jnp.mean(observed, axis=1))
    anomalies = observed - hbar[:, None]
    innovation = obs_value - hbar
    weight = live / obs_var
    gram = jnp.dot(anomalies.T * weight[None, :], anomalies, precision=hp)
    proj = jnp.dot(anomalies.T, weight * innovation, precision=hp)
    mixing = member_transform(gram, proj, M)
    tracer_out = jnp.dot(field.reshape(-1, M), mixing, precision=hp).reshape(LEV, NLAT, NLON * M)
    flux_out = jnp.dot(surface.reshape(-1, M), mixing, precision=hp).reshape(NLAT, NLON * M)
    return (tracer_out, flux_out)
```

```python
import functools

import jax
import jax.numpy as jnp
from jax import lax
from jax.experimental import pallas as pl
from jax.experimental.pallas import tpu as pltpu
from jax.sharding import PartitionSpec as P

M = 48
NS_ITERS = 5
KH = 0.15
MESH = pl.DeviceIdType.MESH
HP = lax.Precision.HIGHEST
F32 = jnp.float32
BF16 = jnp.bfloat16

LEV, ROWS, COLS, OBS = 8, 16, 24, 16
TILES = 9
WIDTH = COLS * M
WIDE = WIDTH + 256
EAST, WEST = WIDTH, WIDTH + 128
ROWS_X = ROWS + 4
SOUTH, NORTH = ROWS, ROWS + 3
GROUP = 8 * M


def kernel(
    n_lat, n_lon,
    tracer, flux, winds, cells, count, value, var,
    tracer_out, flux_out,
    raw, raw_flux, raw_winds, wide_winds, field, mid, last, wc, wx, wcol_out, wcol_in,
    seen, vals, pack, part1, part2, part3, sum1, sum2, high, low, outs, outs_flux,
    in_sem, out_sem, halo_send, halo_recv, ar_send, ar_recv,
):
    lat, lon = lax.axis_index("lat"), lax.axis_index("lon")

    def at(dlat, dlon):
        return (lax.rem(lat + (dlat + n_lat), n_lat), lax.rem(lon + (dlon + n_lon), n_lon))

    copies = [
        pltpu.make_async_copy(winds, raw_winds, in_sem.at[0]),
    ]
    for t in range(TILES):
        lanes = pl.ds(t * 128, 128)
        copies.append(pltpu.make_async_copy(tracer.at[:, lanes], raw.at[t], in_sem.at[1 + t]))
        copies.append(pltpu.make_async_copy(flux.at[:, lanes], raw_flux.at[t], in_sem.at[1 + TILES + t]))
    for copy in copies:
        copy.start()

    sides = [(1, 0), (-1, 0), (0, 1), (0, -1), (1, 1), (1, -1), (-1, 1), (-1, -1)]
    pair = lax.rem(lon, 2)
    base = lon - pair

    def plane_peer(j):
        return (lax.rem(lat + j // 2, n_lat), base + lax.rem(pair + j, 2))

    def line_peer(j):
        return (lat, lax.rem(lon + 2 * j, n_lon))

    core = lax.rem(lat, 2)
    partner = (lat + 1 - 2 * core, lon)
    n_plane, n_line = 2 * n_lat, n_lon // 2

    barrier = pltpu.get_barrier_semaphore()
    for dlat, dlon in sides:
        pl.semaphore_signal(barrier, inc=1, device_id=at(dlat, dlon), device_id_type=MESH)
    for j in range(1, n_plane):
        pl.semaphore_signal(barrier, inc=1, device_id=plane_peer(j), device_id_type=MESH)
    for j in range(1, n_line):
        pl.semaphore_signal(barrier, inc=1, device_id=line_peer(j), device_id_type=MESH)

    for copy in copies:
        copy.wait()
    level = lax.broadcasted_iota(jnp.int32, (LEV, 1), 0)
    wide_winds[:, 0:COLS] = 0.5 * raw_winds[...]

    def enter(r, carry):
        for t in range(TILES):
            own = raw[t, pl.ds(r, LEV, stride=ROWS), :]
            surface = raw_flux[t, pl.ds(r, 1), :]
            field[r, :, t * 128:t * 128 + 128] = own + jnp.where(level == 0, surface, 0.0)
        for v in range(3):
            wc[v, r] = wide_winds[pl.ds(v * LEV * ROWS + r, LEV, stride=ROWS), :]
        return carry

    lax.fori_loop(0, ROWS, enter, 0)

    lane = lax.broadcasted_iota(jnp.int32, (LEV, 128), 1)

    def edge(r, carry):
        first, final = carry
        for v in range(3):
            w = wc[v, r]
            here = lane == v * ROWS + r
            first = jnp.where(here, w[:, 0:1], first)
            final = jnp.where(here, w[:, COLS - 1:COLS], final)
        return first, final

    zero_tile = jnp.zeros((LEV, 128), F32)
    first, final = lax.fori_loop(0, ROWS, edge, (zero_tile, zero_tile))
    wcol_out[0] = first
    wcol_out[1] = final

    pl.semaphore_wait(barrier, len(sides) + n_plane - 1 + n_line - 1)

    def send(i, src, dst, to):
        return pltpu.make_async_remote_copy(
            src_ref=src, dst_ref=dst, send_sem=halo_send.at[i], recv_sem=halo_recv.at[i],
            device_id=to, device_id_type=MESH,
        )

    own_lanes = pl.ds(0, WIDTH)
    left_tile, right_tile = pl.ds(0, 128), pl.ds(WIDTH - 128, 128)
    east_tile, west_tile = pl.ds(EAST, 128), pl.ds(WEST, 128)
    own_rows = pl.ds(0, ROWS)
    top, bottom = 0, ROWS - 1
    halos = [
        send(0, wcol_out.at[0], wcol_in.at[0], at(0, -1)),
        send(1, wcol_out.at[1], wcol_in.at[1], at(0, 1)),
        send(2, wc.at[:, top], wc.at[:, SOUTH], at(-1, 0)),
        send(3, wc.at[:, bottom], wc.at[:, NORTH], at(1, 0)),
        send(4, field.at[pl.ds(top, 2), :, own_lanes], field.at[pl.ds(SOUTH, 2), :, own_lanes], at(-1, 0)),
        send(5, field.at[pl.ds(bottom - 1, 2), :, own_lanes], field.at[pl.ds(NORTH - 1, 2), :, own_lanes], at(1, 0)),
        send(6, field.at[own_rows, :, left_tile], field.at[own_rows, :, east_tile], at(0, -1)),
        send(7, field.at[own_rows, :, right_tile], field.at[own_rows, :, west_tile], at(0, 1)),
        send(8, field.at[top, :, left_tile], field.at[SOUTH, :, east_tile], at(-1, -1)),
        send(9, field.at[top, :, right_tile], field.at[SOUTH, :, west_tile], at(-1, 1)),
        send(10, field.at[bottom, :, left_tile], field.at[NORTH, :, east_tile], at(1, -1)),
        send(11, field.at[bottom, :, right_tile], field.at[NORTH, :, west_tile], at(1, 1)),
    ]
    for copy in halos[4:] + halos[:4]:
        copy.start()

    spread_col = lax.broadcasted_iota(jnp.int32, (COLS, WIDTH), 0)
    spread_lane = lax.broadcasted_iota(jnp.int32, (COLS, WIDTH), 1)
    spread = jnp.where((spread_lane >= spread_col * M) & (spread_lane < spread_col * M + M), 1.0, 0.0).astype(BF16)

    def spread_rows(v, start, rows):
        w = wc[v, pl.ds(start, rows), :, 0:COLS].reshape(rows * LEV, COLS)
        a = w.astype(BF16)
        rest = w - a.astype(F32)
        b = rest.astype(BF16)
        c = (rest - b.astype(F32)).astype(BF16)
        wide = (
            jnp.dot(a, spread, preferred_element_type=F32)
            + jnp.dot(b, spread, preferred_element_type=F32)
            + jnp.dot(c, spread, preferred_element_type=F32)
        )
        wx[v, pl.ds(start, rows), :, 0:WIDTH] = wide.reshape(rows, LEV, WIDTH)

    for v in range(3):
        spread_rows(v, 0, ROWS)

    for i in range(4):
        halos[i].wait_recv()
    for v in range(3):
        spread_rows(v, SOUTH, 1)
        spread_rows(v, NORTH, 1)
        for side, start in ((0, EAST), (1, WEST)):
            got = wcol_in[side]
            for r in range(ROWS):
                wx[v, r, :, start:start + 128] = jnp.broadcast_to(got[:, v * ROWS + r:v * ROWS + r + 1], (LEV, 128))

    for i in range(4, 12):
        halos[i].wait_recv()

    has_north, has_south = lat > 0, lat < n_lat - 1
    field[NORTH] = jnp.where(has_north, field[NORTH], 0.0)
    field[SOUTH] = jnp.where(has_south, field[SOUTH], 0.0)

    def advance(src, r):
        c = src[r]
        north, south = src[lax.rem(r + ROWS_X - 1, ROWS_X)], src[lax.rem(r + 1, ROWS_X)]
        east, west = pltpu.roll(c, WIDE - M, 1), pltpu.roll(c, M, 1)
        above = jnp.where(level == LEV - 1, 0.0, pltpu.roll(c, LEV - 1, 0))
        below = jnp.where(level == 0, 0.0, pltpu.roll(c, 1, 0))
        spread_out = (east + west) + (south + north) + (above + below)
        carried = wx[0, r] * (east - west) + wx[1, r] * (south - north) + wx[2, r] * (above - below)
        return (1.0 - 6.0 * KH) * c + KH * spread_out - carried

    def first_step(i, carry):
        r = lax.rem(i + NORTH, ROWS_X)
        keep = ((r != NORTH) | has_north) & ((r != SOUTH) | has_south)
        mid[r] = jnp.where(keep, advance(field, r), 0.0)
        return carry

    lax.fori_loop(0, ROWS + 2, first_step, 0)

    def second_step(r, carry):
        new = advance(mid, r)
        for t in range(TILES):
            last[t, pl.ds(pl.multiple_of(r * LEV, LEV), LEV), :] = new[:, t * 128:t * 128 + 128]
        return carry

    lax.fori_loop(0, ROWS, second_step, 0)

    lane_1 = lax.broadcasted_iota(jnp.int32, (1, 128), 1)

    def look(k, carry):
        row, col, lev = cells[0, k] - lat * ROWS, cells[1, k] - lon * COLS, cells[2, k]
        cell = jnp.clip(row * LEV + lev, 0, LEV * ROWS - 1)
        for t in range(TILES):
            line = last[t, pl.ds(cell, 1), :]
            inside = (lane_1 >= col * M - t * 128) & (lane_1 < col * M + M - t * 128)
            seen[t, pl.ds(k, 1), :] = jnp.where(inside, line, 0.0)
        live = jnp.where(k < count[0], 1.0, 0.0)
        vals[0, pl.ds(k, 1), :] = jnp.full((1, 128), live, F32)
        vals[1, pl.ds(k, 1), :] = jnp.full((1, 128), var[k], F32)
        vals[2, pl.ds(k, 1), :] = jnp.full((1, 128), value[k], F32)
        return carry

    lax.fori_loop(0, OBS, look, 0)
    hx = jnp.concatenate([seen[t] + seen[t + 3] + seen[t + 6] for t in range(3)], axis=1)
    hx = hx + pltpu.roll(hx, GROUP // 2, 1)
    hx = hx + pltpu.roll(hx, GROUP // 4, 1)
    hx = hx + pltpu.roll(hx, GROUP // 8, 1)
    lane_o = lax.broadcasted_iota(jnp.int32, (OBS, 128), 1)
    hbar = jnp.sum(jnp.where(lane_o < M, hx[:, 0:128], 0.0), axis=1, keepdims=True) * (1.0 / M)
    y = hx - hbar
    q = vals[0] / vals[1]
    d = vals[2] - hbar

    y0 = y[:, 0:128]
    y32 = pltpu.roll(y, 32, 1)[:, 0:128]
    w0 = jnp.where(lane_o < 48, y0, jnp.where(lane_o == 96, d, 0.0))
    w1 = jnp.where((lane_o >= 48) & (lane_o < 80), y32, jnp.where(lane_o == 97, d, 0.0))
    w2 = jnp.where((lane_o >= 80) & (lane_o < 96), y0, jnp.where(lane_o == 98, d, 0.0))
    l1 = pltpu.roll(y, GROUP - 16, 1)[:, 0:128]
    l2 = pltpu.roll(y, GROUP - 32, 1)[:, 0:128]
    lhs = jnp.concatenate([q * y0, q * l1, q * l2], axis=0)
    rhs = jnp.concatenate([w0, w1, w2], axis=0)
    packed = lax.dot_general(lhs, rhs, (((0,), (0,)), ((), ())), precision=HP, preferred_element_type=F32)[0:16]
    pack[...] = packed.reshape(2, 8, 128)

    for j in range(1, n_plane):
        pltpu.make_async_remote_copy(
            src_ref=pack.at[lax.rem(lat + j // 2, 2)], dst_ref=part1.at[j - 1],
            send_sem=ar_send.at[0], recv_sem=ar_recv.at[0], device_id=plane_peer(j), device_id_type=MESH,
        ).start()

    def halves(x, start, rows):
        for t in range(TILES):
            part = x[t]
            hi = part.astype(BF16)
            place = (pl.ds(t // 3 * 144 + start, rows), pl.ds(t % 3 * 128, 128))
            high[place] = hi
            low[place] = (part - hi.astype(F32)).astype(BF16)

    halves(last, 0, LEV * ROWS)
    halves(raw_flux, LEV * ROWS, ROWS)

    def wait_all(ref, sem):
        pltpu.make_async_copy(ref, ref, sem).wait()

    wait_all(part1, ar_recv.at[0])
    sum1[...] = pack[core] + jnp.sum(part1[...], axis=0)
    for j in range(1, n_line):
        pltpu.make_async_remote_copy(
            src_ref=sum1, dst_ref=part2.at[j - 1],
            send_sem=ar_send.at[1], recv_sem=ar_recv.at[1], device_id=line_peer(j), device_id_type=MESH,
        ).start()
    wait_all(part2, ar_recv.at[1])
    sum2[...] = sum1[...] + jnp.sum(part2[...], axis=0)
    swap = pltpu.make_async_remote_copy(
        src_ref=sum2, dst_ref=part3, send_sem=ar_send.at[2], recv_sem=ar_recv.at[2],
        device_id=partner, device_id_type=MESH,
    )
    swap.start()
    swap.wait_recv()
    mine, other = sum2[...], part3[...]
    total = jnp.concatenate([jnp.where(core == 0, mine, other), jnp.where(core == 0, other, mine)], axis=0)

    lane_p = lax.broadcasted_iota(jnp.int32, (16, 128), 1)
    u0 = jnp.where(lane_p < 48, total, 0.0)
    u1 = jnp.where((lane_p >= 16) & (lane_p < 48), pltpu.roll(total, 128 - 32, 1), 0.0)
    u2 = jnp.where((lane_p >= 32) & (lane_p < 48), pltpu.roll(total, 128 - 48, 1), 0.0)
    upper = jnp.concatenate([u0, u1, u2, jnp.zeros((80, 128), F32)], axis=0)
    flipped = upper.T
    row_s = lax.broadcasted_iota(jnp.int32, (M, M), 0)
    col_s = lax.broadcasted_iota(jnp.int32, (M, M), 1)
    gram = jnp.where(row_s // 16 > col_s // 16, flipped[0:M, 0:M], upper[0:M, 0:M])
    proj = jnp.concatenate([total[:, 96:97], total[:, 97:98], total[:, 98:99]], axis=0)
    eye = jnp.where(row_s == col_s, 1.0, 0.0)

    def dot(a, b):
        return jnp.dot(a, b, precision=HP, preferred_element_type=F32)

    system = (M - 1.0) * eye + gram
    scale = jnp.sqrt(jnp.sum(system * system, keepdims=True))
    root_now = system / scale
    factor = 0.5 * (3.0 * eye - root_now)
    root_now, inverse_now = dot(root_now, factor), factor
    for step in range(1, NS_ITERS):
        factor = 0.5 * (3.0 * eye - dot(inverse_now, root_now))
        if step < NS_ITERS - 1:
            root_now = dot(root_now, factor)
        inverse_now = dot(factor, inverse_now)
    inner = jnp.sum(inverse_now * proj, axis=0, keepdims=True)
    wmean = jnp.sum(inverse_now * inner, axis=1, keepdims=True) / scale
    mixed = wmean + jnp.sqrt((M - 1.0) / scale) * inverse_now
    mixing = mixed - jnp.sum(mixed, axis=0, keepdims=True) * (1.0 / M) + 1.0 / M

    g_high = mixing.astype(BF16)
    g_low = (mixing - g_high.astype(F32)).astype(BF16)
    rep_row = lax.broadcasted_iota(jnp.int32, (M, GROUP), 0)
    rep_lane = lax.broadcasted_iota(jnp.int32, (M, GROUP), 1)
    rep = jnp.where(lax.rem(rep_lane, M) == rep_row, 1.0, 0.0).astype(BF16)
    g_high = jnp.dot(g_high, rep, preferred_element_type=F32)
    g_low = jnp.dot(g_low, rep, preferred_element_type=F32)

    def diagonal(g):
        return jnp.concatenate(
            [jnp.where((rep_lane >= b * M) & (rep_lane < b * M + M), g, 0.0).astype(BF16) for b in range(8)], axis=0
        )

    d_high, d_low = diagonal(g_high), diagonal(g_low)
    for g in range(3):
        hi, lo = high[pl.ds(g * 144, 144), :], low[pl.ds(g * 144, 144), :]
        out = (
            jnp.dot(hi, d_high, preferred_element_type=F32)
            + jnp.dot(lo, d_high, preferred_element_type=F32)
            + jnp.dot(hi, d_low, preferred_element_type=F32)
        )
        lanes = pl.ds(g * GROUP, GROUP)
        for t in range(3):
            for r in range(ROWS):
                outs[g * 3 + t, pl.ds(r, LEV, stride=ROWS), :] = out[r * LEV:(r + 1) * LEV, t * 128:t * 128 + 128]
        outs_flux[:, lanes] = out[LEV * ROWS:]
    done = [
        pltpu.make_async_copy(outs.at[t], tracer_out.at[:, pl.ds(t * 128, 128)], out_sem.at[t]) for t in range(TILES)
    ] + [pltpu.make_async_copy(outs_flux, flux_out, out_sem.at[TILES])]
    for copy in done:
        copy.start()
    for copy in halos:
        copy.wait_send()
    wait_all(part1, ar_send.at[0])
    wait_all(part2, ar_send.at[1])
    swap.wait_send()
    for copy in done:
        copy.wait()


def on_device(n_lat, n_lon, tracer, flux, winds, obs_cells, obs_count, obs_value, obs_var):
    anywhere = pl.BlockSpec(memory_space=pl.ANY)
    scalars = pl.BlockSpec(memory_space=pltpu.SMEM)
    n_plane, n_line = 2 * n_lat, n_lon // 2
    vmem = pltpu.VMEM
    tracer_out, flux_out = pl.pallas_call(
        functools.partial(kernel, n_lat, n_lon),
        out_shape=(
            jax.ShapeDtypeStruct((LEV * ROWS, WIDTH), F32),
            jax.ShapeDtypeStruct((ROWS, WIDTH), F32),
        ),
        in_specs=[anywhere] * 3 + [scalars] * 4,
        out_specs=(anywhere, anywhere),
        scratch_shapes=[
            vmem((TILES, LEV * ROWS, 128), F32),
            vmem((TILES, ROWS, 128), F32),
            vmem((3 * LEV * ROWS, COLS), F32),
            vmem((3 * LEV * ROWS, 128), F32),
            vmem((ROWS_X, LEV, WIDE), F32),
            vmem((ROWS_X, LEV, WIDE), F32),
            vmem((TILES, LEV * ROWS, 128), F32),
            vmem((3, ROWS_X, LEV, 128), F32),
            vmem((3, ROWS_X, LEV, WIDE), F32),
            vmem((2, LEV, 128), F32),
            vmem((2, LEV, 128), F32),
            vmem((TILES, OBS, 128), F32),
            vmem((3, OBS, 128), F32),
            vmem((2, 8, 128), F32),
            vmem((n_plane - 1, 8, 128), F32),
            vmem((n_line - 1, 8, 128), F32),
            vmem((8, 128), F32),
            vmem((8, 128), F32),
            vmem((8, 128), F32),
            vmem((432, GROUP), BF16),
            vmem((432, GROUP), BF16),
            vmem((TILES, LEV * ROWS, 128), F32),
            vmem((ROWS, WIDTH), F32),
            pltpu.SemaphoreType.DMA((1 + 2 * TILES,)),
            pltpu.SemaphoreType.DMA((1 + TILES,)),
            pltpu.SemaphoreType.DMA((12,)),
            pltpu.SemaphoreType.DMA((12,)),
            pltpu.SemaphoreType.DMA((3,)),
            pltpu.SemaphoreType.DMA((3,)),
        ],
        compiler_params=pltpu.CompilerParams(
            collective_id=0, has_side_effects=True, vmem_limit_bytes=48 * 1024 * 1024
        ),
        name="analysis",
    )(
        tracer.reshape(LEV * ROWS, WIDTH), flux, winds.reshape(3 * LEV * ROWS, COLS),
        obs_cells.T, obs_count, obs_value, obs_var,
    )
    return tracer_out.reshape(LEV, ROWS, WIDTH), flux_out


def solution(mesh):
    return jax.shard_map(
        functools.partial(on_device, mesh.shape["lat"], mesh.shape["lon"]),
        mesh=mesh,
        in_specs=(
            P(None, "lat", "lon"),
            P("lat", "lon"),
            P(None, None, "lat", "lon"),
            P(("lat", "lon"), None),
            P(("lat", "lon")),
            P(("lat", "lon")),
            P(("lat", "lon")),
        ),
        out_specs=(P(None, "lat", "lon"), P("lat", "lon")),
        check_vma=False,
    )
```

```python
import functools

import jax
import jax.numpy as jnp
from jax import lax
from jax.experimental import pallas as pl
from jax.experimental.pallas import tpu as pltpu
from jax.sharding import PartitionSpec as P

M = 48
NS_ITERS = 5
KH = 0.15
MESH = pl.DeviceIdType.MESH
HP = lax.Precision.HIGHEST
F32 = jnp.float32
BF16 = jnp.bfloat16

LEV, ROWS, COLS, OBS = 8, 16, 24, 16
TILES = 9
WIDTH = COLS * M
WIDE = WIDTH + 256
EAST, WEST = WIDTH, WIDTH + 128
ROWS_X = ROWS + 4
SOUTH, NORTH = ROWS, ROWS + 3
GROUP = 8 * M


def kernel(
    n_lat, n_lon,
    tracer, flux, winds, cells_in, count_in, value_in, var_in,
    tracer_out, flux_out,
    raw, raw_flux, raw_winds, wide_winds, field, mid, last, wc, wx, wcol_out, wcol_in,
    seen, vals, pack, part1, part2, part3, sum1, sum2, high, low,
    cells, count, value, var, in_sem, halo_send, halo_recv, ar_send, ar_recv, here_sem,
):
    lat, lon = lax.axis_index("lat"), lax.axis_index("lon")

    def at(dlat, dlon):
        return (lax.rem(lat + (dlat + n_lat), n_lat), lax.rem(lon + (dlon + n_lon), n_lon))

    copies = [
        pltpu.make_async_copy(winds, raw_winds, in_sem.at[0]),
    ]
    for t in range(TILES):
        lanes = pl.ds(t * 128, 128)
        copies.append(pltpu.make_async_copy(tracer.at[:, lanes], raw.at[t], in_sem.at[1 + t]))
        copies.append(pltpu.make_async_copy(flux.at[:, lanes], raw_flux.at[t], in_sem.at[1 + TILES + t]))
    obs_copies = [
        pltpu.make_async_copy(src, dst, in_sem.at[1 + 2 * TILES + i])
        for i, (src, dst) in enumerate(((cells_in, cells), (count_in, count), (value_in, value), (var_in, var)))
    ]
    for copy in copies + obs_copies:
        copy.start()

    sides = [(1, 0), (-1, 0), (0, 1), (0, -1), (1, 1), (1, -1), (-1, 1), (-1, -1)]
    pair = lax.rem(lon, 2)
    base = lon - pair

    def plane_peer(j):
        return (lax.rem(lat + j // 2, n_lat), base + lax.rem(pair + j, 2))

    def line_peer(j):
        return (lat, lax.rem(lon + 2 * j, n_lon))

    core = lax.rem(lat, 2)
    partner = (lat + 1 - 2 * core, lon)
    n_plane, n_line = 2 * n_lat, n_lon // 2

    near = [k for k in (4, -4, 3, -3, 1, -1)]
    plane_order = sorted(range(1, n_plane), key=lambda j: -min(j // 2, n_lat - j // 2))
    line_order = sorted(range(1, n_line), key=lambda j: -min(j, n_line - j))
    barrier = pltpu.get_barrier_semaphore()
    for j in plane_order:
        pl.semaphore_signal(barrier, inc=1, device_id=plane_peer(j), device_id_type=MESH)
    for dlat, dlon in sides:
        pl.semaphore_signal(barrier, inc=1, device_id=at(dlat, dlon), device_id_type=MESH)
    for k in near:
        pl.semaphore_signal(barrier, inc=1, device_id=line_peer(k % n_line), device_id_type=MESH)

    for copy in copies:
        copy.wait()
    level = lax.broadcasted_iota(jnp.int32, (LEV, 1), 0)
    wide_winds[:, 0:COLS] = 0.5 * raw_winds[...]

    def enter(r, carry):
        for t in range(TILES):
            own = raw[t, pl.ds(r, LEV, stride=ROWS), :]
            surface = raw_flux[t, pl.ds(r, 1), :]
            field[r, :, t * 128:t * 128 + 128] = own + jnp.where(level == 0, surface, 0.0)
        for v in range(3):
            wc[v, r] = wide_winds[pl.ds(v * LEV * ROWS + r, LEV, stride=ROWS), :]
        return carry

    lax.fori_loop(0, ROWS, enter, 0)

    lane = lax.broadcasted_iota(jnp.int32, (LEV, 128), 1)

    def edge(r, carry):
        first, final = carry
        for v in range(3):
            w = wc[v, r]
            here = lane == v * ROWS + r
            first = jnp.where(here, w[:, 0:1], first)
            final = jnp.where(here, w[:, COLS - 1:COLS], final)
        return first, final

    zero_tile = jnp.zeros((LEV, 128), F32)
    first, final = lax.fori_loop(0, ROWS, edge, (zero_tile, zero_tile))
    wcol_out[0] = first
    wcol_out[1] = final

    pl.semaphore_wait(barrier, len(sides) + n_plane - 1 + len(near))

    def send(i, src, dst, to):
        return pltpu.make_async_remote_copy(
            src_ref=src, dst_ref=dst, send_sem=halo_send.at[i], recv_sem=halo_recv.at[i],
            device_id=to, device_id_type=MESH,
        )

    own_lanes = pl.ds(0, WIDTH)
    left_tile, right_tile = pl.ds(0, 128), pl.ds(WIDTH - 128, 128)
    east_tile, west_tile = pl.ds(EAST, 128), pl.ds(WEST, 128)
    own_rows = pl.ds(0, ROWS)
    top, bottom = 0, ROWS - 1
    halos = [
        send(0, wcol_out.at[0], wcol_in.at[0], at(0, -1)),
        send(1, wcol_out.at[1], wcol_in.at[1], at(0, 1)),
        send(2, wc.at[:, top], wc.at[:, SOUTH], at(-1, 0)),
        send(3, wc.at[:, bottom], wc.at[:, NORTH], at(1, 0)),
        send(4, field.at[pl.ds(top, 2), :, own_lanes], field.at[pl.ds(SOUTH, 2), :, own_lanes], at(-1, 0)),
        send(5, field.at[pl.ds(bottom - 1, 2), :, own_lanes], field.at[pl.ds(NORTH - 1, 2), :, own_lanes], at(1, 0)),
        send(6, field.at[own_rows, :, left_tile], field.at[own_rows, :, east_tile], at(0, -1)),
        send(7, field.at[own_rows, :, right_tile], field.at[own_rows, :, west_tile], at(0, 1)),
        send(8, field.at[top, :, left_tile], field.at[SOUTH, :, east_tile], at(-1, -1)),
        send(9, field.at[top, :, right_tile], field.at[SOUTH, :, west_tile], at(-1, 1)),
        send(10, field.at[bottom, :, left_tile], field.at[NORTH, :, east_tile], at(1, -1)),
        send(11, field.at[bottom, :, right_tile], field.at[NORTH, :, west_tile], at(1, 1)),
    ]
    for copy in halos[4:] + halos[:4]:
        copy.start()
    for k in near:
        pl.semaphore_signal(here_sem, inc=1, device_id=line_peer(k % n_line), device_id_type=MESH)

    spread_col = lax.broadcasted_iota(jnp.int32, (COLS, WIDTH), 0)
    spread_lane = lax.broadcasted_iota(jnp.int32, (COLS, WIDTH), 1)
    spread = jnp.where((spread_lane >= spread_col * M) & (spread_lane < spread_col * M + M), 1.0, 0.0).astype(BF16)

    def spread_rows(v, start, rows):
        w = wc[v, pl.ds(start, rows), :, 0:COLS].reshape(rows * LEV, COLS)
        a = w.astype(BF16)
        rest = w - a.astype(F32)
        b = rest.astype(BF16)
        c = (rest - b.astype(F32)).astype(BF16)
        wide = (
            jnp.dot(a, spread, preferred_element_type=F32)
            + jnp.dot(b, spread, preferred_element_type=F32)
            + jnp.dot(c, spread, preferred_element_type=F32)
        )
        wx[v, pl.ds(start, rows), :, 0:WIDTH] = wide.reshape(rows, LEV, WIDTH)

    for v in range(3):
        spread_rows(v, 0, ROWS)

    def stencil(c, n, s, u, v, w, first, final):
        width = c.shape[1]
        keep = slice(first, final)
        east, west = pltpu.roll(c, width - M, 1)[:, keep], pltpu.roll(c, M, 1)[:, keep]
        c = c[:, keep]
        above = jnp.where(level == LEV - 1, 0.0, pltpu.roll(c, LEV - 1, 0))
        below = jnp.where(level == 0, 0.0, pltpu.roll(c, 1, 0))
        spread_out = (east + west) + (s + n) + (above + below)
        carried = u * (east - west) + v * (s - n) + w * (above - below)
        return (1.0 - 6.0 * KH) * c + KH * spread_out - carried

    def strip(src, r, width):
        n, s = lax.rem(r + ROWS_X - 1, ROWS_X), lax.rem(r + 1, ROWS_X)
        return stencil(
            src[r, :, 0:width], src[n, :, 0:width], src[s, :, 0:width],
            wx[0, r, :, 0:width], wx[1, r, :, 0:width], wx[2, r, :, 0:width], 0, width,
        )

    def west_end(src, r, first):
        def of(ref, i):
            return jnp.concatenate([ref[i, :, WEST:WEST + 128], ref[i, :, 0:128]], axis=1)[:, first:]

        c = jnp.concatenate([src[r, :, WEST:WEST + 128], src[r, :, 0:256]], axis=1)
        return stencil(
            c, of(src, r - 1), of(src, r + 1), of(wx.at[0], r), of(wx.at[1], r), of(wx.at[2], r), first, 256
        )

    def east_end(src, r, final):
        lanes = slice(WIDTH - 128, WIDTH - 256 + final)
        return stencil(
            src[r, :, WIDTH - 256:WIDTH + 128], src[r - 1, :, lanes], src[r + 1, :, lanes],
            wx[0, r, :, lanes], wx[1, r, :, lanes], wx[2, r, :, lanes], 128, final,
        )

    def put(r, tiles, value):
        for i, t in enumerate(tiles):
            last[t, pl.ds(pl.multiple_of(r * LEV, LEV), LEV), :] = value[:, i * 128:i * 128 + 128]

    def inner_first(r, carry):
        mid[r, :, 0:WIDTH] = strip(field, r, WIDTH)
        return carry

    lax.fori_loop(1, ROWS - 1, inner_first, 0, unroll=2)

    def inner_second(r, carry):
        put(r, range(1, TILES - 1), strip(mid, r, WIDTH)[:, 128:WIDTH - 128])
        return carry

    lax.fori_loop(2, ROWS - 2, inner_second, 0, unroll=2)

    for copy in obs_copies:
        copy.wait()

    def note(k, carry):
        live = jnp.where(k < count[0], 1.0, 0.0)
        vals[0, pl.ds(k, 1), :] = jnp.full((1, 128), live, F32)
        vals[1, pl.ds(k, 1), :] = jnp.full((1, 128), var[k], F32)
        vals[2, pl.ds(k, 1), :] = jnp.full((1, 128), value[k], F32)
        return carry

    lax.fori_loop(0, OBS, note, 0)

    for i in (0, 1, 6, 7):
        halos[i].wait_recv()
    for v in range(3):
        for side, start in ((0, EAST), (1, WEST)):
            got = wcol_in[side]
            for r in range(ROWS):
                wx[v, r, :, start:start + 128] = jnp.broadcast_to(got[:, v * ROWS + r:v * ROWS + r + 1], (LEV, 128))

    def ends_first(r, carry):
        new = west_end(field, r, 0)
        mid[r, :, WEST:WEST + 128] = new[:, 0:128]
        mid[r, :, 0:128] = new[:, 128:256]
        mid[r, :, WIDTH - 128:WIDTH + 128] = east_end(field, r, 384)
        return carry

    lax.fori_loop(1, ROWS - 1, ends_first, 0, unroll=2)

    for i in (2, 3, 4, 5, 8, 9, 10, 11):
        halos[i].wait_recv()
    for v in range(3):
        spread_rows(v, SOUTH, 1)
        spread_rows(v, NORTH, 1)
    has_north, has_south = lat > 0, lat < n_lat - 1
    field[NORTH] = jnp.where(has_north, field[NORTH], 0.0)
    field[SOUTH] = jnp.where(has_south, field[SOUTH], 0.0)
    mid[0] = strip(field, 0, WIDE)
    mid[ROWS - 1] = strip(field, ROWS - 1, WIDE)
    mid[NORTH] = jnp.where(has_north, strip(field, NORTH, WIDE), 0.0)
    mid[SOUTH] = jnp.where(has_south, strip(field, SOUTH, WIDE), 0.0)

    for r in (0, 1, ROWS - 2, ROWS - 1):
        put(r, range(TILES), strip(mid, r, WIDE)[:, 0:WIDTH])

    def ends_second(r, carry):
        put(r, (0,), west_end(mid, r, 128))
        put(r, (TILES - 1,), east_end(mid, r, 256))
        return carry

    lax.fori_loop(2, ROWS - 2, ends_second, 0, unroll=2)

    lane_1 = lax.broadcasted_iota(jnp.int32, (1, 128), 1)

    def look(k, carry):
        row, col, lev = cells[0, k] - lat * ROWS, cells[1, k] - lon * COLS, cells[2, k]
        cell = jnp.clip(row * LEV + lev, 0, LEV * ROWS - 1)
        for t in range(TILES):
            line = last[t, pl.ds(cell, 1), :]
            inside = (lane_1 >= col * M - t * 128) & (lane_1 < col * M + M - t * 128)
            seen[t, pl.ds(k, 1), :] = jnp.where(inside, line, 0.0)
        return carry

    lax.fori_loop(0, OBS, look, 0, unroll=4)
    hx = jnp.concatenate([seen[t] + seen[t + 3] + seen[t + 6] for t in range(3)], axis=1)
    hx = hx + pltpu.roll(hx, GROUP // 2, 1)
    hx = hx + pltpu.roll(hx, GROUP // 4, 1)
    hx = hx + pltpu.roll(hx, GROUP // 8, 1)
    lane_o = lax.broadcasted_iota(jnp.int32, (OBS, 128), 1)
    hbar = jnp.sum(jnp.where(lane_o < M, hx[:, 0:128], 0.0), axis=1, keepdims=True) * (1.0 / M)
    y = hx - hbar
    q = vals[0] / vals[1]
    d = vals[2] - hbar

    y0 = y[:, 0:128]
    y32 = pltpu.roll(y, 32, 1)[:, 0:128]
    w0 = jnp.where(lane_o < 48, y0, jnp.where(lane_o == 96, d, 0.0))
    w1 = jnp.where((lane_o >= 48) & (lane_o < 80), y32, jnp.where(lane_o == 97, d, 0.0))
    w2 = jnp.where((lane_o >= 80) & (lane_o < 96), y0, jnp.where(lane_o == 98, d, 0.0))
    l1 = pltpu.roll(y, GROUP - 16, 1)[:, 0:128]
    l2 = pltpu.roll(y, GROUP - 32, 1)[:, 0:128]
    lhs = jnp.concatenate([q * y0, q * l1, q * l2], axis=0)
    rhs = jnp.concatenate([w0, w1, w2], axis=0)
    packed = lax.dot_general(lhs, rhs, (((0,), (0,)), ((), ())), precision=HP, preferred_element_type=F32)[0:16]
    pack[...] = packed.reshape(2, 8, 128)

    for j in plane_order:
        pltpu.make_async_remote_copy(
            src_ref=pack.at[lax.rem(lat + j // 2, 2)], dst_ref=part1.at[j - 1],
            send_sem=ar_send.at[0], recv_sem=ar_recv.at[0], device_id=plane_peer(j), device_id_type=MESH,
        ).start()

    for t in range(TILES):
        lanes = pl.ds(t % 3 * 128, 128)
        for lev in range(LEV + 1):
            part = last[t, pl.ds(lev, ROWS, stride=LEV), :] if lev < LEV else raw_flux[t]
            hi = part.astype(BF16)
            rows = pl.ds(t // 3 * 144 + lev * ROWS, ROWS)
            high[rows, lanes] = hi
            low[rows, lanes] = (part - hi.astype(F32)).astype(BF16)

    def wait_all(ref, sem):
        pltpu.make_async_copy(ref, ref, sem).wait()

    wait_all(part1, ar_recv.at[0])
    sum1[...] = pack[core] + jnp.sum(part1[...], axis=0)
    pl.semaphore_wait(here_sem, len(near))
    for j in line_order:
        pltpu.make_async_remote_copy(
            src_ref=sum1, dst_ref=part2.at[j - 1],
            send_sem=ar_send.at[1], recv_sem=ar_recv.at[1], device_id=line_peer(j), device_id_type=MESH,
        ).start()
    wait_all(part2, ar_recv.at[1])
    sum2[...] = sum1[...] + jnp.sum(part2[...], axis=0)
    swap = pltpu.make_async_remote_copy(
        src_ref=sum2, dst_ref=part3, send_sem=ar_send.at[2], recv_sem=ar_recv.at[2],
        device_id=partner, device_id_type=MESH,
    )
    swap.start()
    swap.wait_recv()
    mine, other = sum2[...], part3[...]
    total = jnp.concatenate([jnp.where(core == 0, mine, other), jnp.where(core == 0, other, mine)], axis=0)

    lane_p = lax.broadcasted_iota(jnp.int32, (16, 128), 1)
    u0 = jnp.where(lane_p < 48, total, 0.0)
    u1 = jnp.where((lane_p >= 16) & (lane_p < 48), pltpu.roll(total, 128 - 32, 1), 0.0)
    u2 = jnp.where((lane_p >= 32) & (lane_p < 48), pltpu.roll(total, 128 - 48, 1), 0.0)
    upper = jnp.concatenate([u0, u1, u2, jnp.zeros((80, 128), F32)], axis=0)
    flipped = upper.T
    row_s = lax.broadcasted_iota(jnp.int32, (M, M), 0)
    col_s = lax.broadcasted_iota(jnp.int32, (M, M), 1)
    gram = jnp.where(row_s // 16 > col_s // 16, flipped[0:M, 0:M], upper[0:M, 0:M])
    proj = jnp.concatenate([total[:, 96:97], total[:, 97:98], total[:, 98:99]], axis=0)
    eye = jnp.where(row_s == col_s, 1.0, 0.0)

    def dot(a, b):
        return jnp.dot(a, b, precision=HP, preferred_element_type=F32)

    system = (M - 1.0) * eye + gram
    scale = jnp.sqrt(jnp.sum(system * system, keepdims=True))
    root_now = system / scale
    factor = 0.5 * (3.0 * eye - root_now)
    root_now, inverse_now = dot(root_now, factor), factor
    for step in range(1, NS_ITERS):
        factor = 0.5 * (3.0 * eye - dot(inverse_now, root_now))
        if step < NS_ITERS - 1:
            root_now = dot(root_now, factor)
        inverse_now = dot(factor, inverse_now)
    inner = jnp.sum(inverse_now * proj, axis=0, keepdims=True)
    wmean = jnp.sum(inverse_now * inner, axis=1, keepdims=True) / scale
    mixed = wmean + jnp.sqrt((M - 1.0) / scale) * inverse_now
    mixing = mixed - jnp.sum(mixed, axis=0, keepdims=True) * (1.0 / M) + 1.0 / M

    g_high = mixing.astype(BF16)
    g_low = (mixing - g_high.astype(F32)).astype(BF16)
    rep_row = lax.broadcasted_iota(jnp.int32, (M, GROUP), 0)
    rep_lane = lax.broadcasted_iota(jnp.int32, (M, GROUP), 1)
    rep = jnp.where(lax.rem(rep_lane, M) == rep_row, 1.0, 0.0).astype(BF16)
    g_high = jnp.dot(g_high, rep, preferred_element_type=F32)
    g_low = jnp.dot(g_low, rep, preferred_element_type=F32)

    def diagonal(g):
        return jnp.concatenate(
            [jnp.where((rep_lane >= b * M) & (rep_lane < b * M + M), g, 0.0).astype(BF16) for b in range(8)], axis=0
        )

    d_high, d_low = diagonal(g_high), diagonal(g_low)
    for g in range(3):
        hi, lo = high[pl.ds(g * 144, 144), :], low[pl.ds(g * 144, 144), :]
        out = (
            jnp.dot(hi, d_high, preferred_element_type=F32)
            + jnp.dot(lo, d_high, preferred_element_type=F32)
            + jnp.dot(hi, d_low, preferred_element_type=F32)
        )
        lanes = pl.ds(g * GROUP, GROUP)
        tracer_out[:, lanes] = out[0:LEV * ROWS]
        flux_out[:, lanes] = out[LEV * ROWS:]
    for copy in halos:
        copy.wait_send()
    wait_all(part1, ar_send.at[0])
    wait_all(part2, ar_send.at[1])
    swap.wait_send()


def on_device(n_lat, n_lon, tracer, flux, winds, obs_cells, obs_count, obs_value, obs_var):
    hbm, local = pl.BlockSpec(memory_space=pltpu.HBM), pl.BlockSpec(memory_space=pltpu.VMEM)
    n_plane, n_line = 2 * n_lat, n_lon // 2
    vmem = pltpu.VMEM
    tracer_out, flux_out = pl.pallas_call(
        functools.partial(kernel, n_lat, n_lon),
        out_shape=(
            jax.ShapeDtypeStruct((LEV * ROWS, WIDTH), F32),
            jax.ShapeDtypeStruct((ROWS, WIDTH), F32),
        ),
        in_specs=[hbm] * 7,
        out_specs=(local, local),
        scratch_shapes=[
            vmem((TILES, LEV * ROWS, 128), F32),
            vmem((TILES, ROWS, 128), F32),
            vmem((3 * LEV * ROWS, COLS), F32),
            vmem((3 * LEV * ROWS, 128), F32),
            vmem((ROWS_X, LEV, WIDE), F32),
            vmem((ROWS_X, LEV, WIDE), F32),
            vmem((TILES, LEV * ROWS, 128), F32),
            vmem((3, ROWS_X, LEV, 128), F32),
            vmem((3, ROWS_X, LEV, WIDE), F32),
            vmem((2, LEV, 128), F32),
            vmem((2, LEV, 128), F32),
            vmem((TILES, OBS, 128), F32),
            vmem((3, OBS, 128), F32),
            vmem((2, 8, 128), F32),
            vmem((n_plane - 1, 8, 128), F32),
            vmem((n_line - 1, 8, 128), F32),
            vmem((8, 128), F32),
            vmem((8, 128), F32),
            vmem((8, 128), F32),
            vmem((432, GROUP), BF16),
            vmem((432, GROUP), BF16),
            pltpu.SMEM((3, OBS), jnp.int32),
            pltpu.SMEM((1,), jnp.int32),
            pltpu.SMEM((OBS,), F32),
            pltpu.SMEM((OBS,), F32),
            pltpu.SemaphoreType.DMA((5 + 2 * TILES,)),
            pltpu.SemaphoreType.DMA((12,)),
            pltpu.SemaphoreType.DMA((12,)),
            pltpu.SemaphoreType.DMA((3,)),
            pltpu.SemaphoreType.DMA((3,)),
            pltpu.SemaphoreType.REGULAR,
        ],
        compiler_params=pltpu.CompilerParams(
            collective_id=0, has_side_effects=True, vmem_limit_bytes=62 * 1024 * 1024
        ),
        name="analysis",
    )(
        tracer.reshape(LEV * ROWS, WIDTH), flux, winds.reshape(3 * LEV * ROWS, COLS),
        obs_cells.T, obs_count, obs_value, obs_var,
    )
    return tracer_out.reshape(LEV, ROWS, WIDTH), flux_out


def solution(mesh):
    return jax.shard_map(
        functools.partial(on_device, mesh.shape["lat"], mesh.shape["lon"]),
        mesh=mesh,
        in_specs=(
            P(None, "lat", "lon"),
            P("lat", "lon"),
            P(None, None, "lat", "lon"),
            P(("lat", "lon"), None),
            P(("lat", "lon")),
            P(("lat", "lon")),
            P(("lat", "lon")),
        ),
        out_specs=(P(None, "lat", "lon"), P("lat", "lon")),
        check_vma=False,
    )
```

```python
import functools

import jax
import jax.numpy as jnp
from jax import lax
from jax.experimental import pallas as pl
from jax.experimental.pallas import tpu as pltpu
from jax.sharding import PartitionSpec as P

M = 48
NS_ITERS = 5
KH = 0.15
MESH = pl.DeviceIdType.MESH
HP = lax.Precision.HIGHEST
F32 = jnp.float32
BF16 = jnp.bfloat16

LEV, ROWS, COLS, OBS = 8, 16, 24, 16
TILES = 9
WIDTH = COLS * M
WIDE = WIDTH + 256
EAST, WEST = WIDTH, WIDTH + 128
ROWS_X = ROWS + 4
SOUTH, NORTH = ROWS, ROWS + 3
GROUP = 8 * M


def kernel(
    n_lat, n_lon,
    tracer, flux, winds, cells_in, count_in, value_in, var_in,
    tracer_out, flux_out,
    raw, raw_flux, raw_winds, wide_winds, field, mid, last, wc, wx, wcol_out, wcol_in,
    wrow_out, wrow_in, lon_out, lon_in, seen, vals, pack, part1, part2, part3, sum1, sum2, high, low, outs,
    cells, count, value, var, in_sem, out_sem, halo_send, halo_recv, ar_send, ar_recv, here_sem,
):
    lat, lon = lax.axis_index("lat"), lax.axis_index("lon")

    def at(dlat, dlon):
        return (lax.rem(lat + (dlat + n_lat), n_lat), lax.rem(lon + (dlon + n_lon), n_lon))

    sides = [(1, 0), (-1, 0), (0, 1), (0, -1), (1, 1), (1, -1), (-1, 1), (-1, -1)]
    pair = lax.rem(lon, 2)
    base = lon - pair

    def plane_peer(j):
        return (lax.rem(lat + j // 2, n_lat), base + lax.rem(pair + j, 2))

    def line_peer(j):
        return (lat, lax.rem(lon + 2 * j, n_lon))

    core = lax.rem(lat, 2)
    partner = (lat + 1 - 2 * core, lon)
    n_plane, n_line = 2 * n_lat, n_lon // 2

    n_x = n_lat // 4
    x, y = lat // 4, lax.rem(lat // 2, 2) * 2 + pair

    def plane_near(dx, dy, dc):
        to_x, to_y = lax.rem(x + (dx + n_x), n_x), lax.rem(y + (dy + 4), 4)
        return (to_x * 4 + to_y // 2 * 2 + lax.rem(core + dc, 2), base + lax.rem(to_y, 2))

    near_plane = [
        plane_near(dx, dy, dc) for dx in (-1, 1, 0) for dy in (-1, 1, 0) for dc in (1, 0) if (dx, dy, dc) != (0, 0, 0)
    ]
    near_line = [line_peer(k % n_line) for k in (3, -3, 2, -2)]
    near_halo = [at(dlat, dlon) for dlat, dlon in sides]
    plane_order = sorted(range(1, n_plane), key=lambda j: -min(j // 2, n_lat - j // 2))
    line_order = sorted(range(1, n_line), key=lambda j: -min(j, n_line - j))
    barrier = pltpu.get_barrier_semaphore()
    for peer in near_halo + near_line + near_plane:
        pl.semaphore_signal(barrier, inc=1, device_id=peer, device_id_type=MESH)

    copies = [
        pltpu.make_async_copy(winds, raw_winds, in_sem.at[0]),
    ]
    for t in range(TILES):
        lanes = pl.ds(t * 128, 128)
        copies.append(pltpu.make_async_copy(tracer.at[:, lanes], raw.at[t], in_sem.at[1 + t]))
        copies.append(pltpu.make_async_copy(flux.at[:, lanes], raw_flux.at[t], in_sem.at[1 + TILES + t]))
    obs_copies = [
        pltpu.make_async_copy(src, dst, in_sem.at[1 + 2 * TILES + i])
        for i, (src, dst) in enumerate(((cells_in, cells), (count_in, count), (value_in, value), (var_in, var)))
    ]
    for copy in copies + obs_copies:
        copy.start()

    for copy in copies:
        copy.wait()
    level = lax.broadcasted_iota(jnp.int32, (LEV, 1), 0)
    wide_winds[:, 0:COLS] = 0.5 * raw_winds[...]

    def enter(r, carry):
        for t in range(TILES):
            own = raw[t, pl.ds(r, LEV, stride=ROWS), :]
            surface = raw_flux[t, pl.ds(r, 1), :]
            field[r, :, t * 128:t * 128 + 128] = own + jnp.where(level == 0, surface, 0.0)
        for v in range(3):
            wc[v, r] = wide_winds[pl.ds(v * LEV * ROWS + r, LEV, stride=ROWS), :]
        return carry

    lax.fori_loop(0, ROWS, enter, 0)

    lane = lax.broadcasted_iota(jnp.int32, (LEV, 128), 1)

    def edge(r, carry):
        first, final = carry
        for v in range(3):
            w = wc[v, r]
            here = lane == v * ROWS + r
            first = jnp.where(here, w[:, 0:1], first)
            final = jnp.where(here, w[:, COLS - 1:COLS], final)
        return first, final

    zero_tile = jnp.zeros((LEV, 128), F32)
    first, final = lax.fori_loop(0, ROWS, edge, (zero_tile, zero_tile))
    wcol_out[0] = first
    wcol_out[1] = final
    for side, r in ((0, 0), (1, ROWS - 1)):
        packed_row = jnp.where(lane < COLS, wc[0, r], 0.0)
        for v in (1, 2):
            here = (lane >= v * COLS) & (lane < v * COLS + COLS)
            packed_row = jnp.where(here, pltpu.roll(wc[v, r], v * COLS, 1), packed_row)
        wrow_out[side] = packed_row

    def tuck(i, carry):
        for side, start, free, gap in ((0, 0, 0, 2 * M), (1, WIDTH - 128, 32, 0)):
            fourth = field[4 * i + 3, :, start:start + 128]
            for j in range(3):
                shift = (gap - free - 32 * j) % 128
                moved = pltpu.roll(fourth, shift, 1) if shift else fourth
                here = (lane >= gap) & (lane < gap + 32)
                lon_out[side, 3 * i + j] = jnp.where(here, moved, field[4 * i + j, :, start:start + 128])
        return carry

    lax.fori_loop(0, ROWS // 4, tuck, 0)

    pl.semaphore_wait(barrier, len(near_halo + near_line + near_plane))

    def send(i, src, dst, to):
        return pltpu.make_async_remote_copy(
            src_ref=src, dst_ref=dst, send_sem=halo_send.at[i], recv_sem=halo_recv.at[i],
            device_id=to, device_id_type=MESH,
        )

    own_lanes = pl.ds(0, WIDTH)
    left_tile, right_tile = pl.ds(0, 128), pl.ds(WIDTH - 128, 128)
    east_tile, west_tile = pl.ds(EAST, 128), pl.ds(WEST, 128)
    top, bottom = 0, ROWS - 1
    halos = [
        send(0, wcol_out.at[0], wcol_in.at[0], at(0, -1)),
        send(1, wcol_out.at[1], wcol_in.at[1], at(0, 1)),
        send(2, wrow_out.at[0], wrow_in.at[0], at(-1, 0)),
        send(3, wrow_out.at[1], wrow_in.at[1], at(1, 0)),
        send(4, field.at[pl.ds(top, 2), :, own_lanes], field.at[pl.ds(SOUTH, 2), :, own_lanes], at(-1, 0)),
        send(5, field.at[pl.ds(bottom - 1, 2), :, own_lanes], field.at[pl.ds(NORTH - 1, 2), :, own_lanes], at(1, 0)),
        send(6, lon_out.at[0], lon_in.at[0], at(0, -1)),
        send(7, lon_out.at[1], lon_in.at[1], at(0, 1)),
        send(8, field.at[top, :, left_tile], field.at[SOUTH, :, east_tile], at(-1, -1)),
        send(9, field.at[top, :, right_tile], field.at[SOUTH, :, west_tile], at(-1, 1)),
        send(10, field.at[bottom, :, left_tile], field.at[NORTH, :, east_tile], at(1, -1)),
        send(11, field.at[bottom, :, right_tile], field.at[NORTH, :, west_tile], at(1, 1)),
    ]
    for copy in halos:
        copy.start()
    for peer in near_line + near_plane:
        pl.semaphore_signal(here_sem.at[0], inc=1, device_id=peer, device_id_type=MESH)

    spread_col = lax.broadcasted_iota(jnp.int32, (COLS, WIDTH), 0)
    spread_lane = lax.broadcasted_iota(jnp.int32, (COLS, WIDTH), 1)
    spread = jnp.where((spread_lane >= spread_col * M) & (spread_lane < spread_col * M + M), 1.0, 0.0).astype(BF16)

    def spread_rows(w, v, start, rows):
        a = w.astype(BF16)
        rest = w - a.astype(F32)
        b = rest.astype(BF16)
        c = (rest - b.astype(F32)).astype(BF16)
        wide = (
            jnp.dot(a, spread, preferred_element_type=F32)
            + jnp.dot(b, spread, preferred_element_type=F32)
            + jnp.dot(c, spread, preferred_element_type=F32)
        )
        wx[v, pl.ds(start, rows), :, 0:WIDTH] = wide.reshape(rows, LEV, WIDTH)

    for v in range(3):
        spread_rows(wc[v, :, :, 0:COLS].reshape(ROWS * LEV, COLS), v, 0, ROWS)

    def stencil(c, n, s, u, v, w, first, final):
        width = c.shape[1]
        keep = slice(first, final)
        east, west = pltpu.roll(c, width - M, 1)[:, keep], pltpu.roll(c, M, 1)[:, keep]
        c = c[:, keep]
        above = jnp.where(level == LEV - 1, 0.0, pltpu.roll(c, LEV - 1, 0))
        below = jnp.where(level == 0, 0.0, pltpu.roll(c, 1, 0))
        spread_out = (east + west) + (s + n) + (above + below)
        carried = u * (east - west) + v * (s - n) + w * (above - below)
        return (1.0 - 6.0 * KH) * c + KH * spread_out - carried

    def strip(src, r, width):
        n, s = lax.rem(r + ROWS_X - 1, ROWS_X), lax.rem(r + 1, ROWS_X)
        return stencil(
            src[r, :, 0:width], src[n, :, 0:width], src[s, :, 0:width],
            wx[0, r, :, 0:width], wx[1, r, :, 0:width], wx[2, r, :, 0:width], 0, width,
        )

    def west_end(src, r, first):
        def of(ref, i):
            return jnp.concatenate([ref[i, :, WEST:WEST + 128], ref[i, :, 0:128]], axis=1)[:, first:]

        c = jnp.concatenate([src[r, :, WEST:WEST + 128], src[r, :, 0:256]], axis=1)
        return stencil(
            c, of(src, r - 1), of(src, r + 1), of(wx.at[0], r), of(wx.at[1], r), of(wx.at[2], r), first, 256
        )

    def east_end(src, r, final):
        lanes = slice(WIDTH - 128, WIDTH - 256 + final)
        return stencil(
            src[r, :, WIDTH - 256:WIDTH + 128], src[r - 1, :, lanes], src[r + 1, :, lanes],
            wx[0, r, :, lanes], wx[1, r, :, lanes], wx[2, r, :, lanes], 128, final,
        )

    def put(r, tiles, value):
        for i, t in enumerate(tiles):
            last[t, pl.ds(pl.multiple_of(r * LEV, LEV), LEV), :] = value[:, i * 128:i * 128 + 128]

    def inner_first(r, carry):
        mid[r, :, 0:WIDTH] = strip(field, r, WIDTH)
        return carry

    lax.fori_loop(1, ROWS - 1, inner_first, 0, unroll=2)

    def inner_second(r, carry):
        put(r, range(1, TILES - 1), strip(mid, r, WIDTH)[:, 128:WIDTH - 128])
        return carry

    lax.fori_loop(2, ROWS - 2, inner_second, 0, unroll=2)

    for copy in obs_copies:
        copy.wait()

    def note(k, carry):
        live = jnp.where(k < count[0], 1.0, 0.0)
        vals[0, pl.ds(k, 1), :] = jnp.full((1, 128), live, F32)
        vals[1, pl.ds(k, 1), :] = jnp.full((1, 128), var[k], F32)
        vals[2, pl.ds(k, 1), :] = jnp.full((1, 128), value[k], F32)
        return carry

    lax.fori_loop(0, OBS, note, 0)

    pl.semaphore_wait(here_sem.at[0], len(near_line + near_plane))
    for peer in near_line:
        pl.semaphore_signal(here_sem.at[1], inc=1, device_id=peer, device_id_type=MESH)

    for i in range(4):
        halos[i].wait_recv()
    for v in range(3):
        for side, start in ((0, SOUTH), (1, NORTH)):
            spread_rows(wrow_in[side][:, v * COLS:v * COLS + COLS], v, start, 1)
        for side, start in ((0, EAST), (1, WEST)):
            got = wcol_in[side]
            for r in range(ROWS):
                wx[v, r, :, start:start + 128] = jnp.broadcast_to(got[:, v * ROWS + r:v * ROWS + r + 1], (LEV, 128))

    for i in (6, 7):
        halos[i].wait_recv()

    def untuck(i, carry):
        for side, start, free, gap in ((0, EAST, 0, 2 * M), (1, WEST, 32, 0)):
            fourth = zero_tile
            for j in range(3):
                tile = lon_in[side, 3 * i + j]
                field[4 * i + j, :, start:start + 128] = tile
                shift = (free + 32 * j - gap) % 128
                moved = pltpu.roll(tile, shift, 1) if shift else tile
                here = (lane >= free + 32 * j) & (lane < free + 32 * j + 32)
                fourth = jnp.where(here, moved, fourth)
            field[4 * i + 3, :, start:start + 128] = fourth
        return carry

    lax.fori_loop(0, ROWS // 4, untuck, 0, unroll=2)

    def ends_first(r, carry):
        new = west_end(field, r, 0)
        mid[r, :, WEST:WEST + 128] = new[:, 0:128]
        mid[r, :, 0:128] = new[:, 128:256]
        mid[r, :, WIDTH - 128:WIDTH + 128] = east_end(field, r, 384)
        return carry

    lax.fori_loop(1, ROWS - 1, ends_first, 0, unroll=2)

    for i in (4, 5, 8, 9, 10, 11):
        halos[i].wait_recv()
    has_north, has_south = lat > 0, lat < n_lat - 1
    field[NORTH] = jnp.where(has_north, field[NORTH], 0.0)
    field[SOUTH] = jnp.where(has_south, field[SOUTH], 0.0)
    mid[0] = strip(field, 0, WIDE)
    mid[ROWS - 1] = strip(field, ROWS - 1, WIDE)
    mid[NORTH] = jnp.where(has_north, strip(field, NORTH, WIDE), 0.0)
    mid[SOUTH] = jnp.where(has_south, strip(field, SOUTH, WIDE), 0.0)

    for r in (0, 1, ROWS - 2, ROWS - 1):
        put(r, range(TILES), strip(mid, r, WIDE)[:, 0:WIDTH])

    def ends_second(r, carry):
        put(r, (0,), west_end(mid, r, 128))
        put(r, (TILES - 1,), east_end(mid, r, 256))
        return carry

    lax.fori_loop(2, ROWS - 2, ends_second, 0, unroll=2)

    lane_1 = lax.broadcasted_iota(jnp.int32, (1, 128), 1)

    def look(k, carry):
        row, col, lev = cells[0, k] - lat * ROWS, cells[1, k] - lon * COLS, cells[2, k]
        cell = jnp.clip(row * LEV + lev, 0, LEV * ROWS - 1)
        first_lane = col * M
        tile = jnp.clip(first_lane // 128, 0, TILES - 2)
        lines = []
        for t in range(2):
            place = first_lane - (tile + t) * 128
            inside = (lane_1 >= place) & (lane_1 < place + M)
            lines.append(jnp.where(inside, last[tile + t, pl.ds(cell, 1), :], 0.0))
        turn = lax.rem(tile, 3)
        for t in range(3):
            one = jnp.where(turn == t, lines[0], 0.0)
            seen[t, pl.ds(k, 1), :] = jnp.where(turn == (t + 2) % 3, lines[1], one)
        return carry

    lax.fori_loop(0, OBS, look, 0, unroll=4)
    hx = jnp.concatenate([seen[t] for t in range(3)], axis=1)
    hx = hx + pltpu.roll(hx, GROUP // 2, 1)
    hx = hx + pltpu.roll(hx, GROUP // 4, 1)
    hx = hx + pltpu.roll(hx, GROUP // 8, 1)
    lane_o = lax.broadcasted_iota(jnp.int32, (OBS, 128), 1)
    hbar = jnp.sum(jnp.where(lane_o < M, hx[:, 0:128], 0.0), axis=1, keepdims=True) * (1.0 / M)
    y = hx - hbar
    q = vals[0] / vals[1]
    d = vals[2] - hbar

    y0 = y[:, 0:128]
    y32 = pltpu.roll(y, 32, 1)[:, 0:128]
    w0 = jnp.where(lane_o < 48, y0, jnp.where(lane_o == 96, d, 0.0))
    w1 = jnp.where((lane_o >= 48) & (lane_o < 80), y32, jnp.where(lane_o == 97, d, 0.0))
    w2 = jnp.where((lane_o >= 80) & (lane_o < 96), y0, jnp.where(lane_o == 98, d, 0.0))
    l1 = pltpu.roll(y, GROUP - 16, 1)[:, 0:128]
    l2 = pltpu.roll(y, GROUP - 32, 1)[:, 0:128]
    lhs = jnp.concatenate([q * y0, q * l1, q * l2], axis=0)
    rhs = jnp.concatenate([w0, w1, w2], axis=0)
    packed = lax.dot_general(lhs, rhs, (((0,), (0,)), ((), ())), precision=HP, preferred_element_type=F32)[0:16]
    pack[...] = packed.reshape(2, 8, 128)

    for j in plane_order:
        pltpu.make_async_remote_copy(
            src_ref=pack.at[lax.rem(lat + j // 2, 2)], dst_ref=part1.at[j - 1],
            send_sem=ar_send.at[0], recv_sem=ar_recv.at[0], device_id=plane_peer(j), device_id_type=MESH,
        ).start()

    for t in range(TILES):
        lanes = pl.ds(t % 3 * 128, 128)
        for lev in range(LEV + 1):
            part = last[t, pl.ds(lev, ROWS, stride=LEV), :] if lev < LEV else raw_flux[t]
            hi = part.astype(BF16)
            rows = pl.ds(t // 3 * 144 + lev * ROWS, ROWS)
            high[rows, lanes] = hi
            low[rows, lanes] = (part - hi.astype(F32)).astype(BF16)

    def wait_all(ref, sem):
        pltpu.make_async_copy(ref, ref, sem).wait()

    wait_all(part1, ar_recv.at[0])
    sum1[...] = pack[core] + jnp.sum(part1[...], axis=0)
    pl.semaphore_wait(here_sem.at[1], len(near_line))
    for j in line_order:
        pltpu.make_async_remote_copy(
            src_ref=sum1, dst_ref=part2.at[j - 1],
            send_sem=ar_send.at[1], recv_sem=ar_recv.at[1], device_id=line_peer(j), device_id_type=MESH,
        ).start()
    wait_all(part2, ar_recv.at[1])
    sum2[...] = sum1[...] + jnp.sum(part2[...], axis=0)
    swap = pltpu.make_async_remote_copy(
        src_ref=sum2, dst_ref=part3, send_sem=ar_send.at[2], recv_sem=ar_recv.at[2],
        device_id=partner, device_id_type=MESH,
    )
    swap.start()
    swap.wait_recv()
    mine, other = sum2[...], part3[...]
    total = jnp.concatenate([jnp.where(core == 0, mine, other), jnp.where(core == 0, other, mine)], axis=0)

    lane_p = lax.broadcasted_iota(jnp.int32, (16, 128), 1)
    u0 = jnp.where(lane_p < 48, total, 0.0)
    u1 = jnp.where((lane_p >= 16) & (lane_p < 48), pltpu.roll(total, 128 - 32, 1), 0.0)
    u2 = jnp.where((lane_p >= 32) & (lane_p < 48), pltpu.roll(total, 128 - 48, 1), 0.0)
    upper = jnp.concatenate([u0, u1, u2, jnp.zeros((80, 128), F32)], axis=0)
    flipped = upper.T
    row_s = lax.broadcasted_iota(jnp.int32, (M, M), 0)
    col_s = lax.broadcasted_iota(jnp.int32, (M, M), 1)
    gram = jnp.where(row_s // 16 > col_s // 16, flipped[0:M, 0:M], upper[0:M, 0:M])
    proj = jnp.concatenate([total[:, 96:97], total[:, 97:98], total[:, 98:99]], axis=0)
    eye = jnp.where(row_s == col_s, 1.0, 0.0)

    def dot(a, b):
        return jnp.dot(a, b, precision=HP, preferred_element_type=F32)

    system = (M - 1.0) * eye + gram
    scale = jnp.sqrt(jnp.sum(system * system, keepdims=True))
    root_now = system / scale
    factor = 0.5 * (3.0 * eye - root_now)
    root_now, inverse_now = dot(root_now, factor), factor
    for step in range(1, NS_ITERS):
        factor = 0.5 * (3.0 * eye - dot(inverse_now, root_now))
        if step < NS_ITERS - 1:
            root_now = dot(root_now, factor)
        inverse_now = dot(factor, inverse_now)
    inner = jnp.sum(inverse_now * proj, axis=0, keepdims=True)
    wmean = jnp.sum(inverse_now * inner, axis=1, keepdims=True) / scale
    mixed = wmean + jnp.sqrt((M - 1.0) / scale) * inverse_now
    mixing = mixed - jnp.sum(mixed, axis=0, keepdims=True) * (1.0 / M) + 1.0 / M

    g_high = mixing.astype(BF16)
    g_low = (mixing - g_high.astype(F32)).astype(BF16)
    rep_row = lax.broadcasted_iota(jnp.int32, (M, GROUP), 0)
    rep_lane = lax.broadcasted_iota(jnp.int32, (M, GROUP), 1)
    rep = jnp.where(lax.rem(rep_lane, M) == rep_row, 1.0, 0.0).astype(BF16)
    g_high = jnp.dot(g_high, rep, preferred_element_type=F32)
    g_low = jnp.dot(g_low, rep, preferred_element_type=F32)

    def diagonal(g):
        return jnp.concatenate(
            [jnp.where((rep_lane >= b * M) & (rep_lane < b * M + M), g, 0.0).astype(BF16) for b in range(8)], axis=0
        )

    d_high, d_low = diagonal(g_high), diagonal(g_low)
    done = []
    for g in range(3):
        hi, lo = high[pl.ds(g * 144, 144), :], low[pl.ds(g * 144, 144), :]
        out = (
            jnp.dot(hi, d_high, preferred_element_type=F32)
            + jnp.dot(lo, d_high, preferred_element_type=F32)
            + jnp.dot(hi, d_low, preferred_element_type=F32)
        )
        lanes = pl.ds(g * GROUP, GROUP)
        outs[g] = out
        done.append(pltpu.make_async_copy(outs.at[g, pl.ds(0, LEV * ROWS)], tracer_out.at[:, lanes], out_sem.at[g]))
        done.append(pltpu.make_async_copy(outs.at[g, pl.ds(LEV * ROWS, ROWS)], flux_out.at[:, lanes], out_sem.at[3 + g]))
        for copy in done[-2:]:
            copy.start()
    for copy in halos:
        copy.wait_send()
    wait_all(part1, ar_send.at[0])
    wait_all(part2, ar_send.at[1])
    swap.wait_send()
    for copy in done:
        copy.wait()


def hand_on(tracer_in, flux_in, tracer_out, flux_out, sem):
    copies = [pltpu.make_async_copy(flux_in, flux_out, sem.at[LEV])]
    for lev in range(LEV):
        rows = pl.ds(lev * ROWS, ROWS)
        copies.append(pltpu.make_async_copy(tracer_in.at[rows], tracer_out.at[rows], sem.at[lev]))
    for copy in copies:
        copy.start()
    for copy in copies:
        copy.wait()


def on_device(n_lat, n_lon, tracer, flux, winds, obs_cells, obs_count, obs_value, obs_var):
    hbm = pl.BlockSpec(memory_space=pltpu.HBM)
    n_plane, n_line = 2 * n_lat, n_lon // 2
    vmem = pltpu.VMEM
    tracer_out, flux_out = pl.pallas_call(
        functools.partial(kernel, n_lat, n_lon),
        out_shape=(
            jax.ShapeDtypeStruct((LEV * ROWS, WIDTH), F32),
            jax.ShapeDtypeStruct((ROWS, WIDTH), F32),
        ),
        in_specs=[hbm] * 7,
        out_specs=(hbm, hbm),
        scratch_shapes=[
            vmem((TILES, LEV * ROWS, 128), F32),
            vmem((TILES, ROWS, 128), F32),
            vmem((3 * LEV * ROWS, COLS), F32),
            vmem((3 * LEV * ROWS, 128), F32),
            vmem((ROWS_X, LEV, WIDE), F32),
            vmem((ROWS_X, LEV, WIDE), F32),
            vmem((TILES, LEV * ROWS, 128), F32),
            vmem((3, ROWS, LEV, 128), F32),
            vmem((3, ROWS_X, LEV, WIDE), F32),
            vmem((2, LEV, 128), F32),
            vmem((2, LEV, 128), F32),
            vmem((2, LEV, 128), F32),
            vmem((2, LEV, 128), F32),
            vmem((2, 12, LEV, 128), F32),
            vmem((2, 12, LEV, 128), F32),
            vmem((3, OBS, 128), F32),
            vmem((3, OBS, 128), F32),
            vmem((2, 8, 128), F32),
            vmem((n_plane - 1, 8, 128), F32),
            vmem((n_line - 1, 8, 128), F32),
            vmem((8, 128), F32),
            vmem((8, 128), F32),
            vmem((8, 128), F32),
            vmem((432, GROUP), BF16),
            vmem((432, GROUP), BF16),
            vmem((3, 144, GROUP), F32),
            pltpu.SMEM((3, OBS), jnp.int32),
            pltpu.SMEM((1,), jnp.int32),
            pltpu.SMEM((OBS,), F32),
            pltpu.SMEM((OBS,), F32),
            pltpu.SemaphoreType.DMA((5 + 2 * TILES,)),
            pltpu.SemaphoreType.DMA((6,)),
            pltpu.SemaphoreType.DMA((12,)),
            pltpu.SemaphoreType.DMA((12,)),
            pltpu.SemaphoreType.DMA((3,)),
            pltpu.SemaphoreType.DMA((3,)),
            pltpu.SemaphoreType.REGULAR((2,)),
        ],
        compiler_params=pltpu.CompilerParams(
            collective_id=0, has_side_effects=True, vmem_limit_bytes=62 * 1024 * 1024
        ),
        name="analysis",
    )(
        tracer.reshape(LEV * ROWS, WIDTH), flux, winds.reshape(3 * LEV * ROWS, COLS),
        obs_cells.T, obs_count, obs_value, obs_var,
    )
    tracer_out, flux_out = pl.pallas_call(
        hand_on,
        out_shape=(
            jax.ShapeDtypeStruct((LEV * ROWS, WIDTH), F32),
            jax.ShapeDtypeStruct((ROWS, WIDTH), F32),
        ),
        in_specs=[hbm, hbm],
        out_specs=(hbm, hbm),
        scratch_shapes=[pltpu.SemaphoreType.DMA((LEV + 1,))],
        compiler_params=pltpu.CompilerParams(vmem_limit_bytes=62 * 1024 * 1024),
        name="hand_on",
    )(tracer_out, flux_out)
    return tracer_out.reshape(LEV, ROWS, WIDTH), flux_out


def solution(mesh):
    return jax.shard_map(
        functools.partial(on_device, mesh.shape["lat"], mesh.shape["lon"]),
        mesh=mesh,
        in_specs=(
            P(None, "lat", "lon"),
            P("lat", "lon"),
            P(None, None, "lat", "lon"),
            P(("lat", "lon"), None),
            P(("lat", "lon")),
            P(("lat", "lon")),
            P(("lat", "lon")),
        ),
        out_specs=(P(None, "lat", "lon"), P("lat", "lon")),
        check_vma=False,
    )
```

```python
import functools

import jax
import jax.numpy as jnp
from jax import lax
from jax.experimental import pallas as pl
from jax.experimental.pallas import tpu as pltpu
from jax.sharding import PartitionSpec as P

M = 48
NS_ITERS = 5
KH = 0.15
MESH = pl.DeviceIdType.MESH
HP = lax.Precision.HIGHEST
F32 = jnp.float32
BF16 = jnp.bfloat16

LEV, ROWS, COLS, OBS = 8, 16, 24, 16
TILES = 9
WIDTH = COLS * M
WIDE = WIDTH + 256
EAST, WEST = WIDTH, WIDTH + 128
ROWS_X = ROWS + 4
SOUTH, NORTH = ROWS, ROWS + 3
CHUNKS = 4
GROUP = 8 * M


def kernel(
    n_lat, n_lon,
    tracer, flux, winds, cells_in, count_in, value_in, var_in,
    tracer_out, flux_out,
    raw, raw_flux, raw_winds, wide_winds, field, mid, last, wc, wx, wcol_out, wcol_in,
    wrow_out, wrow_in, lon_out, lon_in, seen, vals, pack, part1, part2, part3, sum1, sum2, high, low, outs,
    cells, count, value, var, in_sem, out_sem, halo_send, halo_recv, ar_send, ar_recv, here_sem,
):
    lat, lon = lax.axis_index("lat"), lax.axis_index("lon")

    def at(dlat, dlon):
        return (lax.rem(lat + (dlat + n_lat), n_lat), lax.rem(lon + (dlon + n_lon), n_lon))

    sides = [(1, 0), (-1, 0), (0, 1), (0, -1), (1, 1), (1, -1), (-1, 1), (-1, -1)]
    pair = lax.rem(lon, 2)
    base = lon - pair

    def plane_peer(j):
        return (lax.rem(lat + j // 2, n_lat), base + lax.rem(pair + j, 2))

    def line_peer(j):
        return (lat, lax.rem(lon + 2 * j, n_lon))

    core = lax.rem(lat, 2)
    partner = (lat + 1 - 2 * core, lon)
    n_plane, n_line = 2 * n_lat, n_lon // 2

    n_x = n_lat // 4
    x, y = lat // 4, lax.rem(lat // 2, 2) * 2 + pair

    def plane_near(dx, dy, dc):
        to_x, to_y = lax.rem(x + (dx + n_x), n_x), lax.rem(y + (dy + 4), 4)
        return (to_x * 4 + to_y // 2 * 2 + lax.rem(core + dc, 2), base + lax.rem(to_y, 2))

    near_plane = [
        plane_near(dx, dy, dc) for dx in (-1, 1, 0) for dy in (-1, 1, 0) for dc in (1, 0) if (dx, dy, dc) != (0, 0, 0)
    ]
    near_line = [line_peer(k % n_line) for k in (3, -3, 2, -2)]
    near_halo = [at(dlat, dlon) for dlat, dlon in sides]
    plane_order = sorted(range(1, n_plane), key=lambda j: -min(j // 2, n_lat - j // 2))
    line_order = sorted(range(1, n_line), key=lambda j: -min(j, n_line - j))
    barrier = pltpu.get_barrier_semaphore()
    for peer in near_halo + near_line + near_plane:
        pl.semaphore_signal(barrier, inc=1, device_id=peer, device_id_type=MESH)

    copies = [
        pltpu.make_async_copy(winds, raw_winds, in_sem.at[0]),
    ]
    for t in range(TILES):
        lanes = pl.ds(t * 128, 128)
        copies.append(pltpu.make_async_copy(tracer.at[:, lanes], raw.at[t], in_sem.at[1 + t]))
        copies.append(pltpu.make_async_copy(flux.at[:, lanes], raw_flux.at[t], in_sem.at[1 + TILES + t]))
    obs_copies = [
        pltpu.make_async_copy(src, dst, in_sem.at[1 + 2 * TILES + i])
        for i, (src, dst) in enumerate(((cells_in, cells), (count_in, count), (value_in, value), (var_in, var)))
    ]
    for copy in copies + obs_copies:
        copy.start()

    for copy in copies:
        copy.wait()
    level = lax.broadcasted_iota(jnp.int32, (LEV, 1), 0)
    wide_winds[:, 0:COLS] = 0.5 * raw_winds[...]

    def enter(r, carry):
        for t in range(TILES):
            own = raw[t, pl.ds(r, LEV, stride=ROWS), :]
            surface = raw_flux[t, pl.ds(r, 1), :]
            field[r, :, t * 128:t * 128 + 128] = own + jnp.where(level == 0, surface, 0.0)
        for v in range(3):
            wc[v, r] = wide_winds[pl.ds(v * LEV * ROWS + r, LEV, stride=ROWS), :]
        return carry

    lax.fori_loop(0, ROWS, enter, 0, unroll=8)

    lane = lax.broadcasted_iota(jnp.int32, (LEV, 128), 1)

    def edge(r, carry):
        first, final = carry
        for v in range(3):
            w = wc[v, r]
            here = lane == v * ROWS + r
            first = jnp.where(here, w[:, 0:1], first)
            final = jnp.where(here, w[:, COLS - 1:COLS], final)
        return first, final

    zero_tile = jnp.zeros((LEV, 128), F32)
    first, final = lax.fori_loop(0, ROWS, edge, (zero_tile, zero_tile), unroll=True)
    wcol_out[0] = first
    wcol_out[1] = final
    for side, r in ((0, 0), (1, ROWS - 1)):
        packed_row = jnp.where(lane < COLS, wc[0, r], 0.0)
        for v in (1, 2):
            here = (lane >= v * COLS) & (lane < v * COLS + COLS)
            packed_row = jnp.where(here, pltpu.roll(wc[v, r], v * COLS, 1), packed_row)
        wrow_out[side] = packed_row

    def tuck(i, carry):
        for side, start, free, gap in ((0, 0, 0, 2 * M), (1, WIDTH - 128, 32, 0)):
            fourth = field[4 * i + 3, :, start:start + 128]
            for j in range(3):
                shift = (gap - free - 32 * j) % 128
                moved = pltpu.roll(fourth, shift, 1) if shift else fourth
                here = (lane >= gap) & (lane < gap + 32)
                lon_out[side, 3 * i + j] = jnp.where(here, moved, field[4 * i + j, :, start:start + 128])
        return carry

    lax.fori_loop(0, ROWS // 4, tuck, 0, unroll=True)

    pl.semaphore_wait(barrier, len(near_halo + near_line + near_plane))

    def send(i, src, dst, to):
        return pltpu.make_async_remote_copy(
            src_ref=src, dst_ref=dst, send_sem=halo_send.at[i], recv_sem=halo_recv.at[i],
            device_id=to, device_id_type=MESH,
        )

    own_lanes = pl.ds(0, WIDTH)
    left_tile, right_tile = pl.ds(0, 128), pl.ds(WIDTH - 128, 128)
    east_tile, west_tile = pl.ds(EAST, 128), pl.ds(WEST, 128)
    top, bottom = 0, ROWS - 1
    halos = [
        send(0, wcol_out.at[0], wcol_in.at[0], at(0, -1)),
        send(1, wcol_out.at[1], wcol_in.at[1], at(0, 1)),
        send(2, wrow_out.at[0], wrow_in.at[0], at(-1, 0)),
        send(3, wrow_out.at[1], wrow_in.at[1], at(1, 0)),
        send(4, field.at[pl.ds(top, 2), :, own_lanes], field.at[pl.ds(SOUTH, 2), :, own_lanes], at(-1, 0)),
        send(5, field.at[pl.ds(bottom - 1, 2), :, own_lanes], field.at[pl.ds(NORTH - 1, 2), :, own_lanes], at(1, 0)),
        send(6, lon_out.at[0], lon_in.at[0], at(0, -1)),
        send(7, lon_out.at[1], lon_in.at[1], at(0, 1)),
        send(8, field.at[top, :, left_tile], field.at[SOUTH, :, east_tile], at(-1, -1)),
        send(9, field.at[top, :, right_tile], field.at[SOUTH, :, west_tile], at(-1, 1)),
        send(10, field.at[bottom, :, left_tile], field.at[NORTH, :, east_tile], at(1, -1)),
        send(11, field.at[bottom, :, right_tile], field.at[NORTH, :, west_tile], at(1, 1)),
    ]
    for copy in halos:
        copy.start()
    for peer in near_line + near_plane:
        pl.semaphore_signal(here_sem.at[0], inc=1, device_id=peer, device_id_type=MESH)

    spread_col = lax.broadcasted_iota(jnp.int32, (COLS, WIDTH), 0)
    spread_lane = lax.broadcasted_iota(jnp.int32, (COLS, WIDTH), 1)
    spread = jnp.where((spread_lane >= spread_col * M) & (spread_lane < spread_col * M + M), 1.0, 0.0).astype(BF16)

    def spread_rows(w, v, start, rows):
        a = w.astype(BF16)
        rest = w - a.astype(F32)
        b = rest.astype(BF16)
        c = (rest - b.astype(F32)).astype(BF16)
        wide = (
            jnp.dot(a, spread, preferred_element_type=F32)
            + jnp.dot(b, spread, preferred_element_type=F32)
            + jnp.dot(c, spread, preferred_element_type=F32)
        )
        wx[v, pl.ds(start, rows), :, 0:WIDTH] = wide.reshape(rows, LEV, WIDTH)

    for v in range(3):
        spread_rows(wc[v, :, :, 0:COLS].reshape(ROWS * LEV, COLS), v, 0, ROWS)

    def stencil(c, n, s, u, v, w, first, final):
        width = c.shape[1]
        keep = slice(first, final)
        east, west = pltpu.roll(c, width - M, 1)[:, keep], pltpu.roll(c, M, 1)[:, keep]
        c = c[:, keep]
        above = jnp.where(level == LEV - 1, 0.0, pltpu.roll(c, LEV - 1, 0))
        below = jnp.where(level == 0, 0.0, pltpu.roll(c, 1, 0))
        spread_out = (east + west) + (s + n) + (above + below)
        carried = u * (east - west) + v * (s - n) + w * (above - below)
        return (1.0 - 6.0 * KH) * c + KH * spread_out - carried

    def strip(src, r, width):
        n, s = lax.rem(r + ROWS_X - 1, ROWS_X), lax.rem(r + 1, ROWS_X)
        return stencil(
            src[r, :, 0:width], src[n, :, 0:width], src[s, :, 0:width],
            wx[0, r, :, 0:width], wx[1, r, :, 0:width], wx[2, r, :, 0:width], 0, width,
        )

    def west_end(src, r, first):
        def of(ref, i):
            return jnp.concatenate([ref[i, :, WEST:WEST + 128], ref[i, :, 0:128]], axis=1)[:, first:]

        c = jnp.concatenate([src[r, :, WEST:WEST + 128], src[r, :, 0:256]], axis=1)
        return stencil(
            c, of(src, r - 1), of(src, r + 1), of(wx.at[0], r), of(wx.at[1], r), of(wx.at[2], r), first, 256
        )

    def east_end(src, r, final):
        lanes = slice(WIDTH - 128, WIDTH - 256 + final)
        return stencil(
            src[r, :, WIDTH - 256:WIDTH + 128], src[r - 1, :, lanes], src[r + 1, :, lanes],
            wx[0, r, :, lanes], wx[1, r, :, lanes], wx[2, r, :, lanes], 128, final,
        )

    def put(r, tiles, value):
        for i, t in enumerate(tiles):
            last[t, pl.ds(pl.multiple_of(r * LEV, LEV), LEV), :] = value[:, i * 128:i * 128 + 128]

    def inner_first(r, carry):
        mid[r, :, 0:WIDTH] = strip(field, r, WIDTH)
        return carry

    lax.fori_loop(1, ROWS - 1, inner_first, 0, unroll=2)

    def inner_second(r, carry):
        put(r, range(1, TILES - 1), strip(mid, r, WIDTH)[:, 128:WIDTH - 128])
        return carry

    lax.fori_loop(2, ROWS - 2, inner_second, 0, unroll=2)

    for copy in obs_copies:
        copy.wait()

    def note(k, carry):
        live = jnp.where(k < count[0], 1.0, 0.0)
        vals[0, pl.ds(k, 1), :] = jnp.full((1, 128), live, F32)
        vals[1, pl.ds(k, 1), :] = jnp.full((1, 128), var[k], F32)
        vals[2, pl.ds(k, 1), :] = jnp.full((1, 128), value[k], F32)
        return carry

    lax.fori_loop(0, OBS, note, 0)

    pl.semaphore_wait(here_sem.at[0], len(near_line + near_plane))
    for peer in near_line:
        pl.semaphore_signal(here_sem.at[1], inc=1, device_id=peer, device_id_type=MESH)

    for i in range(4):
        halos[i].wait_recv()
    for v in range(3):
        for side, start in ((0, SOUTH), (1, NORTH)):
            spread_rows(wrow_in[side][:, v * COLS:v * COLS + COLS], v, start, 1)
        for side, start in ((0, EAST), (1, WEST)):
            got = wcol_in[side]
            for r in range(ROWS):
                wx[v, r, :, start:start + 128] = jnp.broadcast_to(got[:, v * ROWS + r:v * ROWS + r + 1], (LEV, 128))

    for i in (6, 7):
        halos[i].wait_recv()

    def untuck(i, carry):
        for side, start, free, gap in ((0, EAST, 0, 2 * M), (1, WEST, 32, 0)):
            fourth = zero_tile
            for j in range(3):
                tile = lon_in[side, 3 * i + j]
                field[4 * i + j, :, start:start + 128] = tile
                shift = (free + 32 * j - gap) % 128
                moved = pltpu.roll(tile, shift, 1) if shift else tile
                here = (lane >= free + 32 * j) & (lane < free + 32 * j + 32)
                fourth = jnp.where(here, moved, fourth)
            field[4 * i + 3, :, start:start + 128] = fourth
        return carry

    lax.fori_loop(0, ROWS // 4, untuck, 0, unroll=True)

    def ends_first(r, carry):
        new = west_end(field, r, 0)
        mid[r, :, WEST:WEST + 128] = new[:, 0:128]
        mid[r, :, 0:128] = new[:, 128:256]
        mid[r, :, WIDTH - 128:WIDTH + 128] = east_end(field, r, 384)
        return carry

    lax.fori_loop(1, ROWS - 1, ends_first, 0, unroll=7)

    for i in (4, 5, 8, 9, 10, 11):
        halos[i].wait_recv()
    has_north, has_south = lat > 0, lat < n_lat - 1
    field[NORTH] = jnp.where(has_north, field[NORTH], 0.0)
    field[SOUTH] = jnp.where(has_south, field[SOUTH], 0.0)
    mid[0] = strip(field, 0, WIDE)
    mid[ROWS - 1] = strip(field, ROWS - 1, WIDE)
    mid[NORTH] = jnp.where(has_north, strip(field, NORTH, WIDE), 0.0)
    mid[SOUTH] = jnp.where(has_south, strip(field, SOUTH, WIDE), 0.0)

    for r in (0, 1, ROWS - 2, ROWS - 1):
        put(r, range(TILES), strip(mid, r, WIDE)[:, 0:WIDTH])

    def ends_second(r, carry):
        put(r, (0,), west_end(mid, r, 128))
        put(r, (TILES - 1,), east_end(mid, r, 256))
        return carry

    lax.fori_loop(2, ROWS - 2, ends_second, 0, unroll=6)

    lane_1 = lax.broadcasted_iota(jnp.int32, (1, 128), 1)

    def look(k, carry):
        row, col, lev = cells[0, k] - lat * ROWS, cells[1, k] - lon * COLS, cells[2, k]
        cell = jnp.clip(row * LEV + lev, 0, LEV * ROWS - 1)
        first_lane = col * M
        tile = jnp.clip(first_lane // 128, 0, TILES - 2)
        lines = []
        for t in range(2):
            place = first_lane - (tile + t) * 128
            inside = (lane_1 >= place) & (lane_1 < place + M)
            lines.append(jnp.where(inside, last[tile + t, pl.ds(cell, 1), :], 0.0))
        turn = lax.rem(tile, 3)
        for t in range(3):
            one = jnp.where(turn == t, lines[0], 0.0)
            seen[t, pl.ds(k, 1), :] = jnp.where(turn == (t + 2) % 3, lines[1], one)
        return carry

    lax.fori_loop(0, OBS, look, 0, unroll=True)
    hx = jnp.concatenate([seen[t] for t in range(3)], axis=1)
    hx = hx + pltpu.roll(hx, GROUP // 2, 1)
    hx = hx + pltpu.roll(hx, GROUP // 4, 1)
    hx = hx + pltpu.roll(hx, GROUP // 8, 1)
    lane_o = lax.broadcasted_iota(jnp.int32, (OBS, 128), 1)
    hbar = jnp.sum(jnp.where(lane_o < M, hx[:, 0:128], 0.0), axis=1, keepdims=True) * (1.0 / M)
    y = hx - hbar
    q = vals[0] / vals[1]
    d = vals[2] - hbar

    y0 = y[:, 0:128]
    y32 = pltpu.roll(y, 32, 1)[:, 0:128]
    w0 = jnp.where(lane_o < 48, y0, jnp.where(lane_o == 96, d, 0.0))
    w1 = jnp.where((lane_o >= 48) & (lane_o < 80), y32, jnp.where(lane_o == 97, d, 0.0))
    w2 = jnp.where((lane_o >= 80) & (lane_o < 96), y0, jnp.where(lane_o == 98, d, 0.0))
    l1 = pltpu.roll(y, GROUP - 16, 1)[:, 0:128]
    l2 = pltpu.roll(y, GROUP - 32, 1)[:, 0:128]
    lhs = jnp.concatenate([q * y0, q * l1, q * l2], axis=0)
    rhs = jnp.concatenate([w0, w1, w2], axis=0)
    packed = lax.dot_general(lhs, rhs, (((0,), (0,)), ((), ())), precision=HP, preferred_element_type=F32)[0:16]
    pack[...] = packed.reshape(2, 8, 128)

    for j in plane_order:
        pltpu.make_async_remote_copy(
            src_ref=pack.at[lax.rem(lat + j // 2, 2)], dst_ref=part1.at[j - 1],
            send_sem=ar_send.at[0], recv_sem=ar_recv.at[0], device_id=plane_peer(j), device_id_type=MESH,
        ).start()

    for t in range(TILES):
        lanes = pl.ds(t % 3 * 128, 128)
        for lev in range(LEV + 1):
            part = last[t, pl.ds(lev, ROWS, stride=LEV), :] if lev < LEV else raw_flux[t]
            hi = part.astype(BF16)
            rows = pl.ds(t // 3 * 144 + lev * ROWS, ROWS)
            high[rows, lanes] = hi
            low[rows, lanes] = (part - hi.astype(F32)).astype(BF16)

    def wait_all(ref, sem):
        pltpu.make_async_copy(ref, ref, sem).wait()

    wait_all(part1, ar_recv.at[0])
    sum1[...] = pack[core] + jnp.sum(part1[...], axis=0)
    pl.semaphore_wait(here_sem.at[1], len(near_line))
    for j in line_order:
        pltpu.make_async_remote_copy(
            src_ref=sum1, dst_ref=part2.at[j - 1],
            send_sem=ar_send.at[1], recv_sem=ar_recv.at[1], device_id=line_peer(j), device_id_type=MESH,
        ).start()
    wait_all(part2, ar_recv.at[1])
    sum2[...] = sum1[...] + jnp.sum(part2[...], axis=0)
    swap = pltpu.make_async_remote_copy(
        src_ref=sum2, dst_ref=part3, send_sem=ar_send.at[2], recv_sem=ar_recv.at[2],
        device_id=partner, device_id_type=MESH,
    )
    swap.start()
    swap.wait_recv()
    mine, other = sum2[...], part3[...]
    total = jnp.concatenate([jnp.where(core == 0, mine, other), jnp.where(core == 0, other, mine)], axis=0)

    lane_p = lax.broadcasted_iota(jnp.int32, (16, 128), 1)
    u0 = jnp.where(lane_p < 48, total, 0.0)
    u1 = jnp.where((lane_p >= 16) & (lane_p < 48), pltpu.roll(total, 128 - 32, 1), 0.0)
    u2 = jnp.where((lane_p >= 32) & (lane_p < 48), pltpu.roll(total, 128 - 48, 1), 0.0)
    upper = jnp.concatenate([u0, u1, u2, jnp.zeros((80, 128), F32)], axis=0)
    flipped = upper.T
    row_s = lax.broadcasted_iota(jnp.int32, (M, M), 0)
    col_s = lax.broadcasted_iota(jnp.int32, (M, M), 1)
    gram = jnp.where(row_s // 16 > col_s // 16, flipped[0:M, 0:M], upper[0:M, 0:M])
    proj = jnp.concatenate([total[:, 96:97], total[:, 97:98], total[:, 98:99]], axis=0)
    eye = jnp.where(row_s == col_s, 1.0, 0.0)

    def dot(a, b):
        return jnp.dot(a, b, precision=HP, preferred_element_type=F32)

    system = (M - 1.0) * eye + gram
    scale = jnp.sqrt(jnp.sum(system * system, keepdims=True))
    root_now = system / scale
    factor = 0.5 * (3.0 * eye - root_now)
    root_now, inverse_now = dot(root_now, factor), factor
    for step in range(1, NS_ITERS):
        factor = 0.5 * (3.0 * eye - dot(inverse_now, root_now))
        if step < NS_ITERS - 1:
            root_now = dot(root_now, factor)
        inverse_now = dot(factor, inverse_now)
    inner = jnp.sum(inverse_now * proj, axis=0, keepdims=True)
    wmean = jnp.sum(inverse_now * inner, axis=1, keepdims=True) / scale
    mixed = wmean + jnp.sqrt((M - 1.0) / scale) * inverse_now
    mixing = mixed - jnp.sum(mixed, axis=0, keepdims=True) * (1.0 / M) + 1.0 / M

    g_high = mixing.astype(BF16)
    g_low = (mixing - g_high.astype(F32)).astype(BF16)
    rep_row = lax.broadcasted_iota(jnp.int32, (M, GROUP), 0)
    rep_lane = lax.broadcasted_iota(jnp.int32, (M, GROUP), 1)
    rep = jnp.where(lax.rem(rep_lane, M) == rep_row, 1.0, 0.0).astype(BF16)
    g_high = jnp.dot(g_high, rep, preferred_element_type=F32)
    g_low = jnp.dot(g_low, rep, preferred_element_type=F32)

    def diagonal(g):
        return jnp.concatenate(
            [jnp.where((rep_lane >= b * M) & (rep_lane < b * M + M), g, 0.0).astype(BF16) for b in range(8)], axis=0
        )

    d_high, d_low = diagonal(g_high), diagonal(g_low)
    done = []
    for g in range(3):
        hi, lo = high[pl.ds(g * 144, 144), :], low[pl.ds(g * 144, 144), :]
        out = (
            jnp.dot(hi, d_high, preferred_element_type=F32)
            + jnp.dot(lo, d_high, preferred_element_type=F32)
            + jnp.dot(hi, d_low, preferred_element_type=F32)
        )
        lanes = pl.ds(g * GROUP, GROUP)
        outs[g] = out
        done.append(pltpu.make_async_copy(outs.at[g, pl.ds(0, LEV * ROWS)], tracer_out.at[:, lanes], out_sem.at[g]))
        done.append(pltpu.make_async_copy(outs.at[g, pl.ds(LEV * ROWS, ROWS)], flux_out.at[:, lanes], out_sem.at[3 + g]))
        for copy in done[-2:]:
            copy.start()
    for copy in halos:
        copy.wait_send()
    wait_all(part1, ar_send.at[0])
    wait_all(part2, ar_send.at[1])
    swap.wait_send()
    for copy in done:
        copy.wait()


def hand_on(tracer_in, flux_in, tracer_out, flux_out, held, held_flux, in_sem, out_sem):
    parts = [(flux_in, held_flux, flux_out)]
    for i in range(CHUNKS):
        rows = pl.ds(i * (LEV * ROWS // CHUNKS), LEV * ROWS // CHUNKS)
        parts.append((tracer_in.at[rows], held.at[rows], tracer_out.at[rows]))
    into = [pltpu.make_async_copy(src, mid, in_sem.at[i]) for i, (src, mid, _) in enumerate(parts)]
    out = [pltpu.make_async_copy(mid, dst, out_sem.at[i]) for i, (_, mid, dst) in enumerate(parts)]
    for copy in into:
        copy.start()
    for first, second in zip(into, out):
        first.wait()
        second.start()
    for copy in out:
        copy.wait()


def on_device(n_lat, n_lon, tracer, flux, winds, obs_cells, obs_count, obs_value, obs_var):
    hbm = pl.BlockSpec(memory_space=pltpu.HBM)
    n_plane, n_line = 2 * n_lat, n_lon // 2
    vmem = pltpu.VMEM
    tracer_out, flux_out = pl.pallas_call(
        functools.partial(kernel, n_lat, n_lon),
        out_shape=(
            jax.ShapeDtypeStruct((LEV * ROWS, WIDTH), F32),
            jax.ShapeDtypeStruct((ROWS, WIDTH), F32),
        ),
        in_specs=[hbm] * 7,
        out_specs=(hbm, hbm),
        scratch_shapes=[
            vmem((TILES, LEV * ROWS, 128), F32),
            vmem((TILES, ROWS, 128), F32),
            vmem((3 * LEV * ROWS, COLS), F32),
            vmem((3 * LEV * ROWS, 128), F32),
            vmem((ROWS_X, LEV, WIDE), F32),
            vmem((ROWS_X, LEV, WIDE), F32),
            vmem((TILES, LEV * ROWS, 128), F32),
            vmem((3, ROWS, LEV, 128), F32),
            vmem((3, ROWS_X, LEV, WIDE), F32),
            vmem((2, LEV, 128), F32),
            vmem((2, LEV, 128), F32),
            vmem((2, LEV, 128), F32),
            vmem((2, LEV, 128), F32),
            vmem((2, 12, LEV, 128), F32),
            vmem((2, 12, LEV, 128), F32),
            vmem((3, OBS, 128), F32),
            vmem((3, OBS, 128), F32),
            vmem((2, 8, 128), F32),
            vmem((n_plane - 1, 8, 128), F32),
            vmem((n_line - 1, 8, 128), F32),
            vmem((8, 128), F32),
            vmem((8, 128), F32),
            vmem((8, 128), F32),
            vmem((432, GROUP), BF16),
            vmem((432, GROUP), BF16),
            vmem((3, 144, GROUP), F32),
            pltpu.SMEM((3, OBS), jnp.int32),
            pltpu.SMEM((1,), jnp.int32),
            pltpu.SMEM((OBS,), F32),
            pltpu.SMEM((OBS,), F32),
            pltpu.SemaphoreType.DMA((5 + 2 * TILES,)),
            pltpu.SemaphoreType.DMA((6,)),
            pltpu.SemaphoreType.DMA((12,)),
            pltpu.SemaphoreType.DMA((12,)),
            pltpu.SemaphoreType.DMA((3,)),
            pltpu.SemaphoreType.DMA((3,)),
            pltpu.SemaphoreType.REGULAR((2,)),
        ],
        compiler_params=pltpu.CompilerParams(
            collective_id=0, has_side_effects=True, vmem_limit_bytes=62 * 1024 * 1024
        ),
        name="analysis",
    )(
        tracer.reshape(LEV * ROWS, WIDTH), flux, winds.reshape(3 * LEV * ROWS, COLS),
        obs_cells.T, obs_count, obs_value, obs_var,
    )
    tracer_out, flux_out = pl.pallas_call(
        hand_on,
        out_shape=(
            jax.ShapeDtypeStruct((LEV * ROWS, WIDTH), F32),
            jax.ShapeDtypeStruct((ROWS, WIDTH), F32),
        ),
        in_specs=[hbm, hbm],
        out_specs=(hbm, hbm),
        scratch_shapes=[
            vmem((LEV * ROWS, WIDTH), F32),
            vmem((ROWS, WIDTH), F32),
            pltpu.SemaphoreType.DMA((CHUNKS + 1,)),
            pltpu.SemaphoreType.DMA((CHUNKS + 1,)),
        ],
        compiler_params=pltpu.CompilerParams(vmem_limit_bytes=62 * 1024 * 1024),
        name="hand_on",
    )(tracer_out, flux_out)
    return tracer_out.reshape(LEV, ROWS, WIDTH), flux_out


def solution(mesh):
    return jax.shard_map(
        functools.partial(on_device, mesh.shape["lat"], mesh.shape["lon"]),
        mesh=mesh,
        in_specs=(
            P(None, "lat", "lon"),
            P("lat", "lon"),
            P(None, None, "lat", "lon"),
            P(("lat", "lon"), None),
            P(("lat", "lon")),
            P(("lat", "lon")),
            P(("lat", "lon")),
        ),
        out_specs=(P(None, "lat", "lon"), P("lat", "lon")),
        check_vma=False,
    )
```

```python
import functools

import jax
import jax.numpy as jnp
from jax import lax
from jax.experimental import pallas as pl
from jax.experimental.pallas import tpu as pltpu
from jax.sharding import PartitionSpec as P

M = 48
NS_ITERS = 5
KH = 0.15
MESH = pl.DeviceIdType.MESH
HP = lax.Precision.HIGHEST
F32 = jnp.float32
BF16 = jnp.bfloat16

LEV, ROWS, COLS, OBS = 8, 16, 24, 16
TILES = 9
WIDTH = COLS * M
WIDE = WIDTH + 256
EAST, WEST = WIDTH, WIDTH + 128
ROWS_X = ROWS + 4
SOUTH, NORTH = ROWS, ROWS + 3
GROUP = 8 * M


def kernel(
    n_lat, n_lon,
    tracer, flux, winds, cells_in, count_in, value_in, var_in,
    high_out, low_out, mix_out,
    raw, raw_flux, raw_winds, wide_winds, field, mid, last, wc, wx, wcol_out, wcol_in,
    wrow_out, wrow_in, lon_out, lon_in, seen, vals, pack, part1, part2, part3, sum1, sum2, high, low, mix,
    cells, count, value, var, in_sem, out_sem, halo_send, halo_recv, ar_send, ar_recv, here_sem,
):
    lat, lon = lax.axis_index("lat"), lax.axis_index("lon")

    def at(dlat, dlon):
        return (lax.rem(lat + (dlat + n_lat), n_lat), lax.rem(lon + (dlon + n_lon), n_lon))

    sides = [(1, 0), (-1, 0), (0, 1), (0, -1), (1, 1), (1, -1), (-1, 1), (-1, -1)]
    pair = lax.rem(lon, 2)
    base = lon - pair

    def plane_peer(j):
        return (lax.rem(lat + j // 2, n_lat), base + lax.rem(pair + j, 2))

    def line_peer(j):
        return (lat, lax.rem(lon + 2 * j, n_lon))

    core = lax.rem(lat, 2)
    partner = (lat + 1 - 2 * core, lon)
    n_plane, n_line = 2 * n_lat, n_lon // 2

    n_x = n_lat // 4
    x, y = lat // 4, lax.rem(lat // 2, 2) * 2 + pair

    def plane_near(dx, dy, dc):
        to_x, to_y = lax.rem(x + (dx + n_x), n_x), lax.rem(y + (dy + 4), 4)
        return (to_x * 4 + to_y // 2 * 2 + lax.rem(core + dc, 2), base + lax.rem(to_y, 2))

    near_plane = [
        plane_near(dx, dy, dc) for dx in (-1, 1, 0) for dy in (-1, 1, 0) for dc in (1, 0) if (dx, dy, dc) != (0, 0, 0)
    ]
    near_line = [line_peer(k % n_line) for k in (3, -3, 2, -2)]
    near_halo = [at(dlat, dlon) for dlat, dlon in sides]
    plane_order = sorted(range(1, n_plane), key=lambda j: -min(j // 2, n_lat - j // 2))
    line_order = sorted(range(1, n_line), key=lambda j: -min(j, n_line - j))
    barrier = pltpu.get_barrier_semaphore()
    for peer in near_halo + near_line + near_plane:
        pl.semaphore_signal(barrier, inc=1, device_id=peer, device_id_type=MESH)

    copies = [
        pltpu.make_async_copy(winds, raw_winds, in_sem.at[0]),
    ]
    for t in range(TILES):
        lanes = pl.ds(t * 128, 128)
        copies.append(pltpu.make_async_copy(tracer.at[:, lanes], raw.at[t], in_sem.at[1 + t]))
        copies.append(pltpu.make_async_copy(flux.at[:, lanes], raw_flux.at[t], in_sem.at[1 + TILES + t]))
    obs_copies = [
        pltpu.make_async_copy(src, dst, in_sem.at[1 + 2 * TILES + i])
        for i, (src, dst) in enumerate(((cells_in, cells), (count_in, count), (value_in, value), (var_in, var)))
    ]
    for copy in copies + obs_copies:
        copy.start()

    for copy in copies:
        copy.wait()
    level = lax.broadcasted_iota(jnp.int32, (LEV, 1), 0)
    wide_winds[:, 0:COLS] = 0.5 * raw_winds[...]

    def enter(r, carry):
        for t in range(TILES):
            own = raw[t, pl.ds(r, LEV, stride=ROWS), :]
            surface = raw_flux[t, pl.ds(r, 1), :]
            field[r, :, t * 128:t * 128 + 128] = own + jnp.where(level == 0, surface, 0.0)
        for v in range(3):
            wc[v, r] = wide_winds[pl.ds(v * LEV * ROWS + r, LEV, stride=ROWS), :]
        return carry

    lax.fori_loop(0, ROWS, enter, 0, unroll=8)

    lane = lax.broadcasted_iota(jnp.int32, (LEV, 128), 1)

    def edge(r, carry):
        first, final = carry
        for v in range(3):
            w = wc[v, r]
            here = lane == v * ROWS + r
            first = jnp.where(here, w[:, 0:1], first)
            final = jnp.where(here, w[:, COLS - 1:COLS], final)
        return first, final

    zero_tile = jnp.zeros((LEV, 128), F32)
    first, final = lax.fori_loop(0, ROWS, edge, (zero_tile, zero_tile), unroll=True)
    wcol_out[0] = first
    wcol_out[1] = final
    for side, r in ((0, 0), (1, ROWS - 1)):
        packed_row = jnp.where(lane < COLS, wc[0, r], 0.0)
        for v in (1, 2):
            here = (lane >= v * COLS) & (lane < v * COLS + COLS)
            packed_row = jnp.where(here, pltpu.roll(wc[v, r], v * COLS, 1), packed_row)
        wrow_out[side] = packed_row

    def tuck(i, carry):
        for side, start, free, gap in ((0, 0, 0, 2 * M), (1, WIDTH - 128, 32, 0)):
            fourth = field[4 * i + 3, :, start:start + 128]
            for j in range(3):
                shift = (gap - free - 32 * j) % 128
                moved = pltpu.roll(fourth, shift, 1) if shift else fourth
                here = (lane >= gap) & (lane < gap + 32)
                lon_out[side, 3 * i + j] = jnp.where(here, moved, field[4 * i + j, :, start:start + 128])
        return carry

    lax.fori_loop(0, ROWS // 4, tuck, 0, unroll=True)

    pl.semaphore_wait(barrier, len(near_halo + near_line + near_plane))

    def send(i, src, dst, to):
        return pltpu.make_async_remote_copy(
            src_ref=src, dst_ref=dst, send_sem=halo_send.at[i], recv_sem=halo_recv.at[i],
            device_id=to, device_id_type=MESH,
        )

    own_lanes = pl.ds(0, WIDTH)
    left_tile, right_tile = pl.ds(0, 128), pl.ds(WIDTH - 128, 128)
    east_tile, west_tile = pl.ds(EAST, 128), pl.ds(WEST, 128)
    top, bottom = 0, ROWS - 1
    halos = [
        send(0, wcol_out.at[0], wcol_in.at[0], at(0, -1)),
        send(1, wcol_out.at[1], wcol_in.at[1], at(0, 1)),
        send(2, wrow_out.at[0], wrow_in.at[0], at(-1, 0)),
        send(3, wrow_out.at[1], wrow_in.at[1], at(1, 0)),
        send(4, field.at[pl.ds(top, 2), :, own_lanes], field.at[pl.ds(SOUTH, 2), :, own_lanes], at(-1, 0)),
        send(5, field.at[pl.ds(bottom - 1, 2), :, own_lanes], field.at[pl.ds(NORTH - 1, 2), :, own_lanes], at(1, 0)),
        send(6, lon_out.at[0], lon_in.at[0], at(0, -1)),
        send(7, lon_out.at[1], lon_in.at[1], at(0, 1)),
        send(8, field.at[top, :, left_tile], field.at[SOUTH, :, east_tile], at(-1, -1)),
        send(9, field.at[top, :, right_tile], field.at[SOUTH, :, west_tile], at(-1, 1)),
        send(10, field.at[bottom, :, left_tile], field.at[NORTH, :, east_tile], at(1, -1)),
        send(11, field.at[bottom, :, right_tile], field.at[NORTH, :, west_tile], at(1, 1)),
    ]
    for copy in halos:
        copy.start()
    for peer in near_line + near_plane:
        pl.semaphore_signal(here_sem.at[0], inc=1, device_id=peer, device_id_type=MESH)

    spread_col = lax.broadcasted_iota(jnp.int32, (COLS, WIDTH), 0)
    spread_lane = lax.broadcasted_iota(jnp.int32, (COLS, WIDTH), 1)
    spread = jnp.where((spread_lane >= spread_col * M) & (spread_lane < spread_col * M + M), 1.0, 0.0).astype(BF16)

    def spread_rows(w, v, start, rows):
        a = w.astype(BF16)
        rest = w - a.astype(F32)
        b = rest.astype(BF16)
        c = (rest - b.astype(F32)).astype(BF16)
        wide = (
            jnp.dot(a, spread, preferred_element_type=F32)
            + jnp.dot(b, spread, preferred_element_type=F32)
            + jnp.dot(c, spread, preferred_element_type=F32)
        )
        wx[v, pl.ds(start, rows), :, 0:WIDTH] = wide.reshape(rows, LEV, WIDTH)

    for v in range(3):
        spread_rows(wc[v, :, :, 0:COLS].reshape(ROWS * LEV, COLS), v, 0, ROWS)

    def stencil(c, n, s, u, v, w, first, final):
        width = c.shape[1]
        keep = slice(first, final)
        east, west = pltpu.roll(c, width - M, 1)[:, keep], pltpu.roll(c, M, 1)[:, keep]
        c = c[:, keep]
        above = jnp.where(level == LEV - 1, 0.0, pltpu.roll(c, LEV - 1, 0))
        below = jnp.where(level == 0, 0.0, pltpu.roll(c, 1, 0))
        spread_out = (east + west) + (s + n) + (above + below)
        carried = u * (east - west) + v * (s - n) + w * (above - below)
        return (1.0 - 6.0 * KH) * c + KH * spread_out - carried

    def strip(src, r, width):
        n, s = lax.rem(r + ROWS_X - 1, ROWS_X), lax.rem(r + 1, ROWS_X)
        return stencil(
            src[r, :, 0:width], src[n, :, 0:width], src[s, :, 0:width],
            wx[0, r, :, 0:width], wx[1, r, :, 0:width], wx[2, r, :, 0:width], 0, width,
        )

    def west_end(src, r, first):
        def of(ref, i):
            return jnp.concatenate([ref[i, :, WEST:WEST + 128], ref[i, :, 0:128]], axis=1)[:, first:]

        c = jnp.concatenate([src[r, :, WEST:WEST + 128], src[r, :, 0:256]], axis=1)
        return stencil(
            c, of(src, r - 1), of(src, r + 1), of(wx.at[0], r), of(wx.at[1], r), of(wx.at[2], r), first, 256
        )

    def east_end(src, r, final):
        lanes = slice(WIDTH - 128, WIDTH - 256 + final)
        return stencil(
            src[r, :, WIDTH - 256:WIDTH + 128], src[r - 1, :, lanes], src[r + 1, :, lanes],
            wx[0, r, :, lanes], wx[1, r, :, lanes], wx[2, r, :, lanes], 128, final,
        )

    def put(r, tiles, value):
        for i, t in enumerate(tiles):
            last[t, pl.ds(pl.multiple_of(r * LEV, LEV), LEV), :] = value[:, i * 128:i * 128 + 128]

    def inner_first(r, carry):
        mid[r, :, 0:WIDTH] = strip(field, r, WIDTH)
        return carry

    lax.fori_loop(1, ROWS - 1, inner_first, 0, unroll=2)

    def inner_second(r, carry):
        put(r, range(1, TILES - 1), strip(mid, r, WIDTH)[:, 128:WIDTH - 128])
        return carry

    lax.fori_loop(2, ROWS - 2, inner_second, 0, unroll=2)

    for copy in obs_copies:
        copy.wait()

    def note(k, carry):
        live = jnp.where(k < count[0], 1.0, 0.0)
        vals[0, pl.ds(k, 1), :] = jnp.full((1, 128), live, F32)
        vals[1, pl.ds(k, 1), :] = jnp.full((1, 128), var[k], F32)
        vals[2, pl.ds(k, 1), :] = jnp.full((1, 128), value[k], F32)
        return carry

    lax.fori_loop(0, OBS, note, 0)

    pl.semaphore_wait(here_sem.at[0], len(near_line + near_plane))
    for peer in near_line:
        pl.semaphore_signal(here_sem.at[1], inc=1, device_id=peer, device_id_type=MESH)

    for i in range(4):
        halos[i].wait_recv()
    for v in range(3):
        for side, start in ((0, SOUTH), (1, NORTH)):
            spread_rows(wrow_in[side][:, v * COLS:v * COLS + COLS], v, start, 1)
        for side, start in ((0, EAST), (1, WEST)):
            got = wcol_in[side]
            for r in range(ROWS):
                wx[v, r, :, start:start + 128] = jnp.broadcast_to(got[:, v * ROWS + r:v * ROWS + r + 1], (LEV, 128))

    for i in (6, 7):
        halos[i].wait_recv()

    def untuck(i, carry):
        for side, start, free, gap in ((0, EAST, 0, 2 * M), (1, WEST, 32, 0)):
            fourth = zero_tile
            for j in range(3):
                tile = lon_in[side, 3 * i + j]
                field[4 * i + j, :, start:start + 128] = tile
                shift = (free + 32 * j - gap) % 128
                moved = pltpu.roll(tile, shift, 1) if shift else tile
                here = (lane >= free + 32 * j) & (lane < free + 32 * j + 32)
                fourth = jnp.where(here, moved, fourth)
            field[4 * i + 3, :, start:start + 128] = fourth
        return carry

    lax.fori_loop(0, ROWS // 4, untuck, 0, unroll=True)

    def ends_first(r, carry):
        new = west_end(field, r, 0)
        mid[r, :, WEST:WEST + 128] = new[:, 0:128]
        mid[r, :, 0:128] = new[:, 128:256]
        mid[r, :, WIDTH - 128:WIDTH + 128] = east_end(field, r, 384)
        return carry

    lax.fori_loop(1, ROWS - 1, ends_first, 0, unroll=7)

    for i in (4, 5, 8, 9, 10, 11):
        halos[i].wait_recv()
    has_north, has_south = lat > 0, lat < n_lat - 1
    field[NORTH] = jnp.where(has_north, field[NORTH], 0.0)
    field[SOUTH] = jnp.where(has_south, field[SOUTH], 0.0)
    mid[0] = strip(field, 0, WIDE)
    mid[ROWS - 1] = strip(field, ROWS - 1, WIDE)
    mid[NORTH] = jnp.where(has_north, strip(field, NORTH, WIDE), 0.0)
    mid[SOUTH] = jnp.where(has_south, strip(field, SOUTH, WIDE), 0.0)

    for r in (0, 1, ROWS - 2, ROWS - 1):
        put(r, range(TILES), strip(mid, r, WIDE)[:, 0:WIDTH])

    def ends_second(r, carry):
        put(r, (0,), west_end(mid, r, 128))
        put(r, (TILES - 1,), east_end(mid, r, 256))
        return carry

    lax.fori_loop(2, ROWS - 2, ends_second, 0, unroll=6)

    lane_1 = lax.broadcasted_iota(jnp.int32, (1, 128), 1)

    def look(k, carry):
        row, col, lev = cells[0, k] - lat * ROWS, cells[1, k] - lon * COLS, cells[2, k]
        cell = jnp.clip(row * LEV + lev, 0, LEV * ROWS - 1)
        first_lane = col * M
        tile = jnp.clip(first_lane // 128, 0, TILES - 2)
        lines = []
        for t in range(2):
            place = first_lane - (tile + t) * 128
            inside = (lane_1 >= place) & (lane_1 < place + M)
            lines.append(jnp.where(inside, last[tile + t, pl.ds(cell, 1), :], 0.0))
        turn = lax.rem(tile, 3)
        for t in range(3):
            one = jnp.where(turn == t, lines[0], 0.0)
            seen[t, pl.ds(k, 1), :] = jnp.where(turn == (t + 2) % 3, lines[1], one)
        return carry

    lax.fori_loop(0, OBS, look, 0, unroll=True)
    hx = jnp.concatenate([seen[t] for t in range(3)], axis=1)
    hx = hx + pltpu.roll(hx, GROUP // 2, 1)
    hx = hx + pltpu.roll(hx, GROUP // 4, 1)
    hx = hx + pltpu.roll(hx, GROUP // 8, 1)
    lane_o = lax.broadcasted_iota(jnp.int32, (OBS, 128), 1)
    hbar = jnp.sum(jnp.where(lane_o < M, hx[:, 0:128], 0.0), axis=1, keepdims=True) * (1.0 / M)
    y = hx - hbar
    q = vals[0] / vals[1]
    d = vals[2] - hbar

    y0 = y[:, 0:128]
    y32 = pltpu.roll(y, 32, 1)[:, 0:128]
    w0 = jnp.where(lane_o < 48, y0, jnp.where(lane_o == 96, d, 0.0))
    w1 = jnp.where((lane_o >= 48) & (lane_o < 80), y32, jnp.where(lane_o == 97, d, 0.0))
    w2 = jnp.where((lane_o >= 80) & (lane_o < 96), y0, jnp.where(lane_o == 98, d, 0.0))
    l1 = pltpu.roll(y, GROUP - 16, 1)[:, 0:128]
    l2 = pltpu.roll(y, GROUP - 32, 1)[:, 0:128]
    lhs = jnp.concatenate([q * y0, q * l1, q * l2], axis=0)
    rhs = jnp.concatenate([w0, w1, w2], axis=0)
    packed = lax.dot_general(lhs, rhs, (((0,), (0,)), ((), ())), precision=HP, preferred_element_type=F32)[0:16]
    pack[...] = packed.reshape(2, 8, 128)

    for j in plane_order:
        pltpu.make_async_remote_copy(
            src_ref=pack.at[lax.rem(lat + j // 2, 2)], dst_ref=part1.at[j - 1],
            send_sem=ar_send.at[0], recv_sem=ar_recv.at[0], device_id=plane_peer(j), device_id_type=MESH,
        ).start()

    for t in range(TILES):
        lanes = pl.ds(t % 3 * 128, 128)
        for lev in range(LEV + 1):
            part = last[t, pl.ds(lev, ROWS, stride=LEV), :] if lev < LEV else raw_flux[t]
            hi = part.astype(BF16)
            rows = pl.ds(t // 3 * 144 + lev * ROWS, ROWS)
            high[rows, lanes] = hi
            low[rows, lanes] = (part - hi.astype(F32)).astype(BF16)

    factors = [
        pltpu.make_async_copy(high, high_out, out_sem.at[0]), pltpu.make_async_copy(low, low_out, out_sem.at[1]),
    ]
    for copy in factors:
        copy.start()

    def wait_all(ref, sem):
        pltpu.make_async_copy(ref, ref, sem).wait()

    wait_all(part1, ar_recv.at[0])
    sum1[...] = pack[core] + jnp.sum(part1[...], axis=0)
    pl.semaphore_wait(here_sem.at[1], len(near_line))
    for j in line_order:
        pltpu.make_async_remote_copy(
            src_ref=sum1, dst_ref=part2.at[j - 1],
            send_sem=ar_send.at[1], recv_sem=ar_recv.at[1], device_id=line_peer(j), device_id_type=MESH,
        ).start()
    wait_all(part2, ar_recv.at[1])
    sum2[...] = sum1[...] + jnp.sum(part2[...], axis=0)
    swap = pltpu.make_async_remote_copy(
        src_ref=sum2, dst_ref=part3, send_sem=ar_send.at[2], recv_sem=ar_recv.at[2],
        device_id=partner, device_id_type=MESH,
    )
    swap.start()
    swap.wait_recv()
    mine, other = sum2[...], part3[...]
    total = jnp.concatenate([jnp.where(core == 0, mine, other), jnp.where(core == 0, other, mine)], axis=0)

    lane_p = lax.broadcasted_iota(jnp.int32, (16, 128), 1)
    u0 = jnp.where(lane_p < 48, total, 0.0)
    u1 = jnp.where((lane_p >= 16) & (lane_p < 48), pltpu.roll(total, 128 - 32, 1), 0.0)
    u2 = jnp.where((lane_p >= 32) & (lane_p < 48), pltpu.roll(total, 128 - 48, 1), 0.0)
    upper = jnp.concatenate([u0, u1, u2, jnp.zeros((80, 128), F32)], axis=0)
    flipped = upper.T
    row_s = lax.broadcasted_iota(jnp.int32, (M, M), 0)
    col_s = lax.broadcasted_iota(jnp.int32, (M, M), 1)
    gram = jnp.where(row_s // 16 > col_s // 16, flipped[0:M, 0:M], upper[0:M, 0:M])
    proj = jnp.concatenate([total[:, 96:97], total[:, 97:98], total[:, 98:99]], axis=0)
    eye = jnp.where(row_s == col_s, 1.0, 0.0)

    def dot(a, b):
        return jnp.dot(a, b, precision=HP, preferred_element_type=F32)

    system = (M - 1.0) * eye + gram
    scale = jnp.sqrt(jnp.sum(system * system, keepdims=True))
    root_now = system / scale
    factor = 0.5 * (3.0 * eye - root_now)
    root_now, inverse_now = dot(root_now, factor), factor
    for step in range(1, NS_ITERS):
        factor = 0.5 * (3.0 * eye - dot(inverse_now, root_now))
        if step < NS_ITERS - 1:
            root_now = dot(root_now, factor)
        inverse_now = dot(factor, inverse_now)
    inner = jnp.sum(inverse_now * proj, axis=0, keepdims=True)
    wmean = jnp.sum(inverse_now * inner, axis=1, keepdims=True) / scale
    mixed = wmean + jnp.sqrt((M - 1.0) / scale) * inverse_now
    mixing = mixed - jnp.sum(mixed, axis=0, keepdims=True) * (1.0 / M) + 1.0 / M

    mix[...] = mixing
    result = pltpu.make_async_copy(mix, mix_out, out_sem.at[2])
    result.start()
    for copy in halos:
        copy.wait_send()
    wait_all(part1, ar_send.at[0])
    wait_all(part2, ar_send.at[1])
    swap.wait_send()
    for copy in factors:
        copy.wait()
    result.wait()


def transform(high_in, low_in, mix_in, tracer_out, flux_out, high, low, mix, outs, in_sem, out_sem):
    mix_copy = pltpu.make_async_copy(mix_in, mix, in_sem.at[6])
    mix_copy.start()
    copies = []
    for g in range(3):
        rows = pl.ds(g * 144, 144)
        copies.append(pltpu.make_async_copy(high_in.at[rows], high.at[rows], in_sem.at[2 * g]))
        copies.append(pltpu.make_async_copy(low_in.at[rows], low.at[rows], in_sem.at[2 * g + 1]))
    for copy in copies:
        copy.start()

    rep_row = lax.broadcasted_iota(jnp.int32, (M, GROUP), 0)
    rep_lane = lax.broadcasted_iota(jnp.int32, (M, GROUP), 1)
    rep = jnp.where(lax.rem(rep_lane, M) == rep_row, 1.0, 0.0).astype(BF16)
    mix_copy.wait()
    mixing = mix[...]
    g_high = mixing.astype(BF16)
    g_low = (mixing - g_high.astype(F32)).astype(BF16)
    g_high = jnp.dot(g_high, rep, preferred_element_type=F32)
    g_low = jnp.dot(g_low, rep, preferred_element_type=F32)

    def diagonal(g):
        return jnp.concatenate(
            [jnp.where((rep_lane >= b * M) & (rep_lane < b * M + M), g, 0.0).astype(BF16) for b in range(8)], axis=0
        )

    d_high, d_low = diagonal(g_high), diagonal(g_low)
    done = []
    for g in range(3):
        for copy in copies[2 * g:2 * g + 2]:
            copy.wait()
        hi, lo = high[pl.ds(g * 144, 144), :], low[pl.ds(g * 144, 144), :]
        outs[g] = (
            jnp.dot(hi, d_high, preferred_element_type=F32)
            + jnp.dot(lo, d_high, preferred_element_type=F32)
            + jnp.dot(hi, d_low, preferred_element_type=F32)
        )
        lanes = pl.ds(g * GROUP, GROUP)
        done.append(pltpu.make_async_copy(outs.at[g, pl.ds(0, LEV * ROWS)], tracer_out.at[:, lanes], out_sem.at[g]))
        done.append(pltpu.make_async_copy(outs.at[g, pl.ds(LEV * ROWS, ROWS)], flux_out.at[:, lanes], out_sem.at[3 + g]))
        for copy in done[-2:]:
            copy.start()
    for copy in done:
        copy.wait()


def on_device(n_lat, n_lon, tracer, flux, winds, obs_cells, obs_count, obs_value, obs_var):
    hbm = pl.BlockSpec(memory_space=pltpu.HBM)
    n_plane, n_line = 2 * n_lat, n_lon // 2
    vmem = pltpu.VMEM
    high, low, mixing = pl.pallas_call(
        functools.partial(kernel, n_lat, n_lon),
        out_shape=(
            jax.ShapeDtypeStruct((432, GROUP), BF16),
            jax.ShapeDtypeStruct((432, GROUP), BF16),
            jax.ShapeDtypeStruct((M, M), F32),
        ),
        in_specs=[hbm] * 7,
        out_specs=(hbm, hbm, hbm),
        scratch_shapes=[
            vmem((TILES, LEV * ROWS, 128), F32),
            vmem((TILES, ROWS, 128), F32),
            vmem((3 * LEV * ROWS, COLS), F32),
            vmem((3 * LEV * ROWS, 128), F32),
            vmem((ROWS_X, LEV, WIDE), F32),
            vmem((ROWS_X, LEV, WIDE), F32),
            vmem((TILES, LEV * ROWS, 128), F32),
            vmem((3, ROWS, LEV, 128), F32),
            vmem((3, ROWS_X, LEV, WIDE), F32),
            vmem((2, LEV, 128), F32),
            vmem((2, LEV, 128), F32),
            vmem((2, LEV, 128), F32),
            vmem((2, LEV, 128), F32),
            vmem((2, 12, LEV, 128), F32),
            vmem((2, 12, LEV, 128), F32),
            vmem((3, OBS, 128), F32),
            vmem((3, OBS, 128), F32),
            vmem((2, 8, 128), F32),
            vmem((n_plane - 1, 8, 128), F32),
            vmem((n_line - 1, 8, 128), F32),
            vmem((8, 128), F32),
            vmem((8, 128), F32),
            vmem((8, 128), F32),
            vmem((432, GROUP), BF16),
            vmem((432, GROUP), BF16),
            vmem((M, M), F32),
            pltpu.SMEM((3, OBS), jnp.int32),
            pltpu.SMEM((1,), jnp.int32),
            pltpu.SMEM((OBS,), F32),
            pltpu.SMEM((OBS,), F32),
            pltpu.SemaphoreType.DMA((5 + 2 * TILES,)),
            pltpu.SemaphoreType.DMA((3,)),
            pltpu.SemaphoreType.DMA((12,)),
            pltpu.SemaphoreType.DMA((12,)),
            pltpu.SemaphoreType.DMA((3,)),
            pltpu.SemaphoreType.DMA((3,)),
            pltpu.SemaphoreType.REGULAR((2,)),
        ],
        compiler_params=pltpu.CompilerParams(
            collective_id=0, has_side_effects=True, vmem_limit_bytes=62 * 1024 * 1024
        ),
        name="analysis",
    )(
        tracer.reshape(LEV * ROWS, WIDTH), flux, winds.reshape(3 * LEV * ROWS, COLS),
        obs_cells.T, obs_count, obs_value, obs_var,
    )
    tracer_out, flux_out = pl.pallas_call(
        transform,
        out_shape=(
            jax.ShapeDtypeStruct((LEV * ROWS, WIDTH), F32),
            jax.ShapeDtypeStruct((ROWS, WIDTH), F32),
        ),
        in_specs=[hbm] * 3,
        out_specs=(hbm, hbm),
        scratch_shapes=[
            vmem((432, GROUP), BF16),
            vmem((432, GROUP), BF16),
            vmem((M, M), F32),
            vmem((3, 144, GROUP), F32),
            pltpu.SemaphoreType.DMA((7,)),
            pltpu.SemaphoreType.DMA((6,)),
        ],
        compiler_params=pltpu.CompilerParams(vmem_limit_bytes=62 * 1024 * 1024),
        name="transform",
    )(high, low, mixing)
    return tracer_out.reshape(LEV, ROWS, WIDTH), flux_out


def solution(mesh):
    return jax.shard_map(
        functools.partial(on_device, mesh.shape["lat"], mesh.shape["lon"]),
        mesh=mesh,
        in_specs=(
            P(None, "lat", "lon"),
            P("lat", "lon"),
            P(None, None, "lat", "lon"),
            P(("lat", "lon"), None),
            P(("lat", "lon")),
            P(("lat", "lon")),
            P(("lat", "lon")),
        ),
        out_specs=(P(None, "lat", "lon"), P("lat", "lon")),
        check_vma=False,
    )
```

```python
import functools

import jax
import jax.numpy as jnp
from jax import lax
from jax.experimental import pallas as pl
from jax.experimental.pallas import tpu as pltpu
from jax.sharding import PartitionSpec as P

M = 48
NS_ITERS = 5
KH = 0.15
MESH = pl.DeviceIdType.MESH
HP = lax.Precision.HIGHEST
F32 = jnp.float32
BF16 = jnp.bfloat16

LEV, ROWS, COLS, OBS = 8, 16, 24, 16
TILES = 9
WIDTH = COLS * M
WIDE = WIDTH + 256
EAST, WEST = WIDTH, WIDTH + 128
ROWS_X = ROWS + 4
SOUTH, NORTH = ROWS, ROWS + 3
GROUP = 8 * M


def kernel(
    n_lat, n_lon,
    tracer, flux, winds, cells_in, count_in, value_in, var_in,
    high_out, low_out, mix_out,
    raw, raw_flux, raw_winds, wide_winds, field, mid, last, wc, wx, wcol_out, wcol_in,
    wrow_out, wrow_in, lon_out, lon_in, seen, vals, pack, part1, part2, part3, sum1, sum2, high, low, mix,
    cells, count, value, var, in_sem, out_sem, halo_send, halo_recv, ar_send, ar_recv, here_sem,
):
    lat, lon = lax.axis_index("lat"), lax.axis_index("lon")

    def at(dlat, dlon):
        return (lax.rem(lat + (dlat + n_lat), n_lat), lax.rem(lon + (dlon + n_lon), n_lon))

    sides = [(1, 0), (-1, 0), (0, 1), (0, -1), (1, 1), (1, -1), (-1, 1), (-1, -1)]
    pair = lax.rem(lon, 2)
    base = lon - pair

    def plane_peer(j):
        return (lax.rem(lat + j // 2, n_lat), base + lax.rem(pair + j, 2))

    def line_peer(j):
        return (lat, lax.rem(lon + 2 * j, n_lon))

    core = lax.rem(lat, 2)
    partner = (lat + 1 - 2 * core, lon)
    n_plane, n_line = 2 * n_lat, n_lon // 2

    n_x = n_lat // 4
    x, y = lat // 4, lax.rem(lat // 2, 2) * 2 + pair

    def plane_near(dx, dy, dc):
        to_x, to_y = lax.rem(x + (dx + n_x), n_x), lax.rem(y + (dy + 4), 4)
        return (to_x * 4 + to_y // 2 * 2 + lax.rem(core + dc, 2), base + lax.rem(to_y, 2))

    near_plane = [
        plane_near(dx, dy, dc) for dx in (-1, 1, 0) for dy in (-1, 1, 0) for dc in (1, 0) if (dx, dy, dc) != (0, 0, 0)
    ]
    near_line = [line_peer(k % n_line) for k in (3, -3, 2, -2)]
    near_halo = [at(dlat, dlon) for dlat, dlon in sides]
    plane_order = sorted(range(1, n_plane), key=lambda j: -min(j // 2, n_lat - j // 2))
    line_order = sorted(range(1, n_line), key=lambda j: -min(j, n_line - j))
    barrier = pltpu.get_barrier_semaphore()
    for peer in near_halo + near_line + near_plane:
        pl.semaphore_signal(barrier, inc=1, device_id=peer, device_id_type=MESH)

    copies = [
        pltpu.make_async_copy(winds, raw_winds, in_sem.at[0]),
    ]
    for t in range(TILES):
        lanes = pl.ds(t * 128, 128)
        copies.append(pltpu.make_async_copy(tracer.at[:, lanes], raw.at[t], in_sem.at[1 + t]))
        copies.append(pltpu.make_async_copy(flux.at[:, lanes], raw_flux.at[t], in_sem.at[1 + TILES + t]))
    obs_copies = [
        pltpu.make_async_copy(src, dst, in_sem.at[1 + 2 * TILES + i])
        for i, (src, dst) in enumerate(((cells_in, cells), (count_in, count), (value_in, value), (var_in, var)))
    ]
    for copy in copies + obs_copies:
        copy.start()

    for copy in copies:
        copy.wait()
    level = lax.broadcasted_iota(jnp.int32, (LEV, 1), 0)
    wide_winds[:, 0:COLS] = 0.5 * raw_winds[...]

    def enter(r, carry):
        for t in range(TILES):
            own = raw[t, pl.ds(r, LEV, stride=ROWS), :]
            surface = raw_flux[t, pl.ds(r, 1), :]
            field[r, :, t * 128:t * 128 + 128] = own + jnp.where(level == 0, surface, 0.0)
        for v in range(3):
            wc[v, r] = wide_winds[pl.ds(v * LEV * ROWS + r, LEV, stride=ROWS), :]
        return carry

    lax.fori_loop(0, ROWS, enter, 0, unroll=8)

    lane = lax.broadcasted_iota(jnp.int32, (LEV, 128), 1)

    def edge(r, carry):
        first, final = carry
        for v in range(3):
            w = wc[v, r]
            here = lane == v * ROWS + r
            first = jnp.where(here, w[:, 0:1], first)
            final = jnp.where(here, w[:, COLS - 1:COLS], final)
        return first, final

    zero_tile = jnp.zeros((LEV, 128), F32)
    first, final = lax.fori_loop(0, ROWS, edge, (zero_tile, zero_tile), unroll=True)
    wcol_out[0] = first
    wcol_out[1] = final
    for side, r in ((0, 0), (1, ROWS - 1)):
        packed_row = jnp.where(lane < COLS, wc[0, r], 0.0)
        for v in (1, 2):
            here = (lane >= v * COLS) & (lane < v * COLS + COLS)
            packed_row = jnp.where(here, pltpu.roll(wc[v, r], v * COLS, 1), packed_row)
        wrow_out[side] = packed_row

    def tuck(i, carry):
        for side, start, free, gap in ((0, 0, 0, 2 * M), (1, WIDTH - 128, 32, 0)):
            fourth = field[4 * i + 3, :, start:start + 128]
            for j in range(3):
                shift = (gap - free - 32 * j) % 128
                moved = pltpu.roll(fourth, shift, 1) if shift else fourth
                here = (lane >= gap) & (lane < gap + 32)
                lon_out[side, 3 * i + j] = jnp.where(here, moved, field[4 * i + j, :, start:start + 128])
        return carry

    lax.fori_loop(0, ROWS // 4, tuck, 0, unroll=True)

    pl.semaphore_wait(barrier, len(near_halo + near_line + near_plane))

    def send(i, src, dst, to):
        return pltpu.make_async_remote_copy(
            src_ref=src, dst_ref=dst, send_sem=halo_send.at[i], recv_sem=halo_recv.at[i],
            device_id=to, device_id_type=MESH,
        )

    own_lanes = pl.ds(0, WIDTH)
    left_tile, right_tile = pl.ds(0, 128), pl.ds(WIDTH - 128, 128)
    east_tile, west_tile = pl.ds(EAST, 128), pl.ds(WEST, 128)
    top, bottom = 0, ROWS - 1
    halos = [
        send(0, wcol_out.at[0], wcol_in.at[0], at(0, -1)),
        send(1, wcol_out.at[1], wcol_in.at[1], at(0, 1)),
        send(2, wrow_out.at[0], wrow_in.at[0], at(-1, 0)),
        send(3, wrow_out.at[1], wrow_in.at[1], at(1, 0)),
        send(4, field.at[pl.ds(top, 2), :, own_lanes], field.at[pl.ds(SOUTH, 2), :, own_lanes], at(-1, 0)),
        send(5, field.at[pl.ds(bottom - 1, 2), :, own_lanes], field.at[pl.ds(NORTH - 1, 2), :, own_lanes], at(1, 0)),
        send(6, lon_out.at[0], lon_in.at[0], at(0, -1)),
        send(7, lon_out.at[1], lon_in.at[1], at(0, 1)),
        send(8, field.at[top, :, left_tile], field.at[SOUTH, :, east_tile], at(-1, -1)),
        send(9, field.at[top, :, right_tile], field.at[SOUTH, :, west_tile], at(-1, 1)),
        send(10, field.at[bottom, :, left_tile], field.at[NORTH, :, east_tile], at(1, -1)),
        send(11, field.at[bottom, :, right_tile], field.at[NORTH, :, west_tile], at(1, 1)),
    ]
    for copy in halos:
        copy.start()
    for peer in near_line + near_plane:
        pl.semaphore_signal(here_sem.at[0], inc=1, device_id=peer, device_id_type=MESH)

    spread_col = lax.broadcasted_iota(jnp.int32, (COLS, WIDTH), 0)
    spread_lane = lax.broadcasted_iota(jnp.int32, (COLS, WIDTH), 1)
    spread = jnp.where((spread_lane >= spread_col * M) & (spread_lane < spread_col * M + M), 1.0, 0.0).astype(BF16)

    def spread_rows(w, v, start, rows):
        a = w.astype(BF16)
        rest = w - a.astype(F32)
        b = rest.astype(BF16)
        c = (rest - b.astype(F32)).astype(BF16)
        wide = (
            jnp.dot(a, spread, preferred_element_type=F32)
            + jnp.dot(b, spread, preferred_element_type=F32)
            + jnp.dot(c, spread, preferred_element_type=F32)
        )
        wx[v, pl.ds(start, rows), :, 0:WIDTH] = wide.reshape(rows, LEV, WIDTH)

    for v in range(3):
        spread_rows(wc[v, :, :, 0:COLS].reshape(ROWS * LEV, COLS), v, 0, ROWS)

    def stencil(c, n, s, u, v, w, first, final):
        width = c.shape[1]
        keep = slice(first, final)
        east, west = pltpu.roll(c, width - M, 1)[:, keep], pltpu.roll(c, M, 1)[:, keep]
        c = c[:, keep]
        above = jnp.where(level == LEV - 1, 0.0, pltpu.roll(c, LEV - 1, 0))
        below = jnp.where(level == 0, 0.0, pltpu.roll(c, 1, 0))
        spread_out = (east + west) + (s + n) + (above + below)
        carried = u * (east - west) + v * (s - n) + w * (above - below)
        return (1.0 - 6.0 * KH) * c + KH * spread_out - carried

    def strip(src, r, width):
        n, s = lax.rem(r + ROWS_X - 1, ROWS_X), lax.rem(r + 1, ROWS_X)
        return stencil(
            src[r, :, 0:width], src[n, :, 0:width], src[s, :, 0:width],
            wx[0, r, :, 0:width], wx[1, r, :, 0:width], wx[2, r, :, 0:width], 0, width,
        )

    def west_end(src, r, first):
        def of(ref, i):
            return jnp.concatenate([ref[i, :, WEST:WEST + 128], ref[i, :, 0:128]], axis=1)[:, first:]

        c = jnp.concatenate([src[r, :, WEST:WEST + 128], src[r, :, 0:256]], axis=1)
        return stencil(
            c, of(src, r - 1), of(src, r + 1), of(wx.at[0], r), of(wx.at[1], r), of(wx.at[2], r), first, 256
        )

    def east_end(src, r, final):
        lanes = slice(WIDTH - 128, WIDTH - 256 + final)
        return stencil(
            src[r, :, WIDTH - 256:WIDTH + 128], src[r - 1, :, lanes], src[r + 1, :, lanes],
            wx[0, r, :, lanes], wx[1, r, :, lanes], wx[2, r, :, lanes], 128, final,
        )

    def put(r, tiles, value):
        for i, t in enumerate(tiles):
            last[t, pl.ds(pl.multiple_of(r * LEV, LEV), LEV), :] = value[:, i * 128:i * 128 + 128]

    def inner_first(r, carry):
        mid[r, :, 0:WIDTH] = strip(field, r, WIDTH)
        return carry

    lax.fori_loop(1, ROWS - 1, inner_first, 0, unroll=2)

    def inner_second(r, carry):
        put(r, range(1, TILES - 1), strip(mid, r, WIDTH)[:, 128:WIDTH - 128])
        return carry

    lax.fori_loop(2, ROWS - 2, inner_second, 0, unroll=2)

    for copy in obs_copies:
        copy.wait()

    def note(k, carry):
        live = jnp.where(k < count[0], 1.0, 0.0)
        vals[0, pl.ds(k, 1), :] = jnp.full((1, 128), live, F32)
        vals[1, pl.ds(k, 1), :] = jnp.full((1, 128), var[k], F32)
        vals[2, pl.ds(k, 1), :] = jnp.full((1, 128), value[k], F32)
        return carry

    lax.fori_loop(0, OBS, note, 0)
    spots = []
    for k in range(OBS):
        row, first_lane, lev = cells[0, k] - lat * ROWS, (cells[1, k] - lon * COLS) * M, cells[2, k]
        tile = jnp.clip(first_lane // 128, 0, TILES - 2)
        spots.append((jnp.clip(row * LEV + lev, 0, LEV * ROWS - 1), tile, first_lane - tile * 128, lax.rem(tile, 3)))

    pl.semaphore_wait(here_sem.at[0], len(near_line + near_plane))
    for peer in near_line:
        pl.semaphore_signal(here_sem.at[1], inc=1, device_id=peer, device_id_type=MESH)

    for i in range(4):
        halos[i].wait_recv()
    for v in range(3):
        for side, start in ((0, SOUTH), (1, NORTH)):
            spread_rows(wrow_in[side][:, v * COLS:v * COLS + COLS], v, start, 1)
        for side, start in ((0, EAST), (1, WEST)):
            got = wcol_in[side]
            for r in range(ROWS):
                wx[v, r, :, start:start + 128] = jnp.broadcast_to(got[:, v * ROWS + r:v * ROWS + r + 1], (LEV, 128))

    for i in (6, 7):
        halos[i].wait_recv()

    def untuck(i, carry):
        for side, start, free, gap in ((0, EAST, 0, 2 * M), (1, WEST, 32, 0)):
            fourth = zero_tile
            for j in range(3):
                tile = lon_in[side, 3 * i + j]
                field[4 * i + j, :, start:start + 128] = tile
                shift = (free + 32 * j - gap) % 128
                moved = pltpu.roll(tile, shift, 1) if shift else tile
                here = (lane >= free + 32 * j) & (lane < free + 32 * j + 32)
                fourth = jnp.where(here, moved, fourth)
            field[4 * i + 3, :, start:start + 128] = fourth
        return carry

    lax.fori_loop(0, ROWS // 4, untuck, 0, unroll=True)

    def ends_first(r, carry):
        new = west_end(field, r, 0)
        mid[r, :, WEST:WEST + 128] = new[:, 0:128]
        mid[r, :, 0:128] = new[:, 128:256]
        mid[r, :, WIDTH - 128:WIDTH + 128] = east_end(field, r, 384)
        return carry

    lax.fori_loop(1, ROWS - 1, ends_first, 0, unroll=7)

    for i in (4, 5, 8, 9, 10, 11):
        halos[i].wait_recv()
    has_north, has_south = lat > 0, lat < n_lat - 1
    field[NORTH] = jnp.where(has_north, field[NORTH], 0.0)
    field[SOUTH] = jnp.where(has_south, field[SOUTH], 0.0)
    mid[0] = strip(field, 0, WIDE)
    mid[ROWS - 1] = strip(field, ROWS - 1, WIDE)
    mid[NORTH] = jnp.where(has_north, strip(field, NORTH, WIDE), 0.0)
    mid[SOUTH] = jnp.where(has_south, strip(field, SOUTH, WIDE), 0.0)

    for r in (0, 1, ROWS - 2, ROWS - 1):
        put(r, range(TILES), strip(mid, r, WIDE)[:, 0:WIDTH])

    def ends_second(r, carry):
        put(r, (0,), west_end(mid, r, 128))
        put(r, (TILES - 1,), east_end(mid, r, 256))
        return carry

    lax.fori_loop(2, ROWS - 2, ends_second, 0, unroll=6)

    lane_1 = lax.broadcasted_iota(jnp.int32, (1, 128), 1)

    for k, (cell, tile, start, turn) in enumerate(spots):
        lines = []
        for t in range(2):
            inside = (lane_1 >= start - t * 128) & (lane_1 < start - t * 128 + M)
            lines.append(jnp.where(inside, last[tile + t, pl.ds(cell, 1), :], 0.0))
        for t in range(3):
            one = jnp.where(turn == t, lines[0], 0.0)
            seen[t, k:k + 1, :] = jnp.where(turn == (t + 2) % 3, lines[1], one)
    hx = jnp.concatenate([seen[t] for t in range(3)], axis=1)
    hx = hx + pltpu.roll(hx, GROUP // 2, 1)
    hx = hx + pltpu.roll(hx, GROUP // 4, 1)
    hx = hx + pltpu.roll(hx, GROUP // 8, 1)
    lane_o = lax.broadcasted_iota(jnp.int32, (OBS, 128), 1)
    hbar = jnp.sum(jnp.where(lane_o < M, hx[:, 0:128], 0.0), axis=1, keepdims=True) * (1.0 / M)
    y = hx - hbar
    q = vals[0] / vals[1]
    d = vals[2] - hbar

    y0 = y[:, 0:128]
    y32 = pltpu.roll(y, 32, 1)[:, 0:128]
    w0 = jnp.where(lane_o < 48, y0, jnp.where(lane_o == 96, d, 0.0))
    w1 = jnp.where((lane_o >= 48) & (lane_o < 80), y32, jnp.where(lane_o == 97, d, 0.0))
    w2 = jnp.where((lane_o >= 80) & (lane_o < 96), y0, jnp.where(lane_o == 98, d, 0.0))
    l1 = pltpu.roll(y, GROUP - 16, 1)[:, 0:128]
    l2 = pltpu.roll(y, GROUP - 32, 1)[:, 0:128]
    lhs = jnp.concatenate([q * y0, q * l1, q * l2], axis=0)
    rhs = jnp.concatenate([w0, w1, w2], axis=0)
    packed = lax.dot_general(lhs, rhs, (((0,), (0,)), ((), ())), precision=HP, preferred_element_type=F32)[0:16]
    pack[...] = packed.reshape(2, 8, 128)

    for j in plane_order:
        pltpu.make_async_remote_copy(
            src_ref=pack.at[lax.rem(lat + j // 2, 2)], dst_ref=part1.at[j - 1],
            send_sem=ar_send.at[0], recv_sem=ar_recv.at[0], device_id=plane_peer(j), device_id_type=MESH,
        ).start()

    for t in range(TILES):
        lanes = pl.ds(t % 3 * 128, 128)
        for lev in range(LEV + 1):
            part = last[t, pl.ds(lev, ROWS, stride=LEV), :] if lev < LEV else raw_flux[t]
            hi = part.astype(BF16)
            rows = pl.ds(t // 3 * 144 + lev * ROWS, ROWS)
            high[rows, lanes] = hi
            low[rows, lanes] = (part - hi.astype(F32)).astype(BF16)

    factors = [
        pltpu.make_async_copy(high, high_out, out_sem.at[0]), pltpu.make_async_copy(low, low_out, out_sem.at[1]),
    ]
    for copy in factors:
        copy.start()

    def wait_all(ref, sem):
        pltpu.make_async_copy(ref, ref, sem).wait()

    wait_all(part1, ar_recv.at[0])
    sum1[...] = pack[core] + jnp.sum(part1[...], axis=0)
    pl.semaphore_wait(here_sem.at[1], len(near_line))
    for j in line_order:
        pltpu.make_async_remote_copy(
            src_ref=sum1, dst_ref=part2.at[j - 1],
            send_sem=ar_send.at[1], recv_sem=ar_recv.at[1], device_id=line_peer(j), device_id_type=MESH,
        ).start()
    wait_all(part2, ar_recv.at[1])
    sum2[...] = sum1[...] + jnp.sum(part2[...], axis=0)
    swap = pltpu.make_async_remote_copy(
        src_ref=sum2, dst_ref=part3, send_sem=ar_send.at[2], recv_sem=ar_recv.at[2],
        device_id=partner, device_id_type=MESH,
    )
    swap.start()
    swap.wait_recv()
    mine, other = sum2[...], part3[...]
    total = jnp.concatenate([jnp.where(core == 0, mine, other), jnp.where(core == 0, other, mine)], axis=0)

    lane_p = lax.broadcasted_iota(jnp.int32, (16, 128), 1)
    u0 = jnp.where(lane_p < 48, total, 0.0)
    u1 = jnp.where((lane_p >= 16) & (lane_p < 48), pltpu.roll(total, 128 - 32, 1), 0.0)
    u2 = jnp.where((lane_p >= 32) & (lane_p < 48), pltpu.roll(total, 128 - 48, 1), 0.0)
    upper = jnp.concatenate([u0, u1, u2, jnp.zeros((80, 128), F32)], axis=0)
    flipped = upper.T
    row_s = lax.broadcasted_iota(jnp.int32, (M, M), 0)
    col_s = lax.broadcasted_iota(jnp.int32, (M, M), 1)
    gram = jnp.where(row_s // 16 > col_s // 16, flipped[0:M, 0:M], upper[0:M, 0:M])
    proj = jnp.concatenate([total[:, 96:97], total[:, 97:98], total[:, 98:99]], axis=0)
    eye = jnp.where(row_s == col_s, 1.0, 0.0)

    def dot(a, b):
        return jnp.dot(a, b, precision=HP, preferred_element_type=F32)

    system = (M - 1.0) * eye + gram
    scale = jnp.sqrt(jnp.sum(system * system, keepdims=True))
    root_now = system / scale
    factor = 0.5 * (3.0 * eye - root_now)
    root_now, inverse_now = dot(root_now, factor), factor
    for step in range(1, NS_ITERS):
        factor = 0.5 * (3.0 * eye - dot(inverse_now, root_now))
        if step < NS_ITERS - 1:
            root_now = dot(root_now, factor)
        inverse_now = dot(factor, inverse_now)
    inner = jnp.sum(inverse_now * proj, axis=0, keepdims=True)
    wmean = jnp.sum(inverse_now * inner, axis=1, keepdims=True) / scale
    mixed = wmean + jnp.sqrt((M - 1.0) / scale) * inverse_now
    mixing = mixed - jnp.sum(mixed, axis=0, keepdims=True) * (1.0 / M) + 1.0 / M

    mix[...] = mixing
    result = pltpu.make_async_copy(mix, mix_out, out_sem.at[2])
    result.start()
    for copy in halos:
        copy.wait_send()
    wait_all(part1, ar_send.at[0])
    wait_all(part2, ar_send.at[1])
    swap.wait_send()
    for copy in factors:
        copy.wait()
    result.wait()


def transform(high_in, low_in, mix_in, tracer_out, flux_out, high, low, mix, outs, in_sem, out_sem):
    mix_copy = pltpu.make_async_copy(mix_in, mix, in_sem.at[6])
    mix_copy.start()
    copies = []
    for g in range(3):
        rows = pl.ds(g * 144, 144)
        copies.append(pltpu.make_async_copy(high_in.at[rows], high.at[rows], in_sem.at[2 * g]))
        copies.append(pltpu.make_async_copy(low_in.at[rows], low.at[rows], in_sem.at[2 * g + 1]))
    for copy in copies:
        copy.start()

    rep_row = lax.broadcasted_iota(jnp.int32, (M, GROUP), 0)
    rep_lane = lax.broadcasted_iota(jnp.int32, (M, GROUP), 1)
    rep = jnp.where(lax.rem(rep_lane, M) == rep_row, 1.0, 0.0).astype(BF16)
    mix_copy.wait()
    mixing = mix[...]
    g_high = mixing.astype(BF16)
    g_low = (mixing - g_high.astype(F32)).astype(BF16)
    g_high = jnp.dot(g_high, rep, preferred_element_type=F32)
    g_low = jnp.dot(g_low, rep, preferred_element_type=F32)

    def diagonal(g):
        return jnp.concatenate(
            [jnp.where((rep_lane >= b * M) & (rep_lane < b * M + M), g, 0.0).astype(BF16) for b in range(8)], axis=0
        )

    d_high, d_low = diagonal(g_high), diagonal(g_low)
    done = []
    for copy in copies:
        copy.wait()
    for n, (k0, k1) in enumerate(((0, 256), (0, 384), (128, 384))):
        cols = slice(n * 128, n * 128 + 128)
        w_h, w_l = d_high[k0:k1, cols], d_low[k0:k1, cols]
        w = jnp.concatenate([w_h, w_l], axis=1)
        both = jnp.dot(high[:, k0:k1], w, preferred_element_type=F32)
        res = both[:, 0:128] + both[:, 128:256] + jnp.dot(low[:, k0:k1], w_h, preferred_element_type=F32)
        for g in range(3):
            outs[g, :, cols] = res[g * 144:(g + 1) * 144]
    for g in range(3):
        lanes = pl.ds(g * GROUP, GROUP)
        done.append(pltpu.make_async_copy(outs.at[g, pl.ds(0, LEV * ROWS)], tracer_out.at[:, lanes], out_sem.at[g]))
        done.append(pltpu.make_async_copy(outs.at[g, pl.ds(LEV * ROWS, ROWS)], flux_out.at[:, lanes], out_sem.at[3 + g]))
        for copy in done[-2:]:
            copy.start()
    for copy in done:
        copy.wait()


def on_device(n_lat, n_lon, tracer, flux, winds, obs_cells, obs_count, obs_value, obs_var):
    hbm = pl.BlockSpec(memory_space=pltpu.HBM)
    n_plane, n_line = 2 * n_lat, n_lon // 2
    vmem = pltpu.VMEM
    high, low, mixing = pl.pallas_call(
        functools.partial(kernel, n_lat, n_lon),
        out_shape=(
            jax.ShapeDtypeStruct((432, GROUP), BF16),
            jax.ShapeDtypeStruct((432, GROUP), BF16),
            jax.ShapeDtypeStruct((M, M), F32),
        ),
        in_specs=[hbm] * 7,
        out_specs=(hbm, hbm, hbm),
        scratch_shapes=[
            vmem((TILES, LEV * ROWS, 128), F32),
            vmem((TILES, ROWS, 128), F32),
            vmem((3 * LEV * ROWS, COLS), F32),
            vmem((3 * LEV * ROWS, 128), F32),
            vmem((ROWS_X, LEV, WIDE), F32),
            vmem((ROWS_X, LEV, WIDE), F32),
            vmem((TILES, LEV * ROWS, 128), F32),
            vmem((3, ROWS, LEV, 128), F32),
            vmem((3, ROWS_X, LEV, WIDE), F32),
            vmem((2, LEV, 128), F32),
            vmem((2, LEV, 128), F32),
            vmem((2, LEV, 128), F32),
            vmem((2, LEV, 128), F32),
            vmem((2, 12, LEV, 128), F32),
            vmem((2, 12, LEV, 128), F32),
            vmem((3, OBS, 128), F32),
            vmem((3, OBS, 128), F32),
            vmem((2, 8, 128), F32),
            vmem((n_plane - 1, 8, 128), F32),
            vmem((n_line - 1, 8, 128), F32),
            vmem((8, 128), F32),
            vmem((8, 128), F32),
            vmem((8, 128), F32),
            vmem((432, GROUP), BF16),
            vmem((432, GROUP), BF16),
            vmem((M, M), F32),
            pltpu.SMEM((3, OBS), jnp.int32),
            pltpu.SMEM((1,), jnp.int32),
            pltpu.SMEM((OBS,), F32),
            pltpu.SMEM((OBS,), F32),
            pltpu.SemaphoreType.DMA((5 + 2 * TILES,)),
            pltpu.SemaphoreType.DMA((3,)),
            pltpu.SemaphoreType.DMA((12,)),
            pltpu.SemaphoreType.DMA((12,)),
            pltpu.SemaphoreType.DMA((3,)),
            pltpu.SemaphoreType.DMA((3,)),
            pltpu.SemaphoreType.REGULAR((2,)),
        ],
        compiler_params=pltpu.CompilerParams(
            collective_id=0, has_side_effects=True, vmem_limit_bytes=62 * 1024 * 1024
        ),
        name="analysis",
    )(
        tracer.reshape(LEV * ROWS, WIDTH), flux, winds.reshape(3 * LEV * ROWS, COLS),
        obs_cells.T, obs_count, obs_value, obs_var,
    )
    tracer_out, flux_out = pl.pallas_call(
        transform,
        out_shape=(
            jax.ShapeDtypeStruct((LEV * ROWS, WIDTH), F32),
            jax.ShapeDtypeStruct((ROWS, WIDTH), F32),
        ),
        in_specs=[hbm] * 3,
        out_specs=(hbm, hbm),
        scratch_shapes=[
            vmem((432, GROUP), BF16),
            vmem((432, GROUP), BF16),
            vmem((M, M), F32),
            vmem((3, 144, GROUP), F32),
            pltpu.SemaphoreType.DMA((7,)),
            pltpu.SemaphoreType.DMA((6,)),
        ],
        compiler_params=pltpu.CompilerParams(vmem_limit_bytes=62 * 1024 * 1024),
        name="transform",
    )(high, low, mixing)
    return tracer_out.reshape(LEV, ROWS, WIDTH), flux_out


def solution(mesh):
    return jax.shard_map(
        functools.partial(on_device, mesh.shape["lat"], mesh.shape["lon"]),
        mesh=mesh,
        in_specs=(
            P(None, "lat", "lon"),
            P("lat", "lon"),
            P(None, None, "lat", "lon"),
            P(("lat", "lon"), None),
            P(("lat", "lon")),
            P(("lat", "lon")),
            P(("lat", "lon")),
        ),
        out_specs=(P(None, "lat", "lon"), P("lat", "lon")),
        check_vma=False,
    )
```

```python
import functools

import jax
import jax.numpy as jnp
from jax import lax
from jax.experimental import pallas as pl
from jax.experimental.pallas import tpu as pltpu
from jax.sharding import PartitionSpec as P

M = 48
NS_ITERS = 5
KH = 0.15
MESH = pl.DeviceIdType.MESH
HP = lax.Precision.HIGHEST
F32 = jnp.float32
BF16 = jnp.bfloat16

LEV, ROWS, COLS, OBS = 8, 16, 24, 16
TILES = 9
WIDTH = COLS * M
WIDE = WIDTH + 256
EAST, WEST = WIDTH, WIDTH + 128
ROWS_X = ROWS + 4
SOUTH, NORTH = ROWS, ROWS + 3
GROUP = 8 * M


def kernel(
    n_lat, n_lon,
    tracer, flux, winds, cells_in, count_in, value_in, var_in,
    high_out, low_out, mix_out,
    raw, raw_flux, raw_winds, wide_winds, field, mid, last, wc, wx, wcol_out, wcol_in,
    wrow_out, wrow_in, lon_out, lon_in, seen, vals, pack, part1, part2, part3, sum1, sum2, high, low, mix,
    cells, count, value, var, in_sem, out_sem, halo_send, halo_recv, ar_send, ar_recv, here_sem,
):
    lat, lon = lax.axis_index("lat"), lax.axis_index("lon")

    def at(dlat, dlon):
        return (lax.rem(lat + (dlat + n_lat), n_lat), lax.rem(lon + (dlon + n_lon), n_lon))

    sides = [(1, 0), (-1, 0), (0, 1), (0, -1), (1, 1), (1, -1), (-1, 1), (-1, -1)]
    pair = lax.rem(lon, 2)
    base = lon - pair

    def plane_peer(j):
        return (lax.rem(lat + j // 2, n_lat), base + lax.rem(pair + j, 2))

    def line_peer(j):
        return (lat, lax.rem(lon + 2 * j, n_lon))

    core = lax.rem(lat, 2)
    partner = (lat + 1 - 2 * core, lon)
    n_plane, n_line = 2 * n_lat, n_lon // 2

    n_x = n_lat // 4
    x, y = lat // 4, lax.rem(lat // 2, 2) * 2 + pair

    def plane_near(dx, dy, dc):
        to_x, to_y = lax.rem(x + (dx + n_x), n_x), lax.rem(y + (dy + 4), 4)
        return (to_x * 4 + to_y // 2 * 2 + lax.rem(core + dc, 2), base + lax.rem(to_y, 2))

    near_plane = [
        plane_near(dx, dy, dc) for dx in (-1, 1, 0) for dy in (-1, 1, 0) for dc in (1, 0) if (dx, dy, dc) != (0, 0, 0)
    ]
    near_line = [line_peer(k % n_line) for k in (3, -3, 2, -2)]
    near_halo = [at(dlat, dlon) for dlat, dlon in sides]
    plane_order = sorted(range(1, n_plane), key=lambda j: -min(j // 2, n_lat - j // 2))
    line_order = sorted(range(1, n_line), key=lambda j: -min(j, n_line - j))
    barrier = pltpu.get_barrier_semaphore()
    for peer in near_halo + near_line + near_plane:
        pl.semaphore_signal(barrier, inc=1, device_id=peer, device_id_type=MESH)

    copies = [
        pltpu.make_async_copy(winds, raw_winds, in_sem.at[0]),
    ]
    for t in range(TILES):
        lanes = pl.ds(t * 128, 128)
        copies.append(pltpu.make_async_copy(tracer.at[:, lanes], raw.at[t], in_sem.at[1 + t]))
        copies.append(pltpu.make_async_copy(flux.at[:, lanes], raw_flux.at[t], in_sem.at[1 + TILES + t]))
    obs_copies = [
        pltpu.make_async_copy(src, dst, in_sem.at[1 + 2 * TILES + i])
        for i, (src, dst) in enumerate(((cells_in, cells), (count_in, count), (value_in, value), (var_in, var)))
    ]
    for copy in copies + obs_copies:
        copy.start()

    for copy in copies:
        copy.wait()
    level = lax.broadcasted_iota(jnp.int32, (LEV, 1), 0)
    wide_winds[:, 0:COLS] = 0.5 * raw_winds[...]

    def enter(r, carry):
        for t in range(TILES):
            own = raw[t, pl.ds(r, LEV, stride=ROWS), :]
            surface = raw_flux[t, pl.ds(r, 1), :]
            field[r, :, t * 128:t * 128 + 128] = own + jnp.where(level == 0, surface, 0.0)
        for v in range(3):
            wc[v, r] = wide_winds[pl.ds(v * LEV * ROWS + r, LEV, stride=ROWS), :]
        return carry

    lax.fori_loop(0, ROWS, enter, 0, unroll=8)

    lane = lax.broadcasted_iota(jnp.int32, (LEV, 128), 1)

    def edge(r, carry):
        first, final = carry
        for v in range(3):
            w = wc[v, r]
            here = lane == v * ROWS + r
            first = jnp.where(here, w[:, 0:1], first)
            final = jnp.where(here, w[:, COLS - 1:COLS], final)
        return first, final

    zero_tile = jnp.zeros((LEV, 128), F32)
    first, final = lax.fori_loop(0, ROWS, edge, (zero_tile, zero_tile), unroll=True)
    wcol_out[0] = first
    wcol_out[1] = final
    for side, r in ((0, 0), (1, ROWS - 1)):
        packed_row = jnp.where(lane < COLS, wc[0, r], 0.0)
        for v in (1, 2):
            here = (lane >= v * COLS) & (lane < v * COLS + COLS)
            packed_row = jnp.where(here, pltpu.roll(wc[v, r], v * COLS, 1), packed_row)
        wrow_out[side] = packed_row

    def tuck(i, carry):
        for side, start, free, gap in ((0, 0, 0, 2 * M), (1, WIDTH - 128, 32, 0)):
            fourth = field[4 * i + 3, :, start:start + 128]
            for j in range(3):
                shift = (gap - free - 32 * j) % 128
                moved = pltpu.roll(fourth, shift, 1) if shift else fourth
                here = (lane >= gap) & (lane < gap + 32)
                lon_out[side, 3 * i + j] = jnp.where(here, moved, field[4 * i + j, :, start:start + 128])
        return carry

    lax.fori_loop(0, ROWS // 4, tuck, 0, unroll=True)

    pl.semaphore_wait(barrier, len(near_halo + near_line + near_plane))

    def send(i, src, dst, to):
        return pltpu.make_async_remote_copy(
            src_ref=src, dst_ref=dst, send_sem=halo_send.at[i], recv_sem=halo_recv.at[i],
            device_id=to, device_id_type=MESH,
        )

    own_lanes = pl.ds(0, WIDTH)
    left_tile, right_tile = pl.ds(0, 128), pl.ds(WIDTH - 128, 128)
    east_tile, west_tile = pl.ds(EAST, 128), pl.ds(WEST, 128)
    top, bottom = 0, ROWS - 1
    halos = [
        send(0, wcol_out.at[0], wcol_in.at[0], at(0, -1)),
        send(1, wcol_out.at[1], wcol_in.at[1], at(0, 1)),
        send(2, wrow_out.at[0], wrow_in.at[0], at(-1, 0)),
        send(3, wrow_out.at[1], wrow_in.at[1], at(1, 0)),
        send(4, field.at[pl.ds(top, 2), :, own_lanes], field.at[pl.ds(SOUTH, 2), :, own_lanes], at(-1, 0)),
        send(5, field.at[pl.ds(bottom - 1, 2), :, own_lanes], field.at[pl.ds(NORTH - 1, 2), :, own_lanes], at(1, 0)),
        send(6, lon_out.at[0], lon_in.at[0], at(0, -1)),
        send(7, lon_out.at[1], lon_in.at[1], at(0, 1)),
        send(8, field.at[top, :, left_tile], field.at[SOUTH, :, east_tile], at(-1, -1)),
        send(9, field.at[top, :, right_tile], field.at[SOUTH, :, west_tile], at(-1, 1)),
        send(10, field.at[bottom, :, left_tile], field.at[NORTH, :, east_tile], at(1, -1)),
        send(11, field.at[bottom, :, right_tile], field.at[NORTH, :, west_tile], at(1, 1)),
    ]
    for copy in halos:
        copy.start()
    for peer in near_line + near_plane:
        pl.semaphore_signal(here_sem.at[0], inc=1, device_id=peer, device_id_type=MESH)

    spread_col = lax.broadcasted_iota(jnp.int32, (COLS, WIDTH), 0)
    spread_lane = lax.broadcasted_iota(jnp.int32, (COLS, WIDTH), 1)
    spread = jnp.where((spread_lane >= spread_col * M) & (spread_lane < spread_col * M + M), 1.0, 0.0).astype(BF16)

    def spread_rows(w, v, start, rows):
        a = w.astype(BF16)
        rest = w - a.astype(F32)
        b = rest.astype(BF16)
        c = (rest - b.astype(F32)).astype(BF16)
        wide = (
            jnp.dot(a, spread, preferred_element_type=F32)
            + jnp.dot(b, spread, preferred_element_type=F32)
            + jnp.dot(c, spread, preferred_element_type=F32)
        )
        wx[v, pl.ds(start, rows), :, 0:WIDTH] = wide.reshape(rows, LEV, WIDTH)

    for v in range(3):
        spread_rows(wc[v, :, :, 0:COLS].reshape(ROWS * LEV, COLS), v, 0, ROWS)

    def stencil(c, n, s, u, v, w, first, final):
        width = c.shape[1]
        keep = slice(first, final)
        east, west = pltpu.roll(c, width - M, 1)[:, keep], pltpu.roll(c, M, 1)[:, keep]
        c = c[:, keep]
        above = jnp.where(level == LEV - 1, 0.0, pltpu.roll(c, LEV - 1, 0))
        below = jnp.where(level == 0, 0.0, pltpu.roll(c, 1, 0))
        spread_out = (east + west) + (s + n) + (above + below)
        carried = u * (east - west) + v * (s - n) + w * (above - below)
        return (1.0 - 6.0 * KH) * c + KH * spread_out - carried

    def strip(src, r, width):
        n, s = lax.rem(r + ROWS_X - 1, ROWS_X), lax.rem(r + 1, ROWS_X)
        return stencil(
            src[r, :, 0:width], src[n, :, 0:width], src[s, :, 0:width],
            wx[0, r, :, 0:width], wx[1, r, :, 0:width], wx[2, r, :, 0:width], 0, width,
        )

    def west_end(src, r, first):
        def of(ref, i):
            return jnp.concatenate([ref[i, :, WEST:WEST + 128], ref[i, :, 0:128]], axis=1)[:, first:]

        c = jnp.concatenate([src[r, :, WEST:WEST + 128], src[r, :, 0:256]], axis=1)
        return stencil(
            c, of(src, r - 1), of(src, r + 1), of(wx.at[0], r), of(wx.at[1], r), of(wx.at[2], r), first, 256
        )

    def east_end(src, r, final):
        lanes = slice(WIDTH - 128, WIDTH - 256 + final)
        return stencil(
            src[r, :, WIDTH - 256:WIDTH + 128], src[r - 1, :, lanes], src[r + 1, :, lanes],
            wx[0, r, :, lanes], wx[1, r, :, lanes], wx[2, r, :, lanes], 128, final,
        )

    def put(r, tiles, value):
        for i, t in enumerate(tiles):
            last[t, pl.ds(pl.multiple_of(r * LEV, LEV), LEV), :] = value[:, i * 128:i * 128 + 128]

    def inner_first(r, carry):
        mid[r, :, 0:WIDTH] = strip(field, r, WIDTH)
        return carry

    lax.fori_loop(1, ROWS - 1, inner_first, 0, unroll=2)

    def inner_second(r, carry):
        put(r, range(1, TILES - 1), strip(mid, r, WIDTH)[:, 128:WIDTH - 128])
        return carry

    lax.fori_loop(2, ROWS - 2, inner_second, 0, unroll=2)

    for copy in obs_copies:
        copy.wait()

    def note(k, carry):
        live = jnp.where(k < count[0], 1.0, 0.0)
        vals[0, pl.ds(k, 1), :] = jnp.full((1, 128), live, F32)
        vals[1, pl.ds(k, 1), :] = jnp.full((1, 128), var[k], F32)
        vals[2, pl.ds(k, 1), :] = jnp.full((1, 128), value[k], F32)
        return carry

    lax.fori_loop(0, OBS, note, 0)
    spots = []
    for k in range(OBS):
        row, first_lane, lev = cells[0, k] - lat * ROWS, (cells[1, k] - lon * COLS) * M, cells[2, k]
        tile = jnp.clip(first_lane // 128, 0, TILES - 2)
        spots.append((jnp.clip(row * LEV + lev, 0, LEV * ROWS - 1), tile, first_lane - tile * 128, lax.rem(tile, 3)))

    pl.semaphore_wait(here_sem.at[0], len(near_line + near_plane))
    for peer in near_line:
        pl.semaphore_signal(here_sem.at[1], inc=1, device_id=peer, device_id_type=MESH)

    for i in range(4):
        halos[i].wait_recv()
    for v in range(3):
        for side, start in ((0, SOUTH), (1, NORTH)):
            spread_rows(wrow_in[side][:, v * COLS:v * COLS + COLS], v, start, 1)
        for side, start in ((0, EAST), (1, WEST)):
            got = wcol_in[side]
            for r in range(ROWS):
                wx[v, r, :, start:start + 128] = jnp.broadcast_to(got[:, v * ROWS + r:v * ROWS + r + 1], (LEV, 128))

    for i in (6, 7):
        halos[i].wait_recv()

    def untuck(i, carry):
        for side, start, free, gap in ((0, EAST, 0, 2 * M), (1, WEST, 32, 0)):
            fourth = zero_tile
            for j in range(3):
                tile = lon_in[side, 3 * i + j]
                field[4 * i + j, :, start:start + 128] = tile
                shift = (free + 32 * j - gap) % 128
                moved = pltpu.roll(tile, shift, 1) if shift else tile
                here = (lane >= free + 32 * j) & (lane < free + 32 * j + 32)
                fourth = jnp.where(here, moved, fourth)
            field[4 * i + 3, :, start:start + 128] = fourth
        return carry

    lax.fori_loop(0, ROWS // 4, untuck, 0, unroll=True)

    def ends_first(r, carry):
        new = west_end(field, r, 0)
        mid[r, :, WEST:WEST + 128] = new[:, 0:128]
        mid[r, :, 0:128] = new[:, 128:256]
        mid[r, :, WIDTH - 128:WIDTH + 128] = east_end(field, r, 384)
        return carry

    lax.fori_loop(1, ROWS - 1, ends_first, 0, unroll=7)

    for i in (4, 5, 8, 9, 10, 11):
        halos[i].wait_recv()
    has_north, has_south = lat > 0, lat < n_lat - 1
    field[NORTH] = jnp.where(has_north, field[NORTH], 0.0)
    field[SOUTH] = jnp.where(has_south, field[SOUTH], 0.0)
    mid[0] = strip(field, 0, WIDE)
    mid[ROWS - 1] = strip(field, ROWS - 1, WIDE)
    mid[NORTH] = jnp.where(has_north, strip(field, NORTH, WIDE), 0.0)
    mid[SOUTH] = jnp.where(has_south, strip(field, SOUTH, WIDE), 0.0)

    for r in (0, 1, ROWS - 2, ROWS - 1):
        put(r, range(TILES), strip(mid, r, WIDE)[:, 0:WIDTH])

    def ends_second(r, carry):
        put(r, (0,), west_end(mid, r, 128))
        put(r, (TILES - 1,), east_end(mid, r, 256))
        return carry

    lax.fori_loop(2, ROWS - 2, ends_second, 0, unroll=6)

    lane_1 = lax.broadcasted_iota(jnp.int32, (1, 128), 1)

    for k, (cell, tile, start, turn) in enumerate(spots):
        lines = []
        for t in range(2):
            inside = (lane_1 >= start - t * 128) & (lane_1 < start - t * 128 + M)
            lines.append(jnp.where(inside, last[tile + t, pl.ds(cell, 1), :], 0.0))
        for t in range(3):
            one = jnp.where(turn == t, lines[0], 0.0)
            seen[t, k:k + 1, :] = jnp.where(turn == (t + 2) % 3, lines[1], one)
    hx = jnp.concatenate([seen[t] for t in range(3)], axis=1)
    hx = hx + pltpu.roll(hx, GROUP // 2, 1)
    hx = hx + pltpu.roll(hx, GROUP // 4, 1)
    hx = hx + pltpu.roll(hx, GROUP // 8, 1)
    lane_o = lax.broadcasted_iota(jnp.int32, (OBS, 128), 1)
    hbar = jnp.sum(jnp.where(lane_o < M, hx[:, 0:128], 0.0), axis=1, keepdims=True) * (1.0 / M)
    y = hx - hbar
    q = vals[0] / vals[1]
    d = vals[2] - hbar

    y0 = y[:, 0:128]
    y32 = pltpu.roll(y, 32, 1)[:, 0:128]
    w0 = jnp.where(lane_o < 48, y0, jnp.where(lane_o == 96, d, 0.0))
    w1 = jnp.where((lane_o >= 48) & (lane_o < 80), y32, jnp.where(lane_o == 97, d, 0.0))
    w2 = jnp.where((lane_o >= 80) & (lane_o < 96), y0, jnp.where(lane_o == 98, d, 0.0))
    l1 = pltpu.roll(y, GROUP - 16, 1)[:, 0:128]
    l2 = pltpu.roll(y, GROUP - 32, 1)[:, 0:128]
    lhs = jnp.concatenate([q * y0, q * l1, q * l2], axis=0)
    rhs = jnp.concatenate([w0, w1, w2], axis=0)
    packed = lax.dot_general(lhs, rhs, (((0,), (0,)), ((), ())), precision=HP, preferred_element_type=F32)[0:16]
    pack[...] = packed.reshape(2, 8, 128)

    for j in plane_order:
        pltpu.make_async_remote_copy(
            src_ref=pack.at[lax.rem(lat + j // 2, 2)], dst_ref=part1.at[j - 1],
            send_sem=ar_send.at[0], recv_sem=ar_recv.at[0], device_id=plane_peer(j), device_id_type=MESH,
        ).start()

    for t in range(TILES):
        lanes = pl.ds(t % 3 * 128, 128)
        for lev in range(LEV + 1):
            part = last[t, pl.ds(lev, ROWS, stride=LEV), :] if lev < LEV else raw_flux[t]
            hi = part.astype(BF16)
            rows = pl.ds(t // 3 * 144 + lev * ROWS, ROWS)
            high[rows, lanes] = hi
            low[rows, lanes] = (part - hi.astype(F32)).astype(BF16)

    factors = [
        pltpu.make_async_copy(high, high_out, out_sem.at[0]), pltpu.make_async_copy(low, low_out, out_sem.at[1]),
    ]
    for copy in factors:
        copy.start()

    def wait_all(ref, sem):
        pltpu.make_async_copy(ref, ref, sem).wait()

    wait_all(part1, ar_recv.at[0])
    sum1[...] = pack[core] + jnp.sum(part1[...], axis=0)
    pl.semaphore_wait(here_sem.at[1], len(near_line))
    for j in line_order:
        pltpu.make_async_remote_copy(
            src_ref=sum1, dst_ref=part2.at[j - 1],
            send_sem=ar_send.at[1], recv_sem=ar_recv.at[1], device_id=line_peer(j), device_id_type=MESH,
        ).start()
    wait_all(part2, ar_recv.at[1])
    sum2[...] = sum1[...] + jnp.sum(part2[...], axis=0)
    swap = pltpu.make_async_remote_copy(
        src_ref=sum2, dst_ref=part3, send_sem=ar_send.at[2], recv_sem=ar_recv.at[2],
        device_id=partner, device_id_type=MESH,
    )
    swap.start()
    swap.wait_recv()
    mine, other = sum2[...], part3[...]
    total = jnp.concatenate([jnp.where(core == 0, mine, other), jnp.where(core == 0, other, mine)], axis=0)

    lane_p = lax.broadcasted_iota(jnp.int32, (16, 128), 1)
    u0 = jnp.where(lane_p < 48, total, 0.0)
    u1 = jnp.where((lane_p >= 16) & (lane_p < 48), pltpu.roll(total, 128 - 32, 1), 0.0)
    u2 = jnp.where((lane_p >= 32) & (lane_p < 48), pltpu.roll(total, 128 - 48, 1), 0.0)
    upper = jnp.concatenate([u0, u1, u2, jnp.zeros((80, 128), F32)], axis=0)
    flipped = upper.T
    row_s = lax.broadcasted_iota(jnp.int32, (M, M), 0)
    col_s = lax.broadcasted_iota(jnp.int32, (M, M), 1)
    gram = jnp.where(row_s // 16 > col_s // 16, flipped[0:M, 0:M], upper[0:M, 0:M])
    proj = jnp.concatenate([total[:, 96:97], total[:, 97:98], total[:, 98:99]], axis=0)
    eye = jnp.where(row_s == col_s, 1.0, 0.0)

    def dot(a, b):
        return jnp.dot(a, b, precision=HP, preferred_element_type=F32)

    system = (M - 1.0) * eye + gram
    square = dot(system, system)
    norm2 = jnp.sum(system * system, keepdims=True)
    scale = jnp.sqrt(norm2)
    root_now = system / scale
    factor = 0.5 * (3.0 * eye - root_now)
    root_now, inverse_now = 1.5 * root_now - 0.5 * (square / norm2), factor
    for step in range(1, NS_ITERS):
        factor = 0.5 * (3.0 * eye - dot(inverse_now, root_now))
        if step < NS_ITERS - 1:
            root_now = dot(root_now, factor)
        inverse_now = dot(factor, inverse_now)
    inner = jnp.sum(inverse_now * proj, axis=0, keepdims=True)
    wmean = jnp.sum(inverse_now * inner, axis=1, keepdims=True) / scale
    mixed = wmean + jnp.sqrt((M - 1.0) / scale) * inverse_now
    mixing = mixed - jnp.sum(mixed, axis=0, keepdims=True) * (1.0 / M) + 1.0 / M

    mix[...] = mixing
    result = pltpu.make_async_copy(mix, mix_out, out_sem.at[2])
    result.start()
    for copy in halos:
        copy.wait_send()
    wait_all(part1, ar_send.at[0])
    wait_all(part2, ar_send.at[1])
    swap.wait_send()
    for copy in factors:
        copy.wait()
    result.wait()


def transform(high_in, low_in, mix_in, tracer_out, flux_out, high, low, mix, outs, in_sem, out_sem):
    mix_copy = pltpu.make_async_copy(mix_in, mix, in_sem.at[6])
    mix_copy.start()
    copies = []
    for g in range(3):
        rows = pl.ds(g * 144, 144)
        copies.append(pltpu.make_async_copy(high_in.at[rows], high.at[rows], in_sem.at[2 * g]))
        copies.append(pltpu.make_async_copy(low_in.at[rows], low.at[rows], in_sem.at[2 * g + 1]))
    for copy in copies:
        copy.start()

    rep_row = lax.broadcasted_iota(jnp.int32, (M, GROUP), 0)
    rep_lane = lax.broadcasted_iota(jnp.int32, (M, GROUP), 1)
    rep = jnp.where(lax.rem(rep_lane, M) == rep_row, 1.0, 0.0).astype(BF16)
    mix_copy.wait()
    mixing = mix[...]
    g_high = mixing.astype(BF16)
    g_low = (mixing - g_high.astype(F32)).astype(BF16)
    g_high = jnp.dot(g_high, rep, preferred_element_type=F32)
    g_low = jnp.dot(g_low, rep, preferred_element_type=F32)

    def diagonal(g):
        return jnp.concatenate(
            [jnp.where((rep_lane >= b * M) & (rep_lane < b * M + M), g, 0.0).astype(BF16) for b in range(8)], axis=0
        )

    d_high, d_low = diagonal(g_high), diagonal(g_low)
    done = []
    for copy in copies:
        copy.wait()
    for n, (k0, k1) in enumerate(((0, 256), (0, 384), (128, 384))):
        cols = slice(n * 128, n * 128 + 128)
        w_h, w_l = d_high[k0:k1, cols], d_low[k0:k1, cols]
        w = jnp.concatenate([w_h, w_l], axis=1)
        both = jnp.dot(high[:, k0:k1], w, preferred_element_type=F32)
        res = both[:, 0:128] + both[:, 128:256] + jnp.dot(low[:, k0:k1], w_h, preferred_element_type=F32)
        for g in range(3):
            outs[g * 3 + n] = res[g * 144:(g + 1) * 144]
        for t in range(n, TILES, 3):
            lanes = pl.ds(t * 128, 128)
            done.append(pltpu.make_async_copy(outs.at[t, pl.ds(0, LEV * ROWS)], tracer_out.at[:, lanes], out_sem.at[t]))
            done.append(
                pltpu.make_async_copy(outs.at[t, pl.ds(LEV * ROWS, ROWS)], flux_out.at[:, lanes], out_sem.at[TILES + t])
            )
        for copy in done[-6:]:
            copy.start()
    for copy in done:
        copy.wait()


def on_device(n_lat, n_lon, tracer, flux, winds, obs_cells, obs_count, obs_value, obs_var):
    hbm = pl.BlockSpec(memory_space=pltpu.HBM)
    n_plane, n_line = 2 * n_lat, n_lon // 2
    vmem = pltpu.VMEM
    high, low, mixing = pl.pallas_call(
        functools.partial(kernel, n_lat, n_lon),
        out_shape=(
            jax.ShapeDtypeStruct((432, GROUP), BF16),
            jax.ShapeDtypeStruct((432, GROUP), BF16),
            jax.ShapeDtypeStruct((M, M), F32),
        ),
        in_specs=[hbm] * 7,
        out_specs=(hbm, hbm, hbm),
        scratch_shapes=[
            vmem((TILES, LEV * ROWS, 128), F32),
            vmem((TILES, ROWS, 128), F32),
            vmem((3 * LEV * ROWS, COLS), F32),
            vmem((3 * LEV * ROWS, 128), F32),
            vmem((ROWS_X, LEV, WIDE), F32),
            vmem((ROWS_X, LEV, WIDE), F32),
            vmem((TILES, LEV * ROWS, 128), F32),
            vmem((3, ROWS, LEV, 128), F32),
            vmem((3, ROWS_X, LEV, WIDE), F32),
            vmem((2, LEV, 128), F32),
            vmem((2, LEV, 128), F32),
            vmem((2, LEV, 128), F32),
            vmem((2, LEV, 128), F32),
            vmem((2, 12, LEV, 128), F32),
            vmem((2, 12, LEV, 128), F32),
            vmem((3, OBS, 128), F32),
            vmem((3, OBS, 128), F32),
            vmem((2, 8, 128), F32),
            vmem((n_plane - 1, 8, 128), F32),
            vmem((n_line - 1, 8, 128), F32),
            vmem((8, 128), F32),
            vmem((8, 128), F32),
            vmem((8, 128), F32),
            vmem((432, GROUP), BF16),
            vmem((432, GROUP), BF16),
            vmem((M, M), F32),
            pltpu.SMEM((3, OBS), jnp.int32),
            pltpu.SMEM((1,), jnp.int32),
            pltpu.SMEM((OBS,), F32),
            pltpu.SMEM((OBS,), F32),
            pltpu.SemaphoreType.DMA((5 + 2 * TILES,)),
            pltpu.SemaphoreType.DMA((3,)),
            pltpu.SemaphoreType.DMA((12,)),
            pltpu.SemaphoreType.DMA((12,)),
            pltpu.SemaphoreType.DMA((3,)),
            pltpu.SemaphoreType.DMA((3,)),
            pltpu.SemaphoreType.REGULAR((2,)),
        ],
        compiler_params=pltpu.CompilerParams(
            collective_id=0, has_side_effects=True, vmem_limit_bytes=62 * 1024 * 1024
        ),
        name="analysis",
    )(
        tracer.reshape(LEV * ROWS, WIDTH), flux, winds.reshape(3 * LEV * ROWS, COLS),
        obs_cells.T, obs_count, obs_value, obs_var,
    )
    tracer_out, flux_out = pl.pallas_call(
        transform,
        out_shape=(
            jax.ShapeDtypeStruct((LEV * ROWS, WIDTH), F32),
            jax.ShapeDtypeStruct((ROWS, WIDTH), F32),
        ),
        in_specs=[hbm] * 3,
        out_specs=(hbm, hbm),
        scratch_shapes=[
            vmem((432, GROUP), BF16),
            vmem((432, GROUP), BF16),
            vmem((M, M), F32),
            vmem((TILES, 144, 128), F32),
            pltpu.SemaphoreType.DMA((7,)),
            pltpu.SemaphoreType.DMA((2 * TILES,)),
        ],
        compiler_params=pltpu.CompilerParams(vmem_limit_bytes=62 * 1024 * 1024),
        name="transform",
    )(high, low, mixing)
    return tracer_out.reshape(LEV, ROWS, WIDTH), flux_out


def solution(mesh):
    return jax.shard_map(
        functools.partial(on_device, mesh.shape["lat"], mesh.shape["lon"]),
        mesh=mesh,
        in_specs=(
            P(None, "lat", "lon"),
            P("lat", "lon"),
            P(None, None, "lat", "lon"),
            P(("lat", "lon"), None),
            P(("lat", "lon")),
            P(("lat", "lon")),
            P(("lat", "lon")),
        ),
        out_specs=(P(None, "lat", "lon"), P("lat", "lon")),
        check_vma=False,
    )
```

```python
import functools

import jax
import jax.numpy as jnp
from jax import lax
from jax.experimental import pallas as pl
from jax.experimental.pallas import tpu as pltpu
from jax.sharding import PartitionSpec as P

M = 48
NS_ITERS = 5
KH = 0.15
MESH = pl.DeviceIdType.MESH
HP = lax.Precision.HIGHEST
F32 = jnp.float32
BF16 = jnp.bfloat16

LEV, ROWS, COLS, OBS = 8, 16, 24, 16
TILES = 9
WIDTH = COLS * M
WIDE = WIDTH + 256
EAST, WEST = WIDTH, WIDTH + 128
ROWS_X = ROWS + 4
SOUTH, NORTH = ROWS, ROWS + 3
GROUP = 8 * M


def kernel(
    n_lat, n_lon,
    tracer, flux, winds, cells_in, count_in, value_in, var_in,
    high_out, low_out, mix_out,
    raw, raw_flux, raw_winds, wide_winds, field, mid, last, wc, wx, wcol_out, wcol_in,
    wrow_out, wrow_in, lon_out, lon_in, seen, vals, pack, part1, part2, part3, sum1, sum2, high, low, mix,
    cells, count, value, var, in_sem, out_sem, halo_send, halo_recv, ar_send, ar_recv, here_sem,
):
    lat, lon = lax.axis_index("lat"), lax.axis_index("lon")

    def at(dlat, dlon):
        return (lax.rem(lat + (dlat + n_lat), n_lat), lax.rem(lon + (dlon + n_lon), n_lon))

    sides = [(1, 0), (-1, 0), (0, 1), (0, -1), (1, 1), (1, -1), (-1, 1), (-1, -1)]
    pair = lax.rem(lon, 2)
    base = lon - pair

    def plane_peer(j):
        return (lax.rem(lat + j // 2, n_lat), base + lax.rem(pair + j, 2))

    def line_peer(j):
        return (lat, lax.rem(lon + 2 * j, n_lon))

    core = lax.rem(lat, 2)
    partner = (lat + 1 - 2 * core, lon)
    n_plane, n_line = 2 * n_lat, n_lon // 2

    n_x = n_lat // 4
    x, y = lat // 4, lax.rem(lat // 2, 2) * 2 + pair

    def plane_near(dx, dy, dc):
        to_x, to_y = lax.rem(x + (dx + n_x), n_x), lax.rem(y + (dy + 4), 4)
        return (to_x * 4 + to_y // 2 * 2 + lax.rem(core + dc, 2), base + lax.rem(to_y, 2))

    near_plane = [
        plane_near(dx, dy, dc) for dx in (-1, 1, 0) for dy in (-1, 1, 0) for dc in (1, 0) if (dx, dy, dc) != (0, 0, 0)
    ]
    near_line = [line_peer(k % n_line) for k in (3, -3, 2, -2)]
    near_halo = [at(dlat, dlon) for dlat, dlon in sides]
    plane_order = sorted(range(1, n_plane), key=lambda j: -min(j // 2, n_lat - j // 2))
    line_order = sorted(range(1, n_line), key=lambda j: -min(j, n_line - j))
    barrier = pltpu.get_barrier_semaphore()
    for peer in near_halo + near_line + near_plane:
        pl.semaphore_signal(barrier, inc=1, device_id=peer, device_id_type=MESH)

    copies = [
        pltpu.make_async_copy(winds, raw_winds, in_sem.at[0]),
    ]
    for t in range(TILES):
        lanes = pl.ds(t * 128, 128)
        copies.append(pltpu.make_async_copy(tracer.at[:, lanes], raw.at[t], in_sem.at[1 + t]))
        copies.append(pltpu.make_async_copy(flux.at[:, lanes], raw_flux.at[t], in_sem.at[1 + TILES + t]))
    obs_copies = [
        pltpu.make_async_copy(src, dst, in_sem.at[1 + 2 * TILES + i])
        for i, (src, dst) in enumerate(((cells_in, cells), (count_in, count), (value_in, value), (var_in, var)))
    ]
    for copy in copies + obs_copies:
        copy.start()

    for copy in copies:
        copy.wait()
    level = lax.broadcasted_iota(jnp.int32, (LEV, 1), 0)
    wide_winds[:, 0:COLS] = 0.5 * raw_winds[...]

    def enter(r, carry):
        for t in range(TILES):
            own = raw[t, pl.ds(r, LEV, stride=ROWS), :]
            surface = raw_flux[t, pl.ds(r, 1), :]
            field[r, :, t * 128:t * 128 + 128] = own + jnp.where(level == 0, surface, 0.0)
        for v in range(3):
            wc[v, r] = wide_winds[pl.ds(v * LEV * ROWS + r, LEV, stride=ROWS), :]
        return carry

    lax.fori_loop(0, ROWS, enter, 0, unroll=8)

    lane = lax.broadcasted_iota(jnp.int32, (LEV, 128), 1)

    def edge(r, carry):
        first, final = carry
        for v in range(3):
            w = wc[v, r]
            here = lane == v * ROWS + r
            first = jnp.where(here, w[:, 0:1], first)
            final = jnp.where(here, w[:, COLS - 1:COLS], final)
        return first, final

    zero_tile = jnp.zeros((LEV, 128), F32)
    first, final = lax.fori_loop(0, ROWS, edge, (zero_tile, zero_tile), unroll=True)
    wcol_out[0] = first
    wcol_out[1] = final
    for side, r in ((0, 0), (1, ROWS - 1)):
        packed_row = jnp.where(lane < COLS, wc[0, r], 0.0)
        for v in (1, 2):
            here = (lane >= v * COLS) & (lane < v * COLS + COLS)
            packed_row = jnp.where(here, pltpu.roll(wc[v, r], v * COLS, 1), packed_row)
        wrow_out[side] = packed_row

    def tuck(i, carry):
        for side, start, free, gap in ((0, 0, 0, 2 * M), (1, WIDTH - 128, 32, 0)):
            fourth = field[4 * i + 3, :, start:start + 128]
            for j in range(3):
                shift = (gap - free - 32 * j) % 128
                moved = pltpu.roll(fourth, shift, 1) if shift else fourth
                here = (lane >= gap) & (lane < gap + 32)
                lon_out[side, 3 * i + j] = jnp.where(here, moved, field[4 * i + j, :, start:start + 128])
        return carry

    lax.fori_loop(0, ROWS // 4, tuck, 0, unroll=True)

    pl.semaphore_wait(barrier, len(near_halo + near_line + near_plane))

    def send(i, src, dst, to):
        return pltpu.make_async_remote_copy(
            src_ref=src, dst_ref=dst, send_sem=halo_send.at[i], recv_sem=halo_recv.at[i],
            device_id=to, device_id_type=MESH,
        )

    own_lanes = pl.ds(0, WIDTH)
    left_tile, right_tile = pl.ds(0, 128), pl.ds(WIDTH - 128, 128)
    east_tile, west_tile = pl.ds(EAST, 128), pl.ds(WEST, 128)
    top, bottom = 0, ROWS - 1
    halos = [
        send(0, wcol_out.at[0], wcol_in.at[0], at(0, -1)),
        send(1, wcol_out.at[1], wcol_in.at[1], at(0, 1)),
        send(2, wrow_out.at[0], wrow_in.at[0], at(-1, 0)),
        send(3, wrow_out.at[1], wrow_in.at[1], at(1, 0)),
        send(4, field.at[pl.ds(top, 2), :, own_lanes], field.at[pl.ds(SOUTH, 2), :, own_lanes], at(-1, 0)),
        send(5, field.at[pl.ds(bottom - 1, 2), :, own_lanes], field.at[pl.ds(NORTH - 1, 2), :, own_lanes], at(1, 0)),
        send(6, lon_out.at[0], lon_in.at[0], at(0, -1)),
        send(7, lon_out.at[1], lon_in.at[1], at(0, 1)),
        send(8, field.at[top, :, left_tile], field.at[SOUTH, :, east_tile], at(-1, -1)),
        send(9, field.at[top, :, right_tile], field.at[SOUTH, :, west_tile], at(-1, 1)),
        send(10, field.at[bottom, :, left_tile], field.at[NORTH, :, east_tile], at(1, -1)),
        send(11, field.at[bottom, :, right_tile], field.at[NORTH, :, west_tile], at(1, 1)),
    ]
    for copy in halos:
        copy.start()
    for peer in near_line + near_plane:
        pl.semaphore_signal(here_sem.at[0], inc=1, device_id=peer, device_id_type=MESH)

    spread_col = lax.broadcasted_iota(jnp.int32, (COLS, WIDTH), 0)
    spread_lane = lax.broadcasted_iota(jnp.int32, (COLS, WIDTH), 1)
    spread = jnp.where((spread_lane >= spread_col * M) & (spread_lane < spread_col * M + M), 1.0, 0.0).astype(BF16)

    def spread_rows(w, v, start, rows):
        a = w.astype(BF16)
        rest = w - a.astype(F32)
        b = rest.astype(BF16)
        c = (rest - b.astype(F32)).astype(BF16)
        wide = (
            jnp.dot(a, spread, preferred_element_type=F32)
            + jnp.dot(b, spread, preferred_element_type=F32)
            + jnp.dot(c, spread, preferred_element_type=F32)
        )
        wx[v, pl.ds(start, rows), :, 0:WIDTH] = wide.reshape(rows, LEV, WIDTH)

    for v in range(3):
        spread_rows(wc[v, :, :, 0:COLS].reshape(ROWS * LEV, COLS), v, 0, ROWS)

    def stencil(c, n, s, u, v, w, first, final):
        width = c.shape[1]
        keep = slice(first, final)
        east, west = pltpu.roll(c, width - M, 1)[:, keep], pltpu.roll(c, M, 1)[:, keep]
        c = c[:, keep]
        above = jnp.where(level == LEV - 1, 0.0, pltpu.roll(c, LEV - 1, 0))
        below = jnp.where(level == 0, 0.0, pltpu.roll(c, 1, 0))
        spread_out = (east + west) + (s + n) + (above + below)
        carried = u * (east - west) + v * (s - n) + w * (above - below)
        return (1.0 - 6.0 * KH) * c + KH * spread_out - carried

    def strip(src, r, width):
        n, s = lax.rem(r + ROWS_X - 1, ROWS_X), lax.rem(r + 1, ROWS_X)
        return stencil(
            src[r, :, 0:width], src[n, :, 0:width], src[s, :, 0:width],
            wx[0, r, :, 0:width], wx[1, r, :, 0:width], wx[2, r, :, 0:width], 0, width,
        )

    def west_end(src, r, first):
        def of(ref, i):
            return jnp.concatenate([ref[i, :, WEST:WEST + 128], ref[i, :, 0:128]], axis=1)[:, first:]

        c = jnp.concatenate([src[r, :, WEST:WEST + 128], src[r, :, 0:256]], axis=1)
        return stencil(
            c, of(src, r - 1), of(src, r + 1), of(wx.at[0], r), of(wx.at[1], r), of(wx.at[2], r), first, 256
        )

    def east_end(src, r, final):
        lanes = slice(WIDTH - 128, WIDTH - 256 + final)
        return stencil(
            src[r, :, WIDTH - 256:WIDTH + 128], src[r - 1, :, lanes], src[r + 1, :, lanes],
            wx[0, r, :, lanes], wx[1, r, :, lanes], wx[2, r, :, lanes], 128, final,
        )

    def put(r, tiles, value):
        for i, t in enumerate(tiles):
            last[t, pl.ds(pl.multiple_of(r * LEV, LEV), LEV), :] = value[:, i * 128:i * 128 + 128]

    def inner_first(r, carry):
        mid[r, :, 0:WIDTH] = strip(field, r, WIDTH)
        return carry

    lax.fori_loop(1, ROWS - 1, inner_first, 0, unroll=2)

    def inner_second(r, carry):
        put(r, range(1, TILES - 1), strip(mid, r, WIDTH)[:, 128:WIDTH - 128])
        return carry

    lax.fori_loop(2, ROWS - 2, inner_second, 0, unroll=2)

    for copy in obs_copies:
        copy.wait()

    def note(k, carry):
        live = jnp.where(k < count[0], 1.0, 0.0)
        vals[0, pl.ds(k, 1), :] = jnp.full((1, 128), live, F32)
        vals[1, pl.ds(k, 1), :] = jnp.full((1, 128), var[k], F32)
        vals[2, pl.ds(k, 1), :] = jnp.full((1, 128), value[k], F32)
        return carry

    lax.fori_loop(0, OBS, note, 0)
    spots = []
    for k in range(OBS):
        row, first_lane, lev = cells[0, k] - lat * ROWS, (cells[1, k] - lon * COLS) * M, cells[2, k]
        tile = jnp.clip(first_lane // 128, 0, TILES - 2)
        spots.append((jnp.clip(row * LEV + lev, 0, LEV * ROWS - 1), tile, (256 - first_lane + tile * 128) & 255))

    pl.semaphore_wait(here_sem.at[0], len(near_line + near_plane))
    for peer in near_line:
        pl.semaphore_signal(here_sem.at[1], inc=1, device_id=peer, device_id_type=MESH)

    for i in range(4):
        halos[i].wait_recv()
    for v in range(3):
        for side, start in ((0, SOUTH), (1, NORTH)):
            spread_rows(wrow_in[side][:, v * COLS:v * COLS + COLS], v, start, 1)
        for side, start in ((0, EAST), (1, WEST)):
            got = wcol_in[side]
            for r in range(ROWS):
                wx[v, r, :, start:start + 128] = jnp.broadcast_to(got[:, v * ROWS + r:v * ROWS + r + 1], (LEV, 128))

    for i in (6, 7):
        halos[i].wait_recv()

    def untuck(i, carry):
        for side, start, free, gap in ((0, EAST, 0, 2 * M), (1, WEST, 32, 0)):
            fourth = zero_tile
            for j in range(3):
                tile = lon_in[side, 3 * i + j]
                field[4 * i + j, :, start:start + 128] = tile
                shift = (free + 32 * j - gap) % 128
                moved = pltpu.roll(tile, shift, 1) if shift else tile
                here = (lane >= free + 32 * j) & (lane < free + 32 * j + 32)
                fourth = jnp.where(here, moved, fourth)
            field[4 * i + 3, :, start:start + 128] = fourth
        return carry

    lax.fori_loop(0, ROWS // 4, untuck, 0, unroll=True)

    def ends_first(r, carry):
        new = west_end(field, r, 0)
        mid[r, :, WEST:WEST + 128] = new[:, 0:128]
        mid[r, :, 0:128] = new[:, 128:256]
        mid[r, :, WIDTH - 128:WIDTH + 128] = east_end(field, r, 384)
        return carry

    lax.fori_loop(1, ROWS - 1, ends_first, 0, unroll=7)

    for i in (4, 5, 8, 9, 10, 11):
        halos[i].wait_recv()
    has_north, has_south = lat > 0, lat < n_lat - 1
    field[NORTH] = jnp.where(has_north, field[NORTH], 0.0)
    field[SOUTH] = jnp.where(has_south, field[SOUTH], 0.0)
    mid[0] = strip(field, 0, WIDE)
    mid[ROWS - 1] = strip(field, ROWS - 1, WIDE)
    mid[NORTH] = jnp.where(has_north, strip(field, NORTH, WIDE), 0.0)
    mid[SOUTH] = jnp.where(has_south, strip(field, SOUTH, WIDE), 0.0)

    for r in (0, 1, ROWS - 2, ROWS - 1):
        put(r, range(TILES), strip(mid, r, WIDE)[:, 0:WIDTH])

    def ends_second(r, carry):
        put(r, (0,), west_end(mid, r, 128))
        put(r, (TILES - 1,), east_end(mid, r, 256))
        return carry

    lax.fori_loop(2, ROWS - 2, ends_second, 0, unroll=6)


    for k, (cell, tile, shift) in enumerate(spots):
        line = jnp.concatenate([last[tile, pl.ds(cell, 1), :], last[tile + 1, pl.ds(cell, 1), :]], axis=1)
        seen[k:k + 1, :] = pltpu.roll(line, shift, 1)[:, 0:128]
    hx = seen[...]
    lane_o = lax.broadcasted_iota(jnp.int32, (OBS, 128), 1)
    hbar = jnp.sum(jnp.where(lane_o < M, hx, 0.0), axis=1, keepdims=True) * (1.0 / M)
    y = hx - hbar
    q = vals[0] / vals[1]
    d = vals[2] - hbar

    y0, y32, y48 = y, pltpu.roll(y, 32, 1), pltpu.roll(y, 48, 1)
    w0 = jnp.where(lane_o < 48, y0, jnp.where(lane_o == 96, d, 0.0))
    w1 = jnp.where((lane_o >= 48) & (lane_o < 80), y32, jnp.where(lane_o == 97, d, 0.0))
    w2 = jnp.where((lane_o >= 80) & (lane_o < 96), y48, jnp.where(lane_o == 98, d, 0.0))
    l1 = pltpu.roll(y, 128 - 16, 1)
    l2 = pltpu.roll(y, 128 - 32, 1)
    lhs = jnp.concatenate([q * y0, q * l1, q * l2], axis=0)
    rhs = jnp.concatenate([w0, w1, w2], axis=0)
    packed = lax.dot_general(lhs, rhs, (((0,), (0,)), ((), ())), precision=HP, preferred_element_type=F32)[0:16]
    pack[...] = packed.reshape(2, 8, 128)

    for j in plane_order:
        pltpu.make_async_remote_copy(
            src_ref=pack.at[lax.rem(lat + j // 2, 2)], dst_ref=part1.at[j - 1],
            send_sem=ar_send.at[0], recv_sem=ar_recv.at[0], device_id=plane_peer(j), device_id_type=MESH,
        ).start()

    for t in range(TILES):
        lanes = pl.ds(t % 3 * 128, 128)
        for lev in range(LEV + 1):
            part = last[t, pl.ds(lev, ROWS, stride=LEV), :] if lev < LEV else raw_flux[t]
            hi = part.astype(BF16)
            rows = pl.ds(t // 3 * 144 + lev * ROWS, ROWS)
            high[rows, lanes] = hi
            low[rows, lanes] = (part - hi.astype(F32)).astype(BF16)

    factors = [
        pltpu.make_async_copy(high, high_out, out_sem.at[0]), pltpu.make_async_copy(low, low_out, out_sem.at[1]),
    ]
    for copy in factors:
        copy.start()

    def wait_all(ref, sem):
        pltpu.make_async_copy(ref, ref, sem).wait()

    wait_all(part1, ar_recv.at[0])
    sum1[...] = pack[core] + jnp.sum(part1[...], axis=0)
    pl.semaphore_wait(here_sem.at[1], len(near_line))
    for j in line_order:
        pltpu.make_async_remote_copy(
            src_ref=sum1, dst_ref=part2.at[j - 1],
            send_sem=ar_send.at[1], recv_sem=ar_recv.at[1], device_id=line_peer(j), device_id_type=MESH,
        ).start()
    wait_all(part2, ar_recv.at[1])
    sum2[...] = sum1[...] + jnp.sum(part2[...], axis=0)
    swap = pltpu.make_async_remote_copy(
        src_ref=sum2, dst_ref=part3, send_sem=ar_send.at[2], recv_sem=ar_recv.at[2],
        device_id=partner, device_id_type=MESH,
    )
    swap.start()
    swap.wait_recv()
    mine, other = sum2[...], part3[...]
    total = jnp.concatenate([jnp.where(core == 0, mine, other), jnp.where(core == 0, other, mine)], axis=0)

    lane_p = lax.broadcasted_iota(jnp.int32, (16, 128), 1)
    u0 = jnp.where(lane_p < 48, total, 0.0)
    u1 = jnp.where((lane_p >= 16) & (lane_p < 48), pltpu.roll(total, 128 - 32, 1), 0.0)
    u2 = jnp.where((lane_p >= 32) & (lane_p < 48), pltpu.roll(total, 128 - 48, 1), 0.0)
    upper = jnp.concatenate([u0, u1, u2, jnp.zeros((80, 128), F32)], axis=0)
    flipped = upper.T
    row_s = lax.broadcasted_iota(jnp.int32, (M, M), 0)
    col_s = lax.broadcasted_iota(jnp.int32, (M, M), 1)
    gram = jnp.where(row_s // 16 > col_s // 16, flipped[0:M, 0:M], upper[0:M, 0:M])
    proj = jnp.concatenate([total[:, 96:97], total[:, 97:98], total[:, 98:99]], axis=0)
    eye = jnp.where(row_s == col_s, 1.0, 0.0)

    def dot(a, b):
        return jnp.dot(a, b, precision=HP, preferred_element_type=F32)

    system = (M - 1.0) * eye + gram
    square = dot(system, system)
    norm2 = jnp.sum(system * system, keepdims=True)
    scale = jnp.sqrt(norm2)
    root_now = system / scale
    factor = 0.5 * (3.0 * eye - root_now)
    root_now, inverse_now = 1.5 * root_now - 0.5 * (square / norm2), factor
    for step in range(1, NS_ITERS):
        factor = 0.5 * (3.0 * eye - dot(inverse_now, root_now))
        if step < NS_ITERS - 1:
            root_now = dot(root_now, factor)
        inverse_now = dot(factor, inverse_now)
    inner = jnp.sum(inverse_now * proj, axis=0, keepdims=True)
    wmean = jnp.sum(inverse_now * inner, axis=1, keepdims=True) / scale
    mixed = wmean + jnp.sqrt((M - 1.0) / scale) * inverse_now
    mixing = mixed - jnp.sum(mixed, axis=0, keepdims=True) * (1.0 / M) + 1.0 / M

    mix[...] = mixing
    result = pltpu.make_async_copy(mix, mix_out, out_sem.at[2])
    result.start()
    for copy in halos:
        copy.wait_send()
    wait_all(part1, ar_send.at[0])
    wait_all(part2, ar_send.at[1])
    swap.wait_send()
    for copy in factors:
        copy.wait()
    result.wait()


def transform(high_in, low_in, mix_in, tracer_out, flux_out, high, low, mix, outs, in_sem, out_sem):
    mix_copy = pltpu.make_async_copy(mix_in, mix, in_sem.at[6])
    mix_copy.start()
    copies = []
    for g in range(3):
        rows = pl.ds(g * 144, 144)
        copies.append(pltpu.make_async_copy(high_in.at[rows], high.at[rows], in_sem.at[2 * g]))
        copies.append(pltpu.make_async_copy(low_in.at[rows], low.at[rows], in_sem.at[2 * g + 1]))
    for copy in copies:
        copy.start()

    rep_row = lax.broadcasted_iota(jnp.int32, (M, GROUP), 0)
    rep_lane = lax.broadcasted_iota(jnp.int32, (M, GROUP), 1)
    rep = jnp.where(lax.rem(rep_lane, M) == rep_row, 1.0, 0.0).astype(BF16)
    mix_copy.wait()
    mixing = mix[...]
    g_high = mixing.astype(BF16)
    g_low = (mixing - g_high.astype(F32)).astype(BF16)
    g_high = jnp.dot(g_high, rep, preferred_element_type=F32)
    g_low = jnp.dot(g_low, rep, preferred_element_type=F32)

    def diagonal(g):
        return jnp.concatenate(
            [jnp.where((rep_lane >= b * M) & (rep_lane < b * M + M), g, 0.0).astype(BF16) for b in range(8)], axis=0
        )

    d_high, d_low = diagonal(g_high), diagonal(g_low)
    done = []
    for copy in copies:
        copy.wait()
    for n, (k0, k1) in enumerate(((0, 256), (0, 384), (128, 384))):
        cols = slice(n * 128, n * 128 + 128)
        w_h, w_l = d_high[k0:k1, cols], d_low[k0:k1, cols]
        w = jnp.concatenate([w_h, w_l], axis=1)
        both = jnp.dot(high[:, k0:k1], w, preferred_element_type=F32)
        res = both[:, 0:128] + both[:, 128:256] + jnp.dot(low[:, k0:k1], w_h, preferred_element_type=F32)
        for g in range(3):
            outs[g * 3 + n] = res[g * 144:(g + 1) * 144]
        for t in range(n, TILES, 3):
            lanes = pl.ds(t * 128, 128)
            done.append(pltpu.make_async_copy(outs.at[t, pl.ds(0, LEV * ROWS)], tracer_out.at[:, lanes], out_sem.at[t]))
            done.append(
                pltpu.make_async_copy(outs.at[t, pl.ds(LEV * ROWS, ROWS)], flux_out.at[:, lanes], out_sem.at[TILES + t])
            )
        for copy in done[-6:]:
            copy.start()
    for copy in done:
        copy.wait()


def on_device(n_lat, n_lon, tracer, flux, winds, obs_cells, obs_count, obs_value, obs_var):
    hbm = pl.BlockSpec(memory_space=pltpu.HBM)
    n_plane, n_line = 2 * n_lat, n_lon // 2
    vmem = pltpu.VMEM
    high, low, mixing = pl.pallas_call(
        functools.partial(kernel, n_lat, n_lon),
        out_shape=(
            jax.ShapeDtypeStruct((432, GROUP), BF16),
            jax.ShapeDtypeStruct((432, GROUP), BF16),
            jax.ShapeDtypeStruct((M, M), F32),
        ),
        in_specs=[hbm] * 7,
        out_specs=(hbm, hbm, hbm),
        scratch_shapes=[
            vmem((TILES, LEV * ROWS, 128), F32),
            vmem((TILES, ROWS, 128), F32),
            vmem((3 * LEV * ROWS, COLS), F32),
            vmem((3 * LEV * ROWS, 128), F32),
            vmem((ROWS_X, LEV, WIDE), F32),
            vmem((ROWS_X, LEV, WIDE), F32),
            vmem((TILES, LEV * ROWS, 128), F32),
            vmem((3, ROWS, LEV, 128), F32),
            vmem((3, ROWS_X, LEV, WIDE), F32),
            vmem((2, LEV, 128), F32),
            vmem((2, LEV, 128), F32),
            vmem((2, LEV, 128), F32),
            vmem((2, LEV, 128), F32),
            vmem((2, 12, LEV, 128), F32),
            vmem((2, 12, LEV, 128), F32),
            vmem((OBS, 128), F32),
            vmem((3, OBS, 128), F32),
            vmem((2, 8, 128), F32),
            vmem((n_plane - 1, 8, 128), F32),
            vmem((n_line - 1, 8, 128), F32),
            vmem((8, 128), F32),
            vmem((8, 128), F32),
            vmem((8, 128), F32),
            vmem((432, GROUP), BF16),
            vmem((432, GROUP), BF16),
            vmem((M, M), F32),
            pltpu.SMEM((3, OBS), jnp.int32),
            pltpu.SMEM((1,), jnp.int32),
            pltpu.SMEM((OBS,), F32),
            pltpu.SMEM((OBS,), F32),
            pltpu.SemaphoreType.DMA((5 + 2 * TILES,)),
            pltpu.SemaphoreType.DMA((3,)),
            pltpu.SemaphoreType.DMA((12,)),
            pltpu.SemaphoreType.DMA((12,)),
            pltpu.SemaphoreType.DMA((3,)),
            pltpu.SemaphoreType.DMA((3,)),
            pltpu.SemaphoreType.REGULAR((2,)),
        ],
        compiler_params=pltpu.CompilerParams(
            collective_id=0, has_side_effects=True, vmem_limit_bytes=62 * 1024 * 1024
        ),
        name="analysis",
    )(
        tracer.reshape(LEV * ROWS, WIDTH), flux, winds.reshape(3 * LEV * ROWS, COLS),
        obs_cells.T, obs_count, obs_value, obs_var,
    )
    tracer_out, flux_out = pl.pallas_call(
        transform,
        out_shape=(
            jax.ShapeDtypeStruct((LEV * ROWS, WIDTH), F32),
            jax.ShapeDtypeStruct((ROWS, WIDTH), F32),
        ),
        in_specs=[hbm] * 3,
        out_specs=(hbm, hbm),
        scratch_shapes=[
            vmem((432, GROUP), BF16),
            vmem((432, GROUP), BF16),
            vmem((M, M), F32),
            vmem((TILES, 144, 128), F32),
            pltpu.SemaphoreType.DMA((7,)),
            pltpu.SemaphoreType.DMA((2 * TILES,)),
        ],
        compiler_params=pltpu.CompilerParams(vmem_limit_bytes=62 * 1024 * 1024),
        name="transform",
    )(high, low, mixing)
    return tracer_out.reshape(LEV, ROWS, WIDTH), flux_out


def solution(mesh):
    return jax.shard_map(
        functools.partial(on_device, mesh.shape["lat"], mesh.shape["lon"]),
        mesh=mesh,
        in_specs=(
            P(None, "lat", "lon"),
            P("lat", "lon"),
            P(None, None, "lat", "lon"),
            P(("lat", "lon"), None),
            P(("lat", "lon")),
            P(("lat", "lon")),
            P(("lat", "lon")),
        ),
        out_specs=(P(None, "lat", "lon"), P("lat", "lon")),
        check_vma=False,
    )
```

```python
import functools

import jax
import jax.numpy as jnp
from jax import lax
from jax.experimental import pallas as pl
from jax.experimental.pallas import tpu as pltpu
from jax.sharding import PartitionSpec as P

M = 48
NS_ITERS = 5
KH = 0.15
MESH = pl.DeviceIdType.MESH
HP = lax.Precision.HIGHEST
F32 = jnp.float32
BF16 = jnp.bfloat16

LEV, ROWS, COLS, OBS = 8, 16, 24, 16
TILES = 9
WIDTH = COLS * M
WIDE = WIDTH + 256
EAST, WEST = WIDTH, WIDTH + 128
ROWS_X = ROWS + 4
SOUTH, NORTH = ROWS, ROWS + 3
GROUP = 8 * M


def kernel(
    n_lat, n_lon,
    tracer, flux, winds, cells_in, count_in, value_in, var_in,
    high_out, low_out, mix_out,
    raw, raw_flux, raw_winds, wide_winds, field, mid, last, wc, wx, wcol_out, wcol_in,
    wrow_out, wrow_in, lon_out, lon_in, seen, vals, pack, part1, part2, part3, sum1, sum2, high, low, mix,
    cells, count, value, var, in_sem, out_sem, halo_send, halo_recv, ar_send, ar_recv, here_sem,
):
    lat, lon = lax.axis_index("lat"), lax.axis_index("lon")

    def at(dlat, dlon):
        return (lax.rem(lat + (dlat + n_lat), n_lat), lax.rem(lon + (dlon + n_lon), n_lon))

    sides = [(1, 0), (-1, 0), (0, 1), (0, -1), (1, 1), (1, -1), (-1, 1), (-1, -1)]
    pair = lax.rem(lon, 2)
    base = lon - pair

    def plane_peer(j):
        return (lax.rem(lat + j // 2, n_lat), base + lax.rem(pair + j, 2))

    def line_peer(j):
        return (lat, lax.rem(lon + 2 * j, n_lon))

    core = lax.rem(lat, 2)
    partner = (lat + 1 - 2 * core, lon)
    n_plane, n_line = 2 * n_lat, n_lon // 2

    n_x = n_lat // 4
    x, y = lat // 4, lax.rem(lat // 2, 2) * 2 + pair

    def plane_near(dx, dy, dc):
        to_x, to_y = lax.rem(x + (dx + n_x), n_x), lax.rem(y + (dy + 4), 4)
        return (to_x * 4 + to_y // 2 * 2 + lax.rem(core + dc, 2), base + lax.rem(to_y, 2))

    near_plane = [
        plane_near(dx, dy, dc) for dx in (-1, 1, 0) for dy in (-1, 1, 0) for dc in (1, 0) if (dx, dy, dc) != (0, 0, 0)
    ]
    near_line = [line_peer(k % n_line) for k in (3, -3, 2, -2)]
    near_halo = [at(dlat, dlon) for dlat, dlon in sides]
    plane_order = sorted(range(1, n_plane), key=lambda j: -min(j // 2, n_lat - j // 2))
    line_order = sorted(range(1, n_line), key=lambda j: -min(j, n_line - j))
    barrier = pltpu.get_barrier_semaphore()
    for peer in near_halo + near_line + near_plane:
        pl.semaphore_signal(barrier, inc=1, device_id=peer, device_id_type=MESH)

    copies = [
        pltpu.make_async_copy(winds, raw_winds, in_sem.at[0]),
    ]
    for t in range(TILES):
        lanes = pl.ds(t * 128, 128)
        copies.append(pltpu.make_async_copy(tracer.at[:, lanes], raw.at[t], in_sem.at[1 + t]))
        copies.append(pltpu.make_async_copy(flux.at[:, lanes], raw_flux.at[t], in_sem.at[1 + TILES + t]))
    obs_copies = [
        pltpu.make_async_copy(src, dst, in_sem.at[1 + 2 * TILES + i])
        for i, (src, dst) in enumerate(((cells_in, cells), (count_in, count), (value_in, value), (var_in, var)))
    ]
    for copy in copies + obs_copies:
        copy.start()

    for copy in copies:
        copy.wait()
    level = lax.broadcasted_iota(jnp.int32, (LEV, 1), 0)
    wide_winds[:, 0:COLS] = 0.5 * raw_winds[...]

    def enter(r, carry):
        for t in range(TILES):
            own = raw[t, pl.ds(r, LEV, stride=ROWS), :]
            surface = raw_flux[t, pl.ds(r, 1), :]
            field[r, :, t * 128:t * 128 + 128] = own + jnp.where(level == 0, surface, 0.0)
        for v in range(3):
            wc[v, r] = wide_winds[pl.ds(v * LEV * ROWS + r, LEV, stride=ROWS), :]
        return carry

    lax.fori_loop(0, ROWS, enter, 0, unroll=8)

    lane = lax.broadcasted_iota(jnp.int32, (LEV, 128), 1)

    def edge(r, carry):
        first, final = carry
        for v in range(3):
            w = wc[v, r]
            here = lane == v * ROWS + r
            first = jnp.where(here, w[:, 0:1], first)
            final = jnp.where(here, w[:, COLS - 1:COLS], final)
        return first, final

    zero_tile = jnp.zeros((LEV, 128), F32)
    first, final = lax.fori_loop(0, ROWS, edge, (zero_tile, zero_tile), unroll=True)
    wcol_out[0] = first
    wcol_out[1] = final
    for side, r in ((0, 0), (1, ROWS - 1)):
        packed_row = jnp.where(lane < COLS, wc[0, r], 0.0)
        for v in (1, 2):
            here = (lane >= v * COLS) & (lane < v * COLS + COLS)
            packed_row = jnp.where(here, pltpu.roll(wc[v, r], v * COLS, 1), packed_row)
        wrow_out[side] = packed_row

    def tuck(i, carry):
        for side, start, free, gap in ((0, 0, 0, 2 * M), (1, WIDTH - 128, 32, 0)):
            fourth = field[4 * i + 3, :, start:start + 128]
            for j in range(3):
                shift = (gap - free - 32 * j) % 128
                moved = pltpu.roll(fourth, shift, 1) if shift else fourth
                here = (lane >= gap) & (lane < gap + 32)
                lon_out[side, 3 * i + j] = jnp.where(here, moved, field[4 * i + j, :, start:start + 128])
        return carry

    lax.fori_loop(0, ROWS // 4, tuck, 0, unroll=True)

    pl.semaphore_wait(barrier, len(near_halo + near_line + near_plane))

    def send(i, src, dst, to):
        return pltpu.make_async_remote_copy(
            src_ref=src, dst_ref=dst, send_sem=halo_send.at[i], recv_sem=halo_recv.at[i],
            device_id=to, device_id_type=MESH,
        )

    own_lanes = pl.ds(0, WIDTH)
    left_tile, right_tile = pl.ds(0, 128), pl.ds(WIDTH - 128, 128)
    east_tile, west_tile = pl.ds(EAST, 128), pl.ds(WEST, 128)
    top, bottom = 0, ROWS - 1
    halos = [
        send(0, wcol_out.at[0], wcol_in.at[0], at(0, -1)),
        send(1, wcol_out.at[1], wcol_in.at[1], at(0, 1)),
        send(2, wrow_out.at[0], wrow_in.at[0], at(-1, 0)),
        send(3, wrow_out.at[1], wrow_in.at[1], at(1, 0)),
        send(4, field.at[pl.ds(top, 2), :, own_lanes], field.at[pl.ds(SOUTH, 2), :, own_lanes], at(-1, 0)),
        send(5, field.at[pl.ds(bottom - 1, 2), :, own_lanes], field.at[pl.ds(NORTH - 1, 2), :, own_lanes], at(1, 0)),
        send(6, lon_out.at[0], lon_in.at[0], at(0, -1)),
        send(7, lon_out.at[1], lon_in.at[1], at(0, 1)),
        send(8, field.at[top, :, left_tile], field.at[SOUTH, :, east_tile], at(-1, -1)),
        send(9, field.at[top, :, right_tile], field.at[SOUTH, :, west_tile], at(-1, 1)),
        send(10, field.at[bottom, :, left_tile], field.at[NORTH, :, east_tile], at(1, -1)),
        send(11, field.at[bottom, :, right_tile], field.at[NORTH, :, west_tile], at(1, 1)),
    ]
    for copy in halos:
        copy.start()
    for peer in near_line + near_plane:
        pl.semaphore_signal(here_sem.at[0], inc=1, device_id=peer, device_id_type=MESH)

    spread_col = lax.broadcasted_iota(jnp.int32, (COLS, WIDTH), 0)
    spread_lane = lax.broadcasted_iota(jnp.int32, (COLS, WIDTH), 1)
    spread = jnp.where((spread_lane >= spread_col * M) & (spread_lane < spread_col * M + M), 1.0, 0.0).astype(BF16)

    def spread_rows(w, v, start, rows):
        a = w.astype(BF16)
        rest = w - a.astype(F32)
        b = rest.astype(BF16)
        c = (rest - b.astype(F32)).astype(BF16)
        wide = (
            jnp.dot(a, spread, preferred_element_type=F32)
            + jnp.dot(b, spread, preferred_element_type=F32)
            + jnp.dot(c, spread, preferred_element_type=F32)
        )
        wx[v, pl.ds(start, rows), :, 0:WIDTH] = wide.reshape(rows, LEV, WIDTH)

    for v in range(3):
        spread_rows(wc[v, :, :, 0:COLS].reshape(ROWS * LEV, COLS), v, 0, ROWS)

    def stencil(c, n, s, u, v, w, first, final):
        width = c.shape[1]
        keep = slice(first, final)
        east, west = pltpu.roll(c, width - M, 1)[:, keep], pltpu.roll(c, M, 1)[:, keep]
        c = c[:, keep]
        above = jnp.where(level == LEV - 1, 0.0, pltpu.roll(c, LEV - 1, 0))
        below = jnp.where(level == 0, 0.0, pltpu.roll(c, 1, 0))
        spread_out = (east + west) + (s + n) + (above + below)
        carried = u * (east - west) + v * (s - n) + w * (above - below)
        return (1.0 - 6.0 * KH) * c + KH * spread_out - carried

    def strip(src, r, width):
        n, s = lax.rem(r + ROWS_X - 1, ROWS_X), lax.rem(r + 1, ROWS_X)
        return stencil(
            src[r, :, 0:width], src[n, :, 0:width], src[s, :, 0:width],
            wx[0, r, :, 0:width], wx[1, r, :, 0:width], wx[2, r, :, 0:width], 0, width,
        )

    def west_end(src, r, first):
        def of(ref, i):
            return jnp.concatenate([ref[i, :, WEST:WEST + 128], ref[i, :, 0:128]], axis=1)[:, first:]

        c = jnp.concatenate([src[r, :, WEST:WEST + 128], src[r, :, 0:256]], axis=1)
        return stencil(
            c, of(src, r - 1), of(src, r + 1), of(wx.at[0], r), of(wx.at[1], r), of(wx.at[2], r), first, 256
        )

    def east_end(src, r, final):
        lanes = slice(WIDTH - 128, WIDTH - 256 + final)
        return stencil(
            src[r, :, WIDTH - 256:WIDTH + 128], src[r - 1, :, lanes], src[r + 1, :, lanes],
            wx[0, r, :, lanes], wx[1, r, :, lanes], wx[2, r, :, lanes], 128, final,
        )

    def put(r, tiles, value):
        for i, t in enumerate(tiles):
            last[t, pl.ds(pl.multiple_of(r * LEV, LEV), LEV), :] = value[:, i * 128:i * 128 + 128]

    def inner_first(r, carry):
        mid[r, :, 0:WIDTH] = strip(field, r, WIDTH)
        return carry

    lax.fori_loop(1, ROWS - 1, inner_first, 0, unroll=2)

    def inner_second(r, carry):
        put(r, range(1, TILES - 1), strip(mid, r, WIDTH)[:, 128:WIDTH - 128])
        return carry

    lax.fori_loop(2, ROWS - 2, inner_second, 0, unroll=2)

    for copy in obs_copies:
        copy.wait()

    def note(k, carry):
        live = jnp.where(k < count[0], 1.0, 0.0)
        vals[0, pl.ds(k, 1), :] = jnp.full((1, 128), live, F32)
        vals[1, pl.ds(k, 1), :] = jnp.full((1, 128), var[k], F32)
        vals[2, pl.ds(k, 1), :] = jnp.full((1, 128), value[k], F32)
        return carry

    lax.fori_loop(0, OBS, note, 0)
    spots = []
    for k in range(OBS):
        row, first_lane, lev = cells[0, k] - lat * ROWS, (cells[1, k] - lon * COLS) * M, cells[2, k]
        tile = jnp.clip(first_lane // 128, 0, TILES - 2)
        spots.append((jnp.clip(row * LEV + lev, 0, LEV * ROWS - 1), tile, (256 - first_lane + tile * 128) & 255))

    pl.semaphore_wait(here_sem.at[0], len(near_line + near_plane))
    for peer in near_line:
        pl.semaphore_signal(here_sem.at[1], inc=1, device_id=peer, device_id_type=MESH)

    for i in range(4):
        halos[i].wait_recv()
    for v in range(3):
        for side, start in ((0, SOUTH), (1, NORTH)):
            spread_rows(wrow_in[side][:, v * COLS:v * COLS + COLS], v, start, 1)
        for side, start in ((0, EAST), (1, WEST)):
            got = wcol_in[side]
            for r in range(ROWS):
                wx[v, r, :, start:start + 128] = jnp.broadcast_to(got[:, v * ROWS + r:v * ROWS + r + 1], (LEV, 128))

    for i in (6, 7):
        halos[i].wait_recv()

    def untuck(i, carry):
        for side, start, free, gap in ((0, EAST, 0, 2 * M), (1, WEST, 32, 0)):
            fourth = zero_tile
            for j in range(3):
                tile = lon_in[side, 3 * i + j]
                field[4 * i + j, :, start:start + 128] = tile
                shift = (free + 32 * j - gap) % 128
                moved = pltpu.roll(tile, shift, 1) if shift else tile
                here = (lane >= free + 32 * j) & (lane < free + 32 * j + 32)
                fourth = jnp.where(here, moved, fourth)
            field[4 * i + 3, :, start:start + 128] = fourth
        return carry

    lax.fori_loop(0, ROWS // 4, untuck, 0, unroll=True)

    def ends_first(r, carry):
        new = west_end(field, r, 0)
        mid[r, :, WEST:WEST + 128] = new[:, 0:128]
        mid[r, :, 0:128] = new[:, 128:256]
        mid[r, :, WIDTH - 128:WIDTH + 128] = east_end(field, r, 384)
        return carry

    lax.fori_loop(1, ROWS - 1, ends_first, 0, unroll=7)

    for i in (4, 5, 8, 9, 10, 11):
        halos[i].wait_recv()
    has_north, has_south = lat > 0, lat < n_lat - 1
    field[NORTH] = jnp.where(has_north, field[NORTH], 0.0)
    field[SOUTH] = jnp.where(has_south, field[SOUTH], 0.0)
    mid[0] = strip(field, 0, WIDE)
    mid[ROWS - 1] = strip(field, ROWS - 1, WIDE)
    mid[NORTH] = jnp.where(has_north, strip(field, NORTH, WIDE), 0.0)
    mid[SOUTH] = jnp.where(has_south, strip(field, SOUTH, WIDE), 0.0)

    for r in (0, 1, ROWS - 2, ROWS - 1):
        put(r, range(TILES), strip(mid, r, WIDE)[:, 0:WIDTH])

    def ends_second(r, carry):
        put(r, (0,), west_end(mid, r, 128))
        put(r, (TILES - 1,), east_end(mid, r, 256))
        return carry

    lax.fori_loop(2, ROWS - 2, ends_second, 0, unroll=6)


    for k, (cell, tile, shift) in enumerate(spots):
        line = jnp.concatenate([last[tile, pl.ds(cell, 1), :], last[tile + 1, pl.ds(cell, 1), :]], axis=1)
        seen[k:k + 1, :] = pltpu.roll(line, shift, 1)[:, 0:128]
    hx = seen[...]
    lane_o = lax.broadcasted_iota(jnp.int32, (OBS, 128), 1)
    hbar = jnp.sum(jnp.where(lane_o < M, hx, 0.0), axis=1, keepdims=True) * (1.0 / M)
    y = hx - hbar
    q = vals[0] / vals[1]
    d = vals[2] - hbar

    y0, y32, y48 = y, pltpu.roll(y, 32, 1), pltpu.roll(y, 48, 1)
    w0 = jnp.where(lane_o < 48, y0, jnp.where(lane_o == 96, d, 0.0))
    w1 = jnp.where((lane_o >= 48) & (lane_o < 80), y32, jnp.where(lane_o == 97, d, 0.0))
    w2 = jnp.where((lane_o >= 80) & (lane_o < 96), y48, jnp.where(lane_o == 98, d, 0.0))
    l1 = pltpu.roll(y, 128 - 16, 1)
    l2 = pltpu.roll(y, 128 - 32, 1)
    lhs = jnp.concatenate([q * y0, q * l1, q * l2], axis=0)
    rhs = jnp.concatenate([w0, w1, w2], axis=0)
    packed = lax.dot_general(lhs, rhs, (((0,), (0,)), ((), ())), precision=HP, preferred_element_type=F32)[0:16]
    pack[...] = packed.reshape(2, 8, 128)

    for j in plane_order:
        pltpu.make_async_remote_copy(
            src_ref=pack.at[lax.rem(lat + j // 2, 2)], dst_ref=part1.at[j - 1],
            send_sem=ar_send.at[0], recv_sem=ar_recv.at[0], device_id=plane_peer(j), device_id_type=MESH,
        ).start()

    for t in range(TILES):
        lanes = pl.ds(t % 3 * 128, 128)
        for lev in range(LEV + 1):
            part = last[t, pl.ds(lev, ROWS, stride=LEV), :] if lev < LEV else raw_flux[t]
            hi = part.astype(BF16)
            rows = pl.ds(t // 3 * 144 + lev * ROWS, ROWS)
            high[rows, lanes] = hi
            low[rows, lanes] = (part - hi.astype(F32)).astype(BF16)

    factors = [
        pltpu.make_async_copy(high, high_out, out_sem.at[0]), pltpu.make_async_copy(low, low_out, out_sem.at[1]),
    ]
    for copy in factors:
        copy.start()

    def wait_all(ref, sem):
        pltpu.make_async_copy(ref, ref, sem).wait()

    wait_all(part1, ar_recv.at[0])
    sum1[...] = pack[core] + jnp.sum(part1[...], axis=0)
    pl.semaphore_wait(here_sem.at[1], len(near_line))
    for j in line_order:
        pltpu.make_async_remote_copy(
            src_ref=sum1, dst_ref=part2.at[j - 1],
            send_sem=ar_send.at[1], recv_sem=ar_recv.at[1], device_id=line_peer(j), device_id_type=MESH,
        ).start()
    wait_all(part2, ar_recv.at[1])
    sum2[...] = sum1[...] + jnp.sum(part2[...], axis=0)
    swap = pltpu.make_async_remote_copy(
        src_ref=sum2, dst_ref=part3, send_sem=ar_send.at[2], recv_sem=ar_recv.at[2],
        device_id=partner, device_id_type=MESH,
    )
    swap.start()
    swap.wait_recv()
    mine, other = sum2[...], part3[...]
    total = jnp.concatenate([jnp.where(core == 0, mine, other), jnp.where(core == 0, other, mine)], axis=0)

    lane_p = lax.broadcasted_iota(jnp.int32, (16, 128), 1)
    u0 = jnp.where(lane_p < 48, total, 0.0)
    u1 = jnp.where((lane_p >= 16) & (lane_p < 48), pltpu.roll(total, 128 - 32, 1), 0.0)
    u2 = jnp.where((lane_p >= 32) & (lane_p < 48), pltpu.roll(total, 128 - 48, 1), 0.0)
    flipped = total.T
    row_s = lax.broadcasted_iota(jnp.int32, (M, M), 0)
    col_s = lax.broadcasted_iota(jnp.int32, (M, M), 1)
    upper = jnp.concatenate([u0, u1, u2], axis=0)[:, 0:M]
    corner = jnp.concatenate([flipped[32:48], flipped[64:80]], axis=1)
    lower = jnp.concatenate(
        [
            jnp.zeros((16, M), F32),
            jnp.concatenate([flipped[16:32], jnp.zeros((16, 32), F32)], axis=1),
            jnp.concatenate([corner, jnp.zeros((16, 16), F32)], axis=1),
        ],
        axis=0,
    )
    gram = upper + lower
    proj = jnp.concatenate([total[:, 96:97], total[:, 97:98], total[:, 98:99]], axis=0)
    eye = jnp.where(row_s == col_s, 1.0, 0.0)

    def dot(a, b):
        return jnp.dot(a, b, precision=HP, preferred_element_type=F32)

    system = (M - 1.0) * eye + gram
    square = dot(system, system)
    norm2 = jnp.sum(system * system, keepdims=True)
    scale = jnp.sqrt(norm2)
    root_now = system / scale
    factor = 0.5 * (3.0 * eye - root_now)
    root_now, inverse_now = 1.5 * root_now - 0.5 * (square / norm2), factor
    for step in range(1, NS_ITERS):
        factor = 0.5 * (3.0 * eye - dot(inverse_now, root_now))
        if step < NS_ITERS - 1:
            root_now = dot(root_now, factor)
        inverse_now = dot(factor, inverse_now)
    inner = jnp.sum(inverse_now * proj, axis=0, keepdims=True)
    wmean = jnp.sum(inverse_now * inner, axis=1, keepdims=True) / scale
    mixed = wmean + jnp.sqrt((M - 1.0) / scale) * inverse_now
    mixing = mixed - jnp.sum(mixed, axis=0, keepdims=True) * (1.0 / M) + 1.0 / M

    mix[...] = mixing
    result = pltpu.make_async_copy(mix, mix_out, out_sem.at[2])
    result.start()
    for copy in halos:
        copy.wait_send()
    wait_all(part1, ar_send.at[0])
    wait_all(part2, ar_send.at[1])
    swap.wait_send()
    for copy in factors:
        copy.wait()
    result.wait()


def transform(high_in, low_in, mix_in, tracer_out, flux_out, high, low, mix, outs, in_sem, out_sem):
    mix_copy = pltpu.make_async_copy(mix_in, mix, in_sem.at[6])
    mix_copy.start()
    copies = []
    for g in range(3):
        rows = pl.ds(g * 144, 144)
        copies.append(pltpu.make_async_copy(high_in.at[rows], high.at[rows], in_sem.at[2 * g]))
        copies.append(pltpu.make_async_copy(low_in.at[rows], low.at[rows], in_sem.at[2 * g + 1]))
    for copy in copies:
        copy.start()

    rep_row = lax.broadcasted_iota(jnp.int32, (M, GROUP), 0)
    rep_lane = lax.broadcasted_iota(jnp.int32, (M, GROUP), 1)
    rep = jnp.where(lax.rem(rep_lane, M) == rep_row, 1.0, 0.0).astype(BF16)
    mix_copy.wait()
    mixing = mix[...]
    g_high = mixing.astype(BF16)
    g_low = (mixing - g_high.astype(F32)).astype(BF16)
    g_high = jnp.dot(g_high, rep, preferred_element_type=F32)
    g_low = jnp.dot(g_low, rep, preferred_element_type=F32)

    def diagonal(g):
        return jnp.concatenate(
            [jnp.where((rep_lane >= b * M) & (rep_lane < b * M + M), g, 0.0).astype(BF16) for b in range(8)], axis=0
        )

    d_high, d_low = diagonal(g_high), diagonal(g_low)
    done = []
    for copy in copies:
        copy.wait()
    for n, (k0, k1) in enumerate(((0, 256), (0, 384), (128, 384))):
        cols = slice(n * 128, n * 128 + 128)
        w_h, w_l = d_high[k0:k1, cols], d_low[k0:k1, cols]
        w = jnp.concatenate([w_h, w_l], axis=1)
        both = jnp.dot(high[:, k0:k1], w, preferred_element_type=F32)
        res = both[:, 0:128] + both[:, 128:256] + jnp.dot(low[:, k0:k1], w_h, preferred_element_type=F32)
        for g in range(3):
            outs[g * 3 + n] = res[g * 144:(g + 1) * 144]
        for t in range(n, TILES, 3):
            lanes = pl.ds(t * 128, 128)
            done.append(pltpu.make_async_copy(outs.at[t, pl.ds(0, LEV * ROWS)], tracer_out.at[:, lanes], out_sem.at[t]))
            done.append(
                pltpu.make_async_copy(outs.at[t, pl.ds(LEV * ROWS, ROWS)], flux_out.at[:, lanes], out_sem.at[TILES + t])
            )
        for copy in done[-6:]:
            copy.start()
    for copy in done:
        copy.wait()


def on_device(n_lat, n_lon, tracer, flux, winds, obs_cells, obs_count, obs_value, obs_var):
    hbm = pl.BlockSpec(memory_space=pltpu.HBM)
    n_plane, n_line = 2 * n_lat, n_lon // 2
    vmem = pltpu.VMEM
    high, low, mixing = pl.pallas_call(
        functools.partial(kernel, n_lat, n_lon),
        out_shape=(
            jax.ShapeDtypeStruct((432, GROUP), BF16),
            jax.ShapeDtypeStruct((432, GROUP), BF16),
            jax.ShapeDtypeStruct((M, M), F32),
        ),
        in_specs=[hbm] * 7,
        out_specs=(hbm, hbm, hbm),
        scratch_shapes=[
            vmem((TILES, LEV * ROWS, 128), F32),
            vmem((TILES, ROWS, 128), F32),
            vmem((3 * LEV * ROWS, COLS), F32),
            vmem((3 * LEV * ROWS, 128), F32),
            vmem((ROWS_X, LEV, WIDE), F32),
            vmem((ROWS_X, LEV, WIDE), F32),
            vmem((TILES, LEV * ROWS, 128), F32),
            vmem((3, ROWS, LEV, 128), F32),
            vmem((3, ROWS_X, LEV, WIDE), F32),
            vmem((2, LEV, 128), F32),
            vmem((2, LEV, 128), F32),
            vmem((2, LEV, 128), F32),
            vmem((2, LEV, 128), F32),
            vmem((2, 12, LEV, 128), F32),
            vmem((2, 12, LEV, 128), F32),
            vmem((OBS, 128), F32),
            vmem((3, OBS, 128), F32),
            vmem((2, 8, 128), F32),
            vmem((n_plane - 1, 8, 128), F32),
            vmem((n_line - 1, 8, 128), F32),
            vmem((8, 128), F32),
            vmem((8, 128), F32),
            vmem((8, 128), F32),
            vmem((432, GROUP), BF16),
            vmem((432, GROUP), BF16),
            vmem((M, M), F32),
            pltpu.SMEM((3, OBS), jnp.int32),
            pltpu.SMEM((1,), jnp.int32),
            pltpu.SMEM((OBS,), F32),
            pltpu.SMEM((OBS,), F32),
            pltpu.SemaphoreType.DMA((5 + 2 * TILES,)),
            pltpu.SemaphoreType.DMA((3,)),
            pltpu.SemaphoreType.DMA((12,)),
            pltpu.SemaphoreType.DMA((12,)),
            pltpu.SemaphoreType.DMA((3,)),
            pltpu.SemaphoreType.DMA((3,)),
            pltpu.SemaphoreType.REGULAR((2,)),
        ],
        compiler_params=pltpu.CompilerParams(
            collective_id=0, has_side_effects=True, vmem_limit_bytes=62 * 1024 * 1024
        ),
        name="analysis",
    )(
        tracer.reshape(LEV * ROWS, WIDTH), flux, winds.reshape(3 * LEV * ROWS, COLS),
        obs_cells.T, obs_count, obs_value, obs_var,
    )
    tracer_out, flux_out = pl.pallas_call(
        transform,
        out_shape=(
            jax.ShapeDtypeStruct((LEV * ROWS, WIDTH), F32),
            jax.ShapeDtypeStruct((ROWS, WIDTH), F32),
        ),
        in_specs=[hbm] * 3,
        out_specs=(hbm, hbm),
        scratch_shapes=[
            vmem((432, GROUP), BF16),
            vmem((432, GROUP), BF16),
            vmem((M, M), F32),
            vmem((TILES, 144, 128), F32),
            pltpu.SemaphoreType.DMA((7,)),
            pltpu.SemaphoreType.DMA((2 * TILES,)),
        ],
        compiler_params=pltpu.CompilerParams(vmem_limit_bytes=62 * 1024 * 1024),
        name="transform",
    )(high, low, mixing)
    return tracer_out.reshape(LEV, ROWS, WIDTH), flux_out


def solution(mesh):
    return jax.shard_map(
        functools.partial(on_device, mesh.shape["lat"], mesh.shape["lon"]),
        mesh=mesh,
        in_specs=(
            P(None, "lat", "lon"),
            P("lat", "lon"),
            P(None, None, "lat", "lon"),
            P(("lat", "lon"), None),
            P(("lat", "lon")),
            P(("lat", "lon")),
            P(("lat", "lon")),
        ),
        out_specs=(P(None, "lat", "lon"), P("lat", "lon")),
        check_vma=False,
    )
```
